128 devices in a mesh: pts: 32 (over x, z, core), grp: 4 (over y).
Axes of the slice: x: 4, y: 4, z: 4, core: 2. Of those that a mesh axis runs over, the one named last changes fastest.
Arguments:
- feats: bfloat16 [131072, 128], P(('pts', 'grp')), may hold values from -6 to 6
- order: int32 [131072], P(('pts', 'grp')), may hold values from 0 to 131071, as said below
- parent: int32 [131072], P(('pts', 'grp')), may hold values from 0 to 32767, as said below
- gain_one: float32 [128], replicated, may hold values from 0.25 to 1.75
- w_qkv: float32 [128, 384], replicated, may hold values from -0.5 to 0.5
- w_out: float32 [128, 128], replicated, may hold values from -0.5 to 0.5
- w_pool: float32 [128, 256], P(None, 'grp'), may hold values from -0.5 to 0.5
- gain_two: float32 [256], P('grp'), may hold values from 0.25 to 1.75
- cotangent: bfloat16 [32768, 256], P('pts', 'grp'), may hold values from -6 to 6
Outputs:
- section_four: bfloat16 [32768, 256], P('pts', 'grp')
- section_three: bfloat16 [131072, 128], P(('pts', 'grp'))
- grad_feats: bfloat16 [131072, 128], P(('pts', 'grp'))
- grad_gain_one: float32 [128], replicated
- grad_qkv: float32 [128, 384], replicated
- grad_out: float32 [128, 128], replicated
- grad_pool: float32 [128, 256], P(None, 'grp')
- grad_gain_two: float32 [256], P('grp')
The draws below stay inside these ranges and needn't reach their ends.
Inputs may be any that keep to these rules, and one draw needn't show every extreme that they name: `order`: A permutation. Each row stays within its aligned group of 8 consecutive devices along pts+grp; the number of rows going from one device of a group to one device of it (itself included) is 128 + k * 32 with k in -2..2, and k = 2 occurs in every group, so at most 192 rows go from one device to another. `parent`: Nondecreasing. The rows held by the four devices of one index p of pts have parents p * 1024 to (p + 1) * 1024 - 1; each such parent has 1 to 7 rows, and in every such block some parent has 7.
All inputs are finite; a program needn't handle non-finite values.
Results may differ from the reference program's by a relative error of at most 0.0007.
Values may be sent and summed in bfloat16 or wider, within the bound.
No kernel may reach another device: no remote copies, remote signals or barrier semaphores. Data moves between devices by JAX's collectives and lax.ppermute only.
A program may use at most 256 MiB of HBM per device.

```python
import jax
import jax.numpy as jnp
from jax import lax

C = 128
C4 = 256
HD = 16
PATCH = 1024
P3 = 1024
N3 = 131072
N4 = 32768


def draw_order(key, part):
    key = jax.random.fold_in(key, 11)
    groups = N3 // (8 * P3)
    base_count = P3 // 8
    step_count = P3 // 32
    level_table = jnp.array([2, 1, 1, 0, 0, -1, -1, -2], jnp.int32)
    key_levels, key_rows, key_slots = jax.random.split(key, 3)
    shuffled = jax.vmap(lambda sub_key: jax.random.permutation(sub_key, level_table))(jax.random.split(key_levels, groups))
    sender = jnp.arange(8)[:, None]
    target = jnp.arange(8)[None, :]
    pair_counts = base_count + step_count * shuffled[:, (target - sender) % 8]
    send_end = jnp.cumsum(pair_counts, axis=2)
    send_start = send_end - pair_counts
    recv_start = jnp.cumsum(pair_counts, axis=1) - pair_counts
    position = jnp.arange(P3)
    target_of = jnp.sum((position[None, None, :, None] >= send_end[:, :, None, :]).astype(jnp.int32), axis=3)
    offset_in = jnp.take_along_axis(send_start, target_of, axis=2)
    slot_of = jnp.take_along_axis(recv_start, target_of, axis=2) + position[None, None, :] - offset_in
    row_order = jax.vmap(lambda sub_key: jax.random.permutation(sub_key, P3))(jax.random.split(key_rows, groups * 8)).reshape(groups, 8, P3)
    slot_order = jax.vmap(lambda sub_key: jax.random.permutation(sub_key, P3))(jax.random.split(key_slots, groups * 8)).reshape(groups, 8, P3)
    group_ids = jnp.arange(groups)[:, None, None]
    final_slot = slot_order[group_ids, target_of, slot_of]
    destination = group_ids * 8 * P3 + target_of * P3 + final_slot
    anchor = group_ids * 8 * P3 + sender[None, :, :] * P3 + row_order
    return jnp.zeros((N3,), jnp.int32).at[destination.reshape(-1)].set(anchor.reshape(-1).astype(jnp.int32))


def draw_parent(key, part):
    key = jax.random.fold_in(key, 23)
    columns = N3 // (4 * P3)
    key_delta, key_shuffle = jax.random.split(key, 2)
    offsets = jax.random.randint(key_delta, (columns, P3 // 2), -3, 4)
    offsets = offsets.at[:, 0].set(3)
    lengths = jnp.stack([4 + offsets, 4 - offsets], -1).reshape(columns, P3)
    lengths = jax.vmap(lambda sub_key, length_row: jax.random.permutation(sub_key, length_row))(jax.random.split(key_shuffle, columns), lengths)
    parents = jax.vmap(lambda length_row: jnp.repeat(jnp.arange(P3), length_row, total_repeat_length=4 * P3))(lengths)
    return (parents + jnp.arange(columns)[:, None] * P3).reshape(-1).astype(jnp.int32)


def shard_levels(stream_key, extent, pieces, smallest, largest):
    level, own = 1.0, jax.random.fold_in(stream_key, 6)
    for dim, parts in pieces:
        steps = jnp.exp(jax.random.uniform(jax.random.fold_in(own, dim), (parts,), jnp.float32, smallest / len(pieces), largest / len(pieces)))
        level = level * jnp.repeat(steps, extent[dim] // parts).reshape([-1 if axis == dim else 1 for axis in range(len(extent))])
    return level


def scatter_about(key, extent, scale, most, cuts=(), held_as=jnp.bfloat16):
    drawn = scale * jax.random.normal(key, extent, jnp.float32)
    if cuts:
        drawn = drawn * shard_levels(key, extent, cuts, -0.22, 0.18)
    return jnp.clip(drawn, -most, most).astype(held_as)


def setup_inputs(seed: int = 0) -> dict:
    arg_keys = jax.random.split(jax.random.key(seed), 10)
    return {
        "feats": scatter_about(arg_keys[0], (N3, C), 1.0, 6.0, ((0, 128),)),
        "order": draw_order(jax.random.fold_in(arg_keys[9], 71), 0),
        "parent": draw_parent(jax.random.fold_in(arg_keys[9], 71), 0),
        "gain_one": jnp.clip(1.0 + 0.15 * jax.random.normal(arg_keys[3], (C,), jnp.float32), 0.25, 1.75),
        "w_qkv": scatter_about(arg_keys[4], (C, 3 * C), C ** -0.5, 0.5, (), jnp.float32),
        "w_out": scatter_about(arg_keys[5], (C, C), C ** -0.5, 0.5, (), jnp.float32),
        "w_pool": scatter_about(arg_keys[6], (C, C4), C ** -0.5, 0.5, ((1, 4),), jnp.float32),
        "gain_two": jnp.clip(1.0 + 0.15 * jax.random.normal(arg_keys[7], (C4,), jnp.float32), 0.25, 1.75),
        "cotangent": scatter_about(arg_keys[8], (N4, C4), 1.0, 6.0, ((0, 32), (1, 4))),
    }


EPS = 1e-05
HIGH = lax.Precision.HIGHEST

def matmul(left_side, right_side):
    return jnp.dot(left_side, right_side, precision=HIGH, preferred_element_type=jnp.float32)

def layer_norm(values, gain_vec):
    center = values - lax.optimization_barrier(jnp.mean(values, -1, keepdims=True))
    spread = lax.optimization_barrier(jnp.mean(center * center, -1, keepdims=True))
    return center * lax.rsqrt(spread + EPS) * gain_vec

def patch_block(single_patch, gain_first, qkv_matrix, out_matrix):
    length, width = single_patch.shape
    head_count = width // HD
    normed = layer_norm(single_patch, gain_first)
    packed = matmul(normed, qkv_matrix).reshape(length, 3, head_count, HD)
    scores = jnp.einsum('qhd,khd->hqk', packed[:, 0], packed[:, 1], precision=HIGH) * HD ** (-0.5)
    weights = jax.nn.softmax(scores, axis=-1)
    mixed_heads = jnp.einsum('hqk,khd->qhd', weights, packed[:, 2], precision=HIGH).reshape(length, width)
    return single_patch + matmul(mixed_heads, out_matrix)

def reference(feats, order, parent, gain_one, w_qkv, w_out, w_pool, gain_two, cotangent):
    counts = jax.ops.segment_sum(jnp.ones((N3,), jnp.float32), parent, N4)

    def forward(inputs, gain_first, qkv_matrix, out_matrix, pool_matrix, gain_second):
        hilbert = inputs[order]
        blocked = jax.checkpoint(patch_block)
        outputs = lax.map(lambda single_patch: blocked(single_patch, gain_first, qkv_matrix, out_matrix), hilbert.reshape(-1, PATCH, C)).reshape(N3, C)
        section_rows = jnp.zeros_like(outputs).at[order].set(outputs)
        pooled = jax.ops.segment_sum(section_rows, parent, N4) / counts[:, None]
        scaled = layer_norm(matmul(pooled, pool_matrix), gain_second)
        return (jax.nn.gelu(scaled, approximate=True), section_rows)
    (section_four, section_rows), back_fn = jax.vjp(forward, feats.astype(jnp.float32), gain_one, w_qkv, w_out, w_pool, gain_two)
    gradients = back_fn((cotangent.astype(jnp.float32), jnp.zeros_like(section_rows)))
    return (section_four.astype(jnp.bfloat16), section_rows.astype(jnp.bfloat16), gradients[0].astype(jnp.bfloat16), gradients[1], gradients[2], gradients[3], gradients[4], gradients[5])
```

```python
import math

import jax
import jax.numpy as jnp
from jax import lax
from jax.experimental import pallas as pl
from jax.experimental.pallas import tpu as pltpu
from jax.sharding import Mesh, PartitionSpec as P

F32 = jnp.float32
BF16 = jnp.bfloat16
HEADS = 8
HD = 16
C = 128
ROWS = 1024
BLK = 256
EPS = 1e-05
QSCALE = HD ** (-0.5) * math.log2(math.e)
LN2 = math.log(2.0)
GELU_A = math.sqrt(2.0 / math.pi)
GELU_B = 0.044715
PARAMS = pltpu.CompilerParams(vmem_limit_bytes=52 * 1024 * 1024)


def dot(a, b):
    return jnp.dot(a, b, preferred_element_type=F32)


def dot_nt(a, b):
    return lax.dot_general(a, b, (((1,), (1,)), ((), ())), preferred_element_type=F32)


def split2(x):
    hi = x.astype(BF16)
    return hi, (x - hi.astype(F32)).astype(BF16)


def dot3(a, b):
    ah, al = split2(a)
    bh, bl = split2(b)
    return dot(ah, bh) + (dot(al, bh) + dot(ah, bl))


def dot3_nt(a, b):
    ah, al = split2(a)
    bh, bl = split2(b)
    return dot_nt(ah, bh) + (dot_nt(al, bh) + dot_nt(ah, bl))


def norm_rows(values):
    center = values - jnp.mean(values, -1, keepdims=True)
    rstd = lax.rsqrt(jnp.mean(center * center, -1, keepdims=True) + EPS)
    return center * rstd, rstd


def select_matrix(parts, part_of_slot):
    shape = (parts * C, HEADS * C)
    row = lax.broadcasted_iota(jnp.int32, shape, 0)
    col = lax.broadcasted_iota(jnp.int32, shape, 1)
    slot = (col >> 4) & 7
    wanted = jnp.full(shape, parts, jnp.int32)
    for index, part in enumerate(part_of_slot):
        wanted = jnp.where(slot == index, part, wanted)
    hit = (row & 127) == ((col >> 7) * HD + (col & 15))
    hit = hit & ((row >> 7) == wanted)
    return jnp.where(hit, 1.0, 0.0).astype(BF16)


def place(parts, part_of_slot, out_ref, const=None):
    sel = select_matrix(len(parts), part_of_slot)
    packed = jnp.concatenate(parts, axis=1)
    for pair in range(HEADS // 2):
        both = dot(packed, sel[:, pair * 256 : pair * 256 + 256])
        for half in range(2):
            block = both[:, half * C : half * C + C]
            if const is not None:
                block = jnp.where(const(lax.broadcasted_iota(jnp.int32, block.shape, 1)), 1.0, block)
            out_ref[2 * pair + half] = block.astype(BF16)


def head_mask(shape, h):
    return (lax.broadcasted_iota(jnp.int32, shape, 1) >> 4) == h


def place_of_device():
    return lax.axis_index("core"), lax.axis_index("grp")


HALF = 528
MESSAGE = 2 * HALF


def pack_kernel(feats_ref, order_ref, parent_ref, cot_ref, w_ref, gain_ref, msg_ref, *w_msgs):
    _, y = place_of_device()
    msg_ref[:ROWS] = feats_ref[...]
    order = order_ref[...] & 8191
    parent = parent_ref[...] & 2047
    ids = jnp.concatenate([order >> 6, order & 63, parent >> 6, parent & 63], axis=0)
    msg_ref[ROWS:] = ids.astype(F32).astype(BF16)
    w_high, w_low = split2(w_ref[...])
    gain = gain_ref[...]
    first = gain.astype(BF16).astype(F32)
    second = (gain - first).astype(BF16).astype(F32)
    third = gain - first - second
    row = lax.broadcasted_iota(jnp.int32, (16, 64), 0)
    gains = jnp.where(row == 0, first, jnp.where(row == 1, second, jnp.where(row == 2, third, 0.0)))
    gains = jnp.concatenate([gains, jnp.zeros((16, 64), F32)], axis=1).astype(BF16)
    weights = jnp.concatenate([w_high, w_low], axis=0)
    for k, ref in enumerate(w_msgs):
        cot = cot_ref[pl.ds(pl.multiple_of(((y + k) & 3) * 256, 256), 256)]
        ref[:256] = jnp.concatenate([cot, weights], axis=1)
        ref[256:] = gains


def pack(feats, order, parent, cotangent, w_pool, gain_two):
    return pl.pallas_call(
        pack_kernel,
        out_shape=(jax.ShapeDtypeStruct((MESSAGE, C), BF16),) + (jax.ShapeDtypeStruct((272, C), BF16),) * 4,
        compiler_params=PARAMS,
        name="pack",
    )(feats, order, parent, cotangent, w_pool, gain_two)


def gather_rows(order_ref, blocks, tab, rep, hil_ref, pid_ref, gord_ref, cnt_ref):
    core, y = place_of_device()
    lane = lax.broadcasted_iota(jnp.int32, (C, C), 1)
    digits = []
    for slot, (rows, ids) in enumerate(blocks):
        for start, part in rows:
            tab[slot, start : start + part.shape[0], :C] = part
        ids = ids.astype(F32)
        gord_ref[slot * 8 : slot * 8 + 8] = (ids[:8] * 64.0 + ids[8:16]).astype(jnp.int32)
        digits.append(ids[16:])
    digits = jnp.concatenate(digits, axis=0)
    turned = digits.T
    for slot in range(8):
        for t in range(8):
            tab[slot, t * C : t * C + C, C:] = jnp.where((lane & ~8) == slot * 16 + t, turned, 0.0).astype(BF16)

    count = jnp.zeros((256, C), F32)
    target = (lax.broadcasted_iota(jnp.int32, (256, C), 0) + (core * 1024 + y * 256)).astype(F32)
    for slot in range(4):
        parents = digits[slot * 16 : slot * 16 + 8] * 64.0 + digits[slot * 16 + 8 : slot * 16 + 16]
        for t in range(8):
            count = count + jnp.where(target == parents[t : t + 1], 1.0, 0.0)
    cnt_ref[...] = jnp.broadcast_to(jnp.sum(count, axis=1, keepdims=True), cnt_ref.shape)

    order = order_ref[...]
    source = (order >> 10) & 7
    slot = (((source >> 2) ^ core) << 2) + ((y - source) & 3)
    index = (slot * ROWS + (order & 1023)).astype(F32)
    for t in range(8):
        column = jnp.broadcast_to(index[t : t + 1], (C, C)).T
        rep[t * C : t * C + C] = column.astype(jnp.int32) - lane
    weight = jnp.where(lax.broadcasted_iota(jnp.int32, (BLK, C), 1) & 8 == 0, 64.0, 1.0)
    for blk in range(ROWS // BLK):
        rows = pl.ds(blk * BLK, BLK)
        away = rep[rows]
        got = jnp.zeros((BLK, 2 * C), F32)
        for slot in range(8):
            hot = jnp.concatenate(
                [jnp.where(away == slot * ROWS + t * C, 1.0, 0.0) for t in range(8)], axis=1
            ).astype(BF16)
            got = got + dot(hot, tab[slot])
        hil_ref[rows] = got[:, :C].astype(BF16)
        parent = jnp.sum(got[:, C:] * weight, axis=1, keepdims=True).astype(jnp.int32)
        pid_ref[rows] = jnp.broadcast_to(parent, (BLK, C))


def fwd_kernel(
    order_ref, m0, m1, m2a, m2b, m3, other, gain_ref, wqkv_ref, wout_ref,
    hil_ref, pid_ref, gord_ref, cnt_ref, att_ref, mine_ref, theirs_ref, o_ref, lse_ref,
    tab, rep, qp, kp, vh, vl, ac,
):
    core, y = place_of_device()
    blocks = [
        ([(0, m0[:ROWS])], m0[ROWS:]),
        ([(0, m1[:ROWS])], m1[ROWS:]),
        ([(0, m2a[...]), (HALF, m2b[: ROWS - HALF])], m2b[ROWS - HALF :]),
        ([(0, m3[:ROWS])], m3[ROWS:]),
    ] + [([(0, other[k, :ROWS])], other[k, ROWS:]) for k in range(4)]
    gather_rows(order_ref, blocks, tab, rep, hil_ref, pid_ref, gord_ref, cnt_ref)

    r = hil_ref[...].astype(F32)
    xhat, _ = norm_rows(r)
    u = xhat * gain_ref[...]
    qkv = dot3(u, wqkv_ref[...])
    place(split2(qkv[:, :C] * QSCALE), (0, 0, 1, 1), qp)
    place(split2(qkv[:, C : 2 * C]), (0, 1, 0, 1), kp)
    vh[...], vl[...] = split2(qkv[:, 2 * C :])

    def head(h, carry):
        vmask = head_mask((ROWS, C), h)
        zero = jnp.zeros((), BF16)
        one = jnp.ones((), BF16)
        va = jnp.concatenate([jnp.where(vmask, vh[...], zero), jnp.where(vmask, vl[...], one)], axis=1)
        keys = kp[h]
        mask = head_mask((BLK, C), h)
        for blk in range(ROWS // BLK):
            rows = pl.ds(blk * BLK, BLK)
            s = dot_nt(qp[h, rows], keys)
            m = jnp.max(s, axis=1, keepdims=True)
            ph, plo = split2(jnp.exp2(s - m))
            oa = dot(ph, va) + dot(plo, va)
            first, second = oa[:, :C], oa[:, C:]
            total = pltpu.roll(second, HD, 1)
            o_ref[rows] = jnp.where(mask, (first + second) / total, o_ref[rows])
            lse_ref[rows] = jnp.where(mask, m + jnp.log2(total), lse_ref[rows])
        return carry

    lax.fori_loop(0, HEADS, head, 0)
    att = r + dot3(o_ref[...], wout_ref[...])
    hi, lo = split2(att)
    att_ref[...] = hi
    ac[...] = jnp.concatenate([hi, lo], axis=1)
    parent = pid_ref[...].astype(F32).T[0:1].astype(jnp.int32)
    pid = (((parent >> 10) ^ core) << 10) + ((((parent >> 8) - y) & 3) << 8) + (parent & 255)
    for chunk in range(8):
        own = lax.broadcasted_iota(jnp.int32, (256, ROWS), 0) + chunk * 256
        hot = jnp.where(own == pid, 1.0, 0.0).astype(BF16)
        sums = dot(hot, ac[...])
        target = mine_ref if chunk < 4 else theirs_ref
        target[chunk & 3] = sums[:, :C] + sums[:, C:]


def attention_forward(order, blocks, gain, w_qkv, w_out):
    return pl.pallas_call(
        fwd_kernel,
        out_shape=(
            jax.ShapeDtypeStruct((ROWS, C), BF16),
            jax.ShapeDtypeStruct((ROWS, C), jnp.int32),
            jax.ShapeDtypeStruct((64, C), jnp.int32),
            jax.ShapeDtypeStruct((256, C), F32),
            jax.ShapeDtypeStruct((ROWS, C), BF16),
            jax.ShapeDtypeStruct((4, 256, C), F32),
            jax.ShapeDtypeStruct((4, 256, C), F32),
            jax.ShapeDtypeStruct((ROWS, C), F32),
            jax.ShapeDtypeStruct((ROWS, C), F32),
        ),
        scratch_shapes=[
            pltpu.VMEM((8, ROWS, 2 * C), BF16),
            pltpu.VMEM((ROWS, C), jnp.int32),
            pltpu.VMEM((HEADS, ROWS, C), BF16),
            pltpu.VMEM((HEADS, ROWS, C), BF16),
            pltpu.VMEM((ROWS, C), BF16),
            pltpu.VMEM((ROWS, C), BF16),
            pltpu.VMEM((ROWS, 2 * C), BF16),
        ],
        compiler_params=PARAMS,
        cost_estimate=pl.CostEstimate(flops=30_000_000_000, bytes_accessed=4_000_000, transcendentals=8_400_000),
        name="attention_forward",
    )(order, *blocks, gain, w_qkv, w_out)


def pool_kernel(mine, theirs, c1, c2, c3, cnt_ref, w0, w1, w2, w3, s0, s1, s2, s3, dp_ref, gw_ref, gg_ref):
    cnt = cnt_ref[...]
    pooled = (mine[0] + theirs[0] + c1[...] + c2[...] + c3[...]) / cnt
    msgs = (w0, w1, w2, w3)
    wh = jnp.concatenate([m[:C, 64:] for m in msgs], axis=1)
    wl = jnp.concatenate([m[C:256, 64:] for m in msgs], axis=1)
    cot = jnp.concatenate([m[:256, :64] for m in msgs], axis=1).astype(F32)
    gains = jnp.concatenate([m[256:, :64] for m in msgs], axis=1).astype(F32)
    gain = gains[0:1] + gains[1:2] + gains[2:3]
    ph, plo = split2(pooled)
    normed, rstd = norm_rows(dot(ph, wh) + (dot(plo, wh) + dot(ph, wl)))
    v = normed * gain
    t = jnp.tanh(GELU_A * (v + GELU_B * (v * v * v)))
    s4 = 0.5 * v * (1.0 + t)
    for k, ref in enumerate((s0, s1, s2, s3)):
        ref[...] = s4[:, 64 * k : 64 * k + 64].astype(BF16)
    slope = 0.5 * (1.0 + t) + 0.5 * v * (1.0 - t * t) * (GELU_A * (1.0 + (3.0 * GELU_B) * (v * v)))
    d_scaled = cot * slope
    gg_ref[...] = jnp.sum(d_scaled * normed, axis=0, keepdims=True)
    d_normed = d_scaled * gain
    d_proj = rstd * (
        d_normed
        - jnp.mean(d_normed, -1, keepdims=True)
        - normed * jnp.mean(d_normed * normed, -1, keepdims=True)
    )
    dh, dl = split2(d_proj)
    dp_ref[...] = (dot_nt(dh, wh) + (dot_nt(dl, wh) + dot_nt(dh, wl))) / cnt
    gw_ref[...] = dot3(pooled.T, d_proj)


def pooled_section(mine, theirs, chunks, cnt, msgs):
    return pl.pallas_call(
        pool_kernel,
        out_shape=(jax.ShapeDtypeStruct((256, 64), BF16),) * 4
        + (
            jax.ShapeDtypeStruct((256, C), F32),
            jax.ShapeDtypeStruct((C, 256), F32),
            jax.ShapeDtypeStruct((1, 256), F32),
        ),
        compiler_params=PARAMS,
        name="pooled_section",
    )(mine, theirs, *chunks, cnt, *msgs)

PIECE = 104


def bwd_kernel(
    r_ref, o_ref, lse_ref, gain_ref, wqkv_ref, wout_ref, pid_ref, gw_ref, gg2_ref,
    d0, d1, d2, d3, e0, e1, e2, e3,
    df_ref, keep_ref, send_ref,
    qp, kp, dop, vp, kh, kl, tab, da_ref, dot_t, q_t, dv_t, dk_t, dq_ref, flat,
):
    core, y = place_of_device()
    for chunk, ref in enumerate((d0, d1, d2, d3, e0, e1, e2, e3)):
        hi, lo = split2(ref[...])
        tab[chunk * 256 : chunk * 256 + 256, :C] = hi
        tab[chunk * 256 : chunk * 256 + 256, C:] = lo
    lane = lax.broadcasted_iota(jnp.int32, (BLK, C), 1)
    for blk in range(ROWS // BLK):
        rows = pl.ds(blk * BLK, BLK)
        pid = pid_ref[rows]
        away = (((pid >> 10) ^ core) << 10) + (((y - (pid >> 8)) & 3) << 8) + (pid & 255) - lane
        hot = jnp.concatenate([jnp.where(away == t * C, 1.0, 0.0) for t in range(16)], axis=1).astype(BF16)
        got = dot(hot, tab[...])
        da_ref[rows] = got[:, :C] + got[:, C:]

    r = r_ref[...].astype(F32)
    xhat, rstd = norm_rows(r)
    u = xhat * gain_ref[...]
    qkv = dot3(u, wqkv_ref[...])
    q = qkv[:, :C] * QSCALE
    qh, ql = split2(q)
    lse = -lse_ref[...]
    l1 = lse.astype(BF16).astype(F32)
    l2 = (lse - l1).astype(BF16).astype(F32)
    l3 = lse - l1 - l2
    which = lax.broadcasted_iota(jnp.int32, (ROWS, C), 1) & 15
    lp = jnp.where(which == 0, l1, jnp.where(which == 1, l2, jnp.where(which == 2, l3, 0.0))).astype(BF16)
    place((qh, ql, lp), (0, 0, 1, 1, 2), qp)
    khi, klo = split2(qkv[:, C : 2 * C])
    place((khi, klo), (0, 1, 0, 1), kp, const=lambda lane: (lane >= 64) & (lane < 67))
    kh[...] = khi
    kl[...] = klo
    place(split2(qkv[:, 2 * C :]), (0, 1, 0, 1), vp, const=lambda lane: (lane >= 64) & (lane < 96))
    da = da_ref[...]
    do = dot3_nt(da, wout_ref[...])
    place((*split2(do), *split2(-do * o_ref[...])), (0, 0, 1, 1, 2, 3), dop)
    for source, target in ((do, dot_t), (q, q_t)):
        hi, lo = split2(source.T)
        for h in range(HEADS):
            target[h, :HD] = hi[h * HD : h * HD + HD]
            target[h, HD:] = lo[h * HD : h * HD + HD]

    def head(h, carry):
        kmask = head_mask((ROWS, C), h)
        zero = jnp.zeros((), BF16)
        ka = jnp.concatenate([jnp.where(kmask, kh[...], zero), jnp.where(kmask, kl[...], zero)], axis=1)
        keys, vals = kp[h], vp[h]
        mask = head_mask((BLK, C), h)
        dv = jnp.zeros((2 * HD, ROWS), F32)
        dk = jnp.zeros((2 * HD, ROWS), F32)
        for blk in range(ROWS // BLK):
            rows = pl.ds(blk * BLK, BLK)
            p = jnp.exp2(dot_nt(qp[h, rows], keys))
            ds = p * dot_nt(dop[h, rows], vals)
            ph, plo = split2(p)
            sh, sl = split2(ds)
            left = dot_t[h, :, rows]
            dv = dv + (dot(left, ph) + dot(left, plo))
            left = q_t[h, :, rows]
            dk = dk + (dot(left, sh) + dot(left, sl))
            dq = dot(sh, ka) + dot(sl, ka)
            dq_ref[rows] = jnp.where(mask, dq[:, :C] + dq[:, C:], dq_ref[rows])
        place_rows = pl.ds(pl.multiple_of(h * HD, HD), HD)
        dv_t[place_rows] = dv[:HD] + dv[HD:]
        dk_t[place_rows] = dk[:HD] + dk[HD:]
        return carry

    lax.fori_loop(0, HEADS, head, 0)
    grads = jnp.concatenate([dq_ref[...] * HD ** (-0.5), dk_t[...].T * LN2, dv_t[...].T], axis=1)
    du = dot3_nt(grads, wqkv_ref[...])
    gq = dot3(u.T, grads)
    for part in range(3):
        flat[part * C : part * C + C] = gq[:, part * C : part * C + C]
    flat[3 * C :] = dot3(o_ref[...].T, da)
    gain_one = jnp.sum(du * xhat, axis=0, keepdims=True)
    row = lax.broadcasted_iota(jnp.int32, (8, C), 0)
    for side, ref in enumerate((keep_ref, send_ref)):
        half = core ^ side
        for k in range(4):
            piece = ((y + k) & 3) * 2 + half
            ref[k, :64] = flat[pl.ds(pl.multiple_of(piece * 64, 64), 64)]
            block = 64 * ((4 - k) % 4)
            start = pl.multiple_of(half * 64, 64)
            upper = gw_ref[pl.ds(start, 32)][:, block : block + 64]
            lower = gw_ref[pl.ds(start + 32, 32)][:, block : block + 64]
            ref[k, 64:96] = jnp.concatenate([upper, lower], axis=1)
            gain_two = jnp.concatenate([gg2_ref[:, block : block + 64], jnp.zeros((1, 64), F32)], axis=1)
            ref[k, 96:] = jnp.where(row == 0, gain_one, jnp.where(row == 1, gain_two, 0.0))
    dn = du * gain_ref[...]
    dx = rstd * (dn - jnp.mean(dn, -1, keepdims=True) - xhat * jnp.mean(dn * xhat, -1, keepdims=True))
    df_ref[...] = (da + dx).astype(BF16)


def attention_backward(rows, o, lse, gain, w_qkv, w_out, pid, grad_pool, grad_gain_two, d_pooled):
    return pl.pallas_call(
        bwd_kernel,
        out_shape=(
            jax.ShapeDtypeStruct((ROWS, C), BF16),
            jax.ShapeDtypeStruct((4, PIECE, C), F32),
            jax.ShapeDtypeStruct((4, PIECE, C), F32),
        ),
        scratch_shapes=[
            pltpu.VMEM((HEADS, ROWS, C), BF16),
            pltpu.VMEM((HEADS, ROWS, C), BF16),
            pltpu.VMEM((HEADS, ROWS, C), BF16),
            pltpu.VMEM((HEADS, ROWS, C), BF16),
            pltpu.VMEM((ROWS, C), BF16),
            pltpu.VMEM((ROWS, C), BF16),
            pltpu.VMEM((2048, 2 * C), BF16),
            pltpu.VMEM((ROWS, C), F32),
            pltpu.VMEM((HEADS, 2 * HD, ROWS), BF16),
            pltpu.VMEM((HEADS, 2 * HD, ROWS), BF16),
            pltpu.VMEM((C, ROWS), F32),
            pltpu.VMEM((C, ROWS), F32),
            pltpu.VMEM((ROWS, C), F32),
            pltpu.VMEM((4 * C, C), F32),
        ],
        compiler_params=PARAMS,
        cost_estimate=pl.CostEstimate(flops=90_000_000_000, bytes_accessed=8_000_000, transcendentals=8_400_000),
        name="attention_backward",
    )(rows, o, lse, gain, w_qkv, w_out, pid, grad_pool, grad_gain_two, *d_pooled)


def rows_kernel(gord_ref, a0, a1, a2, a3, ao, f0, f1, f2, f3, fo, s0, s1, s2, s3, s3_ref, gf_ref, s4_ref):
    core, y = place_of_device()
    att = [a0[...], a1[...], a2[...], a3[...]] + [ao[k] for k in range(4)]
    grad = [f0[...], f1[...], f2[...], f3[...]] + [fo[k] for k in range(4)]
    own = lax.broadcasted_iota(jnp.int32, (BLK, C), 0) + (core * 4 + y) * ROWS
    for blk in range(ROWS // BLK):
        got = jnp.zeros((BLK, 2 * C), F32)
        for slot in range(8):
            hot = jnp.concatenate(
                [jnp.where(own == gord_ref[slot * 8 + t : slot * 8 + t + 1] - blk * BLK, 1.0, 0.0) for t in range(8)],
                axis=1,
            ).astype(BF16)
            got = got + dot(hot, jnp.concatenate([att[slot], grad[slot]], axis=1))
        s3_ref[blk * BLK : blk * BLK + BLK] = got[:, :C].astype(BF16)
        gf_ref[blk * BLK : blk * BLK + BLK] = got[:, C:].astype(BF16)
    for k, ref in enumerate((s0, s1, s2, s3)):
        s4_ref[pl.ds(pl.multiple_of(((y + k) & 3) * 256, 256), 256)] = ref[...]


def results(gord, att, grad, s4):
    return pl.pallas_call(
        rows_kernel,
        out_shape=(
            jax.ShapeDtypeStruct((ROWS, C), BF16),
            jax.ShapeDtypeStruct((ROWS, C), BF16),
            jax.ShapeDtypeStruct((ROWS, 64), BF16),
        ),
        compiler_params=PARAMS,
        cost_estimate=pl.CostEstimate(flops=8_000_000_000, bytes_accessed=5_000_000, transcendentals=0),
        name="rows_to_z_order",
    )(gord, *att, *grad, *s4)


def params_kernel(b0, b1, b2, b3, gq_ref, go_ref, g1_ref, gw_ref, g2_ref, flat, gains):
    core, y = place_of_device()
    for k, ref in enumerate((b0, b1, b2, b3)):
        for side in range(2):
            piece = ((y - k) & 3) * 2 + (core ^ side)
            flat[pl.ds(pl.multiple_of(piece * 64, 64), 64)] = ref[side, :64]
            gains[pl.ds(pl.multiple_of(piece * 8, 8), 8)] = ref[side, 96:]
    for part in range(3):
        gq_ref[:, part * C : part * C + C] = flat[part * C : part * C + C]
    go_ref[...] = flat[3 * C :]
    g1_ref[...] = gains[0:1]
    for side in range(2):
        start = pl.multiple_of((core ^ side) * 64, 64)
        gw_ref[pl.ds(start, 32)] = b0[side, 64:96, :64]
        gw_ref[pl.ds(start + 32, 32)] = b0[side, 64:96, 64:]
    g2_ref[...] = gains[pl.ds(pl.multiple_of(y * 16, 16), 8)][1:2, :64]


def parameter_results(blocks):
    return pl.pallas_call(
        params_kernel,
        out_shape=(
            jax.ShapeDtypeStruct((C, 3 * C), F32),
            jax.ShapeDtypeStruct((C, C), F32),
            jax.ShapeDtypeStruct((1, C), F32),
            jax.ShapeDtypeStruct((C, 64), F32),
            jax.ShapeDtypeStruct((1, 64), F32),
        ),
        scratch_shapes=[pltpu.VMEM((4 * C, C), F32), pltpu.VMEM((64, C), F32)],
        compiler_params=PARAMS,
        name="parameter_results",
    )(*blocks)


def shift(block, axis, apart):
    count = lax.axis_size(axis)
    return lax.ppermute(block, axis, [(i, (i + apart) % count) for i in range(count)])


def along_y(block):
    return [block] + [shift(block, "grp", k) for k in (1, 2, 3)]


def sum_axis(block, axis):
    one, two, three = (shift(block, axis, k) for k in (1, 2, 3))
    return (block + two) + (one + three)


def shards(feats, order, parent, gain_one, w_qkv, w_out, w_pool, gain_two, cotangent):
    order = order.reshape(8, C)
    msg, *w_msgs = pack(feats, order, parent.reshape(8, C), cotangent, w_pool, gain_two[None])

    left = shift(msg, "grp", 1)
    right = shift(msg, "grp", -1)
    w_msgs = [w_msgs[0]] + [shift(w_msgs[k], "grp", k) for k in (1, 2, 3)]
    upper = shift(right[:HALF], "grp", -1)
    lower = shift(left[HALF:], "grp", 1)
    four = jnp.concatenate([msg, left, upper, lower, right], axis=0).reshape(4, MESSAGE, C)
    other = shift(four, "core", 1)
    hilbert, pid, gord, cnt, att, mine, theirs, o, lse = attention_forward(
        order, (msg, left, upper, lower, right, other), gain_one[None], w_qkv, w_out
    )

    theirs = shift(theirs, "core", 1)
    chunks = [shift(mine[k] + theirs[k], "grp", k) for k in (1, 2, 3)]
    *s4, d_pool, grad_pool, grad_gain_two = pooled_section(mine, theirs, chunks, cnt, w_msgs)
    own = along_y(d_pool)
    d_pooled = own + [shift(block, "core", 1) for block in own]

    s4 = [s4[0]] + [shift(s4[k], "grp", -k) for k in (1, 2, 3)]
    att = along_y(att)
    att.append(shift(jnp.stack(att), "core", 1))

    df, keep, send = attention_backward(
        hilbert, o, lse, gain_one[None], w_qkv, w_out, pid, grad_pool, grad_gain_two, d_pooled
    )
    df = along_y(df)
    df.append(shift(jnp.stack(df), "core", 1))
    section_three, grad_feats, section_four = results(gord, att, df, s4)

    kept = keep + shift(send, "core", 1)
    piece = (kept[0] + shift(kept[2], "grp", 2)) + (shift(kept[1], "grp", 1) + shift(kept[3], "grp", 3))
    piece = sum_axis(sum_axis(piece, "x"), "z")
    both = jnp.stack([piece, shift(piece, "core", 1)])
    g_qkv, g_out, g_one, g_pool, g_two = parameter_results(along_y(both))
    return (section_four, section_three, grad_feats, g_one[0], g_qkv, g_out, g_pool, g_two[0])


def solution(mesh):
    fine = Mesh(mesh.devices.reshape(4, 4, 2, 4), ("x", "z", "core", "grp"))
    pts = ("x", "z", "core")
    everywhere = pts + ("grp",)
    placed = (
        P(everywhere, None),
        P(everywhere),
        P(everywhere),
        P(),
        P(),
        P(),
        P(None, "grp"),
        P("grp"),
        P(pts, "grp"),
    )
    return jax.shard_map(
        shards,
        mesh=fine,
        in_specs=placed,
        out_specs=(
            P(pts, "grp"),
            P(everywhere, None),
            P(everywhere, None),
            P(),
            P(),
            P(),
            P(None, "grp"),
            P("grp"),
        ),
        check_vma=False,
    )
```

```python
import math

import jax
import jax.numpy as jnp
from jax import lax
from jax.experimental import pallas as pl
from jax.experimental.pallas import tpu as pltpu
from jax.sharding import Mesh, PartitionSpec as P

F32 = jnp.float32
BF16 = jnp.bfloat16
HEADS = 8
HD = 16
C = 128
ROWS = 1024
BLK = 256
EPS = 1e-05
QSCALE = HD ** (-0.5) * math.log2(math.e)
LN2 = math.log(2.0)
GELU_A = math.sqrt(2.0 / math.pi)
GELU_B = 0.044715
PARAMS = pltpu.CompilerParams(vmem_limit_bytes=52 * 1024 * 1024)


def dot(a, b):
    return jnp.dot(a, b, preferred_element_type=F32)


def dot_nt(a, b):
    return lax.dot_general(a, b, (((1,), (1,)), ((), ())), preferred_element_type=F32)


def split2(x):
    hi = x.astype(BF16)
    return hi, (x - hi.astype(F32)).astype(BF16)


def dot3(a, b):
    ah, al = split2(a)
    bh, bl = split2(b)
    return dot(ah, bh) + (dot(al, bh) + dot(ah, bl))


def dot3_nt(a, b):
    ah, al = split2(a)
    bh, bl = split2(b)
    return dot_nt(ah, bh) + (dot_nt(al, bh) + dot_nt(ah, bl))


def norm_rows(values):
    center = values - jnp.mean(values, -1, keepdims=True)
    rstd = lax.rsqrt(jnp.mean(center * center, -1, keepdims=True) + EPS)
    return center * rstd, rstd


def select_matrix(parts, part_of_slot):
    shape = (parts * C, HEADS * C)
    row = lax.broadcasted_iota(jnp.int32, shape, 0)
    col = lax.broadcasted_iota(jnp.int32, shape, 1)
    slot = (col >> 4) & 7
    wanted = jnp.full(shape, parts, jnp.int32)
    for index, part in enumerate(part_of_slot):
        wanted = jnp.where(slot == index, part, wanted)
    hit = (row & 127) == ((col >> 7) * HD + (col & 15))
    hit = hit & ((row >> 7) == wanted)
    return jnp.where(hit, 1.0, 0.0).astype(BF16)


def place(parts, part_of_slot, out_ref, const=None):
    sel = select_matrix(len(parts), part_of_slot)
    packed = jnp.concatenate(parts, axis=1)
    for pair in range(HEADS // 2):
        both = dot(packed, sel[:, pair * 256 : pair * 256 + 256])
        for half in range(2):
            block = both[:, half * C : half * C + C]
            if const is not None:
                block = jnp.where(const(lax.broadcasted_iota(jnp.int32, block.shape, 1)), 1.0, block)
            out_ref[2 * pair + half] = block.astype(BF16)


def tile_key(column, lane):
    return jnp.where((column & 127) == lane, column >> 7, -1).astype(F32).astype(BF16)


def one_hot_tiles(key, tiles):
    one, zero = jnp.ones((), BF16), jnp.zeros((), BF16)
    return jnp.concatenate([jnp.where(key == jnp.full((), t, BF16), one, zero) for t in tiles], axis=1)


def one_hot_rows(row, iota):
    row = jnp.where((row >= 0) & (row < 256), row, 512).astype(F32)
    row = jnp.broadcast_to(row, (16, row.shape[1])).astype(BF16)
    row = jnp.concatenate([row] * 16, axis=0)
    return jnp.where(row == iota, jnp.ones((), BF16), jnp.zeros((), BF16))


def iota_rows(columns):
    return lax.broadcasted_iota(jnp.int32, (256, columns), 0).astype(F32).astype(BF16)


def head_mask(shape, h):
    return (lax.broadcasted_iota(jnp.int32, shape, 1) >> 4) == h


def place_of_device():
    return lax.axis_index("core"), lax.axis_index("grp")


HALF = 528
MESSAGE = 2 * HALF


def pack_kernel(feats, order, parent, cot, w, gain, msg_ref, m0, m1, m2, m3, order_v, parent_v, cot_v, w_v, gain_v, sems):
    _, y = place_of_device()
    copies = [
        pltpu.make_async_copy(source, target, sems.at[index])
        for index, (source, target) in enumerate(
            (
                (order, order_v),
                (parent, parent_v),
                (feats, msg_ref.at[pl.ds(0, ROWS)]),
                (gain, gain_v),
                (w, w_v),
                (cot, cot_v),
            )
        )
    ]
    for copy in copies:
        copy.start()
    for copy in copies:
        copy.wait()
    near = order_v[...] & 8191
    owner = parent_v[...] & 2047
    ids = jnp.concatenate([near >> 6, near & 63, owner >> 6, owner & 63], axis=0)
    msg_ref[ROWS:] = ids.astype(F32).astype(BF16)
    w_high, w_low = split2(w_v[...])
    weights = jnp.concatenate([w_high, w_low], axis=1)
    total = gain_v[...]
    first = total.astype(BF16).astype(F32)
    second = (total - first).astype(BF16).astype(F32)
    third = total - first - second
    row = lax.broadcasted_iota(jnp.int32, (16, 64), 0)
    gains = jnp.where(row == 0, first, jnp.where(row == 1, second, jnp.where(row == 2, third, 0.0)))
    gains = jnp.concatenate([gains, jnp.zeros((16, 192), F32)], axis=1).astype(BF16)
    for k, ref in enumerate((m0, m1, m2, m3)):
        ref[:64] = cot_v[:, pl.ds(pl.multiple_of(((y + k) & 3) * 256, 256), 256)]
        ref[64:128] = weights
        ref[128:] = gains


def pack(feats, order, parent, cot_t, w_t, gain_two):
    return pl.pallas_call(
        pack_kernel,
        in_specs=[pl.BlockSpec(memory_space=pl.ANY)] * 6,
        out_shape=(jax.ShapeDtypeStruct((MESSAGE, C), BF16),) + (jax.ShapeDtypeStruct((144, 256), BF16),) * 4,
        scratch_shapes=[
            pltpu.VMEM((8, C), jnp.int32),
            pltpu.VMEM((8, C), jnp.int32),
            pltpu.VMEM((64, ROWS), BF16),
            pltpu.VMEM((64, C), F32),
            pltpu.VMEM((1, 64), F32),
            pltpu.SemaphoreType.DMA((6,)),
        ],
        compiler_params=PARAMS,
        name="pack",
    )(feats, order, parent, cot_t, w_t, gain_two)


def gather_rows(order_ref, blocks, tab, rep, hil_ref, pid_ref, gord_ref, cnt_ref):
    core, y = place_of_device()
    lane = lax.broadcasted_iota(jnp.int32, (C, C), 1)
    digits = []
    for slot, (rows, ids) in enumerate(blocks):
        for start, part in rows:
            tab[slot, start : start + part.shape[0], :C] = part
        ids = ids.astype(F32)
        gord_ref[slot * 8 : slot * 8 + 8] = (ids[:8] * 64.0 + ids[8:16]).astype(jnp.int32)
        digits.append(ids[16:])
    digits = jnp.concatenate(digits, axis=0)
    turned = digits.T
    for slot in range(8):
        for t in range(8):
            tab[slot, t * C : t * C + C, C:] = jnp.where((lane & ~8) == slot * 16 + t, turned, 0.0).astype(BF16)

    count = jnp.zeros((256, C), F32)
    target = (lax.broadcasted_iota(jnp.int32, (256, C), 0) + (core * 1024 + y * 256)).astype(F32)
    for slot in range(4):
        parents = digits[slot * 16 : slot * 16 + 8] * 64.0 + digits[slot * 16 + 8 : slot * 16 + 16]
        for t in range(8):
            count = count + jnp.where(target == parents[t : t + 1], 1.0, 0.0)
    cnt_ref[...] = jnp.broadcast_to(jnp.sum(count, axis=1, keepdims=True), cnt_ref.shape)

    order = order_ref[...]
    source = (order >> 10) & 7
    slot = (((source >> 2) ^ core) << 2) + ((y - source) & 3)
    index = (slot * ROWS + (order & 1023)).astype(F32)
    for t in range(8):
        column = jnp.broadcast_to(index[t : t + 1], (C, C)).T.astype(jnp.int32)
        rep[t * C : t * C + C] = tile_key(column, lane)
    weight = jnp.where(lax.broadcasted_iota(jnp.int32, (BLK, C), 1) & 8 == 0, 64.0, 1.0)
    for blk in range(ROWS // BLK):
        rows = pl.ds(blk * BLK, BLK)
        away = rep[rows]
        got = jnp.zeros((BLK, 2 * C), F32)
        for slot in range(8):
            got = got + dot(one_hot_tiles(away, range(slot * 8, slot * 8 + 8)), tab[slot])
        hil_ref[rows] = got[:, :C].astype(BF16)
        parent = jnp.sum(got[:, C:] * weight, axis=1, keepdims=True).astype(jnp.int32)
        pid_ref[rows] = jnp.broadcast_to(parent, (BLK, C))


def fwd_kernel(
    order_ref, m0, m1, m2a, m2b, m3, other, gain_ref, wqkv_ref, wout_ref,
    hil_ref, pid_ref, gord_ref, cnt_ref, att_ref, mine_ref, theirs_ref, o_ref, lse_ref,
    tab, rep, qp, kp, vh, vl, ac,
):
    core, y = place_of_device()
    blocks = [
        ([(0, m0[:ROWS])], m0[ROWS:]),
        ([(0, m1[:ROWS])], m1[ROWS:]),
        ([(0, m2a[...]), (HALF, m2b[: ROWS - HALF])], m2b[ROWS - HALF :]),
        ([(0, m3[:ROWS])], m3[ROWS:]),
    ] + [([(0, other[k, :ROWS])], other[k, ROWS:]) for k in range(4)]
    gather_rows(order_ref, blocks, tab, rep, hil_ref, pid_ref, gord_ref, cnt_ref)

    r = hil_ref[...].astype(F32)
    xhat, _ = norm_rows(r)
    u = xhat * gain_ref[...]
    qkv = dot3(u, wqkv_ref[...])
    place(split2(qkv[:, :C] * QSCALE), (0, 0, 1, 1), qp)
    place(split2(qkv[:, C : 2 * C]), (0, 1, 0, 1), kp)
    vh[...], vl[...] = split2(qkv[:, 2 * C :])

    def head(h, carry):
        vmask = head_mask((ROWS, C), h)
        zero = jnp.zeros((), BF16)
        one = jnp.ones((), BF16)
        va = jnp.concatenate([jnp.where(vmask, vh[...], zero), jnp.where(vmask, vl[...], one)], axis=1)
        keys = kp[h]
        mask = head_mask((BLK, C), h)
        for blk in range(ROWS // BLK):
            rows = pl.ds(blk * BLK, BLK)
            s = dot_nt(qp[h, rows], keys)
            m = jnp.max(s, axis=1, keepdims=True)
            ph, plo = split2(jnp.exp2(s - m))
            oa = dot(ph, va) + dot(plo, va)
            first, second = oa[:, :C], oa[:, C:]
            total = pltpu.roll(second, HD, 1)
            o_ref[rows] = jnp.where(mask, (first + second) / total, o_ref[rows])
            lse_ref[rows] = jnp.where(mask, m + jnp.log2(total), lse_ref[rows])
        return carry

    lax.fori_loop(0, HEADS, head, 0)
    att = r + dot3(o_ref[...], wout_ref[...])
    hi, lo = split2(att)
    att_ref[...] = hi
    ac[...] = jnp.concatenate([hi, lo], axis=1)
    parent = pid_ref[...].astype(F32).T[0:1].astype(jnp.int32)
    pid = (((parent >> 10) ^ core) << 10) + ((((parent >> 8) - y) & 3) << 8) + (parent & 255)
    for chunk in range(8):
        sums = dot(one_hot_rows(pid - chunk * 256, iota_rows(ROWS)), ac[...])
        target = mine_ref if chunk < 4 else theirs_ref
        target[chunk & 3] = sums[:, :C] + sums[:, C:]


def attention_forward(order, blocks, gain, w_qkv, w_out):
    return pl.pallas_call(
        fwd_kernel,
        out_shape=(
            jax.ShapeDtypeStruct((ROWS, C), BF16),
            jax.ShapeDtypeStruct((ROWS, C), jnp.int32),
            jax.ShapeDtypeStruct((64, C), jnp.int32),
            jax.ShapeDtypeStruct((256, C), F32),
            jax.ShapeDtypeStruct((ROWS, C), BF16),
            jax.ShapeDtypeStruct((4, 256, C), F32),
            jax.ShapeDtypeStruct((4, 256, C), F32),
            jax.ShapeDtypeStruct((ROWS, C), F32),
            jax.ShapeDtypeStruct((ROWS, C), F32),
        ),
        scratch_shapes=[
            pltpu.VMEM((8, ROWS, 2 * C), BF16),
            pltpu.VMEM((ROWS, C), BF16),
            pltpu.VMEM((HEADS, ROWS, C), BF16),
            pltpu.VMEM((HEADS, ROWS, C), BF16),
            pltpu.VMEM((ROWS, C), BF16),
            pltpu.VMEM((ROWS, C), BF16),
            pltpu.VMEM((ROWS, 2 * C), BF16),
        ],
        compiler_params=PARAMS,
        cost_estimate=pl.CostEstimate(flops=30_000_000_000, bytes_accessed=4_000_000, transcendentals=8_400_000),
        name="attention_forward",
    )(order, *blocks, gain, w_qkv, w_out)


def pool_kernel(mine, theirs, c1, c2, c3, cnt_ref, att_ref, w0, w1, w2, w3, s0, t1, t2, t3, dp_ref, gw_ref, gg_ref):
    cnt = cnt_ref[...]
    pooled = (mine[0] + theirs[0] + c1[...] + c2[...] + c3[...]) / cnt
    msgs = (w0, w1, w2, w3)
    wh = jnp.concatenate([m[64:128, :C] for m in msgs], axis=0)
    wl = jnp.concatenate([m[64:128, C:] for m in msgs], axis=0)
    cot = jnp.concatenate([m[:64] for m in msgs], axis=0).astype(F32).T
    gains = jnp.concatenate([m[128:, :64] for m in msgs], axis=1).astype(F32)
    gain = gains[0:1] + gains[1:2] + gains[2:3]
    ph, plo = split2(pooled)
    normed, rstd = norm_rows(dot_nt(ph, wh) + (dot_nt(plo, wh) + dot_nt(ph, wl)))
    v = normed * gain
    t = jnp.tanh(GELU_A * (v + GELU_B * (v * v * v)))
    s4 = (0.5 * v * (1.0 + t)).T.astype(BF16)
    s0[...] = s4[:64]
    for k, ref in enumerate((t1, t2, t3)):
        block = s4[64 * k + 64 : 64 * k + 128]
        ref[:ROWS] = att_ref[...]
        ref[ROWS : ROWS + 64] = block[:, :C]
        ref[ROWS + 64 :] = block[:, C:]
    slope = 0.5 * (1.0 + t) + 0.5 * v * (1.0 - t * t) * (GELU_A * (1.0 + (3.0 * GELU_B) * (v * v)))
    d_scaled = cot * slope
    d_normed = d_scaled * gain
    d_proj = rstd * (
        d_normed
        - jnp.mean(d_normed, -1, keepdims=True)
        - normed * jnp.mean(d_normed * normed, -1, keepdims=True)
    )
    dh, dl = split2(d_proj)
    dp_ref[...] = (dot(dh, wh) + (dot(dl, wh) + dot(dh, wl))) / cnt
    gw_ref[...] = dot3(d_proj.T, pooled)
    gg = jnp.sum(d_scaled * normed, axis=0, keepdims=True)
    row = lax.broadcasted_iota(jnp.int32, (8, C), 0)
    for k in range(4):
        block = jnp.concatenate([gg[:, 64 * k : 64 * k + 64], jnp.zeros((1, 64), F32)], axis=1)
        gg_ref[k] = jnp.where(row == 1, block, 0.0)


def pooled_section(mine, theirs, chunks, cnt, att, msgs):
    return pl.pallas_call(
        pool_kernel,
        out_shape=(jax.ShapeDtypeStruct((64, 256), BF16),)
        + (jax.ShapeDtypeStruct((ROWS + 128, C), BF16),) * 3
        + (
            jax.ShapeDtypeStruct((256, C), F32),
            jax.ShapeDtypeStruct((256, C), F32),
            jax.ShapeDtypeStruct((4, 8, C), F32),
        ),
        compiler_params=PARAMS,
        name="pooled_section",
    )(mine, theirs, *chunks, cnt, att, *msgs)


PIECE = 104
GRAY_ORDER = (0, 2, 1, 3)


def gray_apart(y, apart):
    code = y ^ (y >> 1) ^ apart
    return code ^ (code >> 1)


def bwd_kernel(
    r_ref, o_ref, lse_ref, gain_ref, wqkv_ref, wout_ref, pid_ref, gw_ref, gg2_ref,
    d0, d1, d2, d3, e0, e1, e2, e3,
    df_ref, keep_ref, send_ref,
    qp, kp, dop, vp, kh, kl, tab, da_ref, dot_t, q_t, dv_t, dk_t, dq_ref, flat,
):
    core, y = place_of_device()
    for chunk, ref in enumerate((d0, d1, d2, d3, e0, e1, e2, e3)):
        hi, lo = split2(ref[...])
        tab[chunk * 256 : chunk * 256 + 256, :C] = hi
        tab[chunk * 256 : chunk * 256 + 256, C:] = lo
    lane = lax.broadcasted_iota(jnp.int32, (BLK, C), 1)
    for blk in range(ROWS // BLK):
        rows = pl.ds(blk * BLK, BLK)
        pid = pid_ref[rows]
        index = (((pid >> 10) ^ core) << 10) + (((y - (pid >> 8)) & 3) << 8) + (pid & 255)
        got = dot(one_hot_tiles(tile_key(index, lane), range(16)), tab[...])
        da_ref[rows] = got[:, :C] + got[:, C:]

    r = r_ref[...].astype(F32)
    xhat, rstd = norm_rows(r)
    u = xhat * gain_ref[...]
    qkv = dot3(u, wqkv_ref[...])
    q = qkv[:, :C] * QSCALE
    qh, ql = split2(q)
    lse = -lse_ref[...]
    l1 = lse.astype(BF16).astype(F32)
    l2 = (lse - l1).astype(BF16).astype(F32)
    l3 = lse - l1 - l2
    which = lax.broadcasted_iota(jnp.int32, (ROWS, C), 1) & 15
    lp = jnp.where(which == 0, l1, jnp.where(which == 1, l2, jnp.where(which == 2, l3, 0.0))).astype(BF16)
    place((qh, ql, lp), (0, 0, 1, 1, 2), qp)
    khi, klo = split2(qkv[:, C : 2 * C])
    place((khi, klo), (0, 1, 0, 1), kp, const=lambda lane: (lane >= 64) & (lane < 67))
    kh[...] = khi
    kl[...] = klo
    place(split2(qkv[:, 2 * C :]), (0, 1, 0, 1), vp, const=lambda lane: (lane >= 64) & (lane < 96))
    da = da_ref[...]
    do = dot3_nt(da, wout_ref[...])
    place((*split2(do), *split2(-do * o_ref[...])), (0, 0, 1, 1, 2, 3), dop)
    for source, target in ((do, dot_t), (q, q_t)):
        hi, lo = split2(source.T)
        for h in range(HEADS):
            target[h, :HD] = hi[h * HD : h * HD + HD]
            target[h, HD:] = lo[h * HD : h * HD + HD]

    def head(h, carry):
        kmask = head_mask((ROWS, C), h)
        zero = jnp.zeros((), BF16)
        ka = jnp.concatenate([jnp.where(kmask, kh[...], zero), jnp.where(kmask, kl[...], zero)], axis=1)
        keys, vals = kp[h], vp[h]
        mask = head_mask((BLK, C), h)
        dv = jnp.zeros((2 * HD, ROWS), F32)
        dk = jnp.zeros((2 * HD, ROWS), F32)
        for blk in range(ROWS // BLK):
            rows = pl.ds(blk * BLK, BLK)
            p = jnp.exp2(dot_nt(qp[h, rows], keys))
            ds = p * dot_nt(dop[h, rows], vals)
            ph, plo = split2(p)
            sh, sl = split2(ds)
            left = dot_t[h, :, rows]
            dv = dv + (dot(left, ph) + dot(left, plo))
            left = q_t[h, :, rows]
            dk = dk + (dot(left, sh) + dot(left, sl))
            dq = dot(sh, ka) + dot(sl, ka)
            dq_ref[rows] = jnp.where(mask, dq[:, :C] + dq[:, C:], dq_ref[rows])
        place_rows = pl.ds(pl.multiple_of(h * HD, HD), HD)
        dv_t[place_rows] = dv[:HD] + dv[HD:]
        dk_t[place_rows] = dk[:HD] + dk[HD:]
        return carry

    lax.fori_loop(0, HEADS, head, 0)
    grads = jnp.concatenate([dq_ref[...] * HD ** (-0.5), dk_t[...].T * LN2, dv_t[...].T], axis=1)
    du = dot3_nt(grads, wqkv_ref[...])
    gq = dot3(u.T, grads)
    for part in range(3):
        flat[part * C : part * C + C] = gq[:, part * C : part * C + C]
    flat[3 * C :] = dot3(o_ref[...].T, da)
    gain_one = jnp.sum(du * xhat, axis=0, keepdims=True)
    row = lax.broadcasted_iota(jnp.int32, (8, C), 0)
    for side, ref in enumerate((keep_ref, send_ref)):
        half = core ^ side
        for index, apart in enumerate(GRAY_ORDER):
            owner = gray_apart(y, apart)
            ref[index, :64] = flat[pl.ds(pl.multiple_of((owner * 2 + half) * 64, 64), 64)]
            block = (y - owner) & 3
            ref[index, 64:96] = gw_ref[pl.ds(pl.multiple_of(block * 64 + half * 32, 32), 32)]
            ref[index, 96:] = jnp.where(row == 0, gain_one, gg2_ref[block])
    dn = du * gain_ref[...]
    dx = rstd * (dn - jnp.mean(dn, -1, keepdims=True) - xhat * jnp.mean(dn * xhat, -1, keepdims=True))
    df_ref[...] = (da + dx).astype(BF16)


def attention_backward(rows, o, lse, gain, w_qkv, w_out, pid, grad_pool, grad_gain_two, d_pooled):
    return pl.pallas_call(
        bwd_kernel,
        out_shape=(
            jax.ShapeDtypeStruct((ROWS, C), BF16),
            jax.ShapeDtypeStruct((4, PIECE, C), F32),
            jax.ShapeDtypeStruct((4, PIECE, C), F32),
        ),
        scratch_shapes=[
            pltpu.VMEM((HEADS, ROWS, C), BF16),
            pltpu.VMEM((HEADS, ROWS, C), BF16),
            pltpu.VMEM((HEADS, ROWS, C), BF16),
            pltpu.VMEM((HEADS, ROWS, C), BF16),
            pltpu.VMEM((ROWS, C), BF16),
            pltpu.VMEM((ROWS, C), BF16),
            pltpu.VMEM((2048, 2 * C), BF16),
            pltpu.VMEM((ROWS, C), F32),
            pltpu.VMEM((HEADS, 2 * HD, ROWS), BF16),
            pltpu.VMEM((HEADS, 2 * HD, ROWS), BF16),
            pltpu.VMEM((C, ROWS), F32),
            pltpu.VMEM((C, ROWS), F32),
            pltpu.VMEM((ROWS, C), F32),
            pltpu.VMEM((4 * C, C), F32),
        ],
        compiler_params=PARAMS,
        cost_estimate=pl.CostEstimate(flops=90_000_000_000, bytes_accessed=8_000_000, transcendentals=8_400_000),
        name="attention_backward",
    )(rows, o, lse, gain, w_qkv, w_out, pid, grad_pool, grad_gain_two, *d_pooled)


def rows_kernel(gord_ref, a0, a1, a2, a3, ao, f0, f1, f2a, f2b, f3, fo, s0, s3_ref, gf_ref, s4_ref):
    core, y = place_of_device()
    att = [a0[...], a1[:ROWS], a2[:ROWS], a3[:ROWS]] + [ao[k] for k in range(4)]
    opposite = jnp.concatenate([f2a[...], f2b[...]], axis=0)
    grad = [f0[...], f1[...], opposite, f3[...]] + [fo[k] for k in range(4)]
    first = (core * 4 + y) * ROWS
    iota = iota_rows(C)
    for blk in range(ROWS // BLK):
        got = jnp.zeros((BLK, 2 * C), F32)
        for slot in range(8):
            hot = jnp.concatenate(
                [
                    one_hot_rows(gord_ref[slot * 8 + t : slot * 8 + t + 1] - (first + blk * BLK), iota)
                    for t in range(8)
                ],
                axis=1,
            )
            got = got + dot(hot, jnp.concatenate([att[slot], grad[slot]], axis=1))
        s3_ref[blk * BLK : blk * BLK + BLK] = got[:, :C].astype(BF16)
        gf_ref[blk * BLK : blk * BLK + BLK] = got[:, C:].astype(BF16)
    s4_ref[:, pl.ds(pl.multiple_of(y * 256, 256), 256)] = s0[...]
    for k, ref in ((1, a3), (2, a2), (3, a1)):
        block = jnp.concatenate([ref[ROWS : ROWS + 64], ref[ROWS + 64 :]], axis=1)
        s4_ref[:, pl.ds(pl.multiple_of(((y + k) & 3) * 256, 256), 256)] = block


def results(gord, att, grad, s4):
    return pl.pallas_call(
        rows_kernel,
        out_shape=(
            jax.ShapeDtypeStruct((ROWS, C), BF16),
            jax.ShapeDtypeStruct((ROWS, C), BF16),
            jax.ShapeDtypeStruct((64, ROWS), BF16),
        ),
        compiler_params=PARAMS,
        cost_estimate=pl.CostEstimate(flops=8_000_000_000, bytes_accessed=5_000_000, transcendentals=0),
        name="rows_to_z_order",
    )(gord, *att, *grad, s4)


def params_kernel(mine, theirs, gq_ref, go_ref, g1_ref, gw_ref, g2_ref, flat, gains):
    core, y = place_of_device()
    for side, ref in enumerate((mine, theirs)):
        half = core ^ side
        for index, apart in enumerate(GRAY_ORDER):
            piece = gray_apart(y, apart) * 2 + half
            flat[pl.ds(pl.multiple_of(piece * 64, 64), 64)] = ref[index, :64]
            gains[pl.ds(pl.multiple_of(piece * 8, 8), 8)] = ref[index, 96:]
        gw_ref[pl.ds(pl.multiple_of(half * 32, 32), 32)] = ref[0, 64:96]
    for part in range(3):
        gq_ref[:, part * C : part * C + C] = flat[part * C : part * C + C]
    go_ref[...] = flat[3 * C :]
    g1_ref[...] = gains[0:1]
    g2_ref[...] = gains[pl.ds(pl.multiple_of(y * 16, 16), 8)][1:2, :64]


def parameter_results(mine, theirs):
    return pl.pallas_call(
        params_kernel,
        out_shape=(
            jax.ShapeDtypeStruct((C, 3 * C), F32),
            jax.ShapeDtypeStruct((C, C), F32),
            jax.ShapeDtypeStruct((1, C), F32),
            jax.ShapeDtypeStruct((64, C), F32),
            jax.ShapeDtypeStruct((1, 64), F32),
        ),
        scratch_shapes=[pltpu.VMEM((4 * C, C), F32), pltpu.VMEM((64, C), F32)],
        compiler_params=PARAMS,
        name="parameter_results",
    )(mine, theirs)


def shift(block, axis, apart):
    count = lax.axis_size(axis)
    return lax.ppermute(block, axis, [(i, (i + apart) % count) for i in range(count)])


NEAR = ((0, 1), (2, 3))
FAR = ((0, 3), (1, 2))


def swap(block, axis, pairs):
    return lax.ppermute(block, axis, [edge for a, b in pairs for edge in ((a, b), (b, a))])


def sum_axis(block, axis):
    for pairs in (NEAR, FAR):
        block = block + swap(block, axis, pairs)
    return block


def relay_y(block):
    half = block.shape[0] // 2
    left = shift(block, "grp", 1)
    right = shift(block, "grp", -1)
    return left, shift(right[:half], "grp", -1), shift(left[half:], "grp", 1), right


def shards(feats, order, parent, gain_one, w_qkv, w_out, w_pool, gain_two, cotangent):
    order = order.reshape(8, C)
    msg, *w_msgs = pack(feats, order, parent.reshape(8, C), cotangent.T, w_pool.T, gain_two[None])

    around = relay_y(msg)
    w_msgs = [w_msgs[0]] + [shift(w_msgs[k], "grp", k) for k in (1, 2, 3)]
    other = shift(jnp.concatenate((msg, *around), axis=0).reshape(4, MESSAGE, C), "core", 1)
    hilbert, pid, gord, cnt, att, mine, theirs, o, lse = attention_forward(
        order, (msg, *around, other), gain_one[None], w_qkv, w_out
    )

    theirs = shift(theirs, "core", 1)
    chunks = [shift(mine[k] + theirs[k], "grp", k) for k in (1, 2, 3)]
    s4, *rows, d_pool, grad_pool, grad_gain_two = pooled_section(mine, theirs, chunks, cnt, att, w_msgs)
    own = [d_pool] + [shift(d_pool, "grp", k) for k in (1, 2, 3)]
    d_pooled = own + [shift(block, "core", 1) for block in own]

    from_y = [shift(rows[k - 1], "grp", -k) for k in (3, 2, 1)]
    att = [att] + from_y
    att.append(shift(jnp.stack([block[:ROWS] for block in att]), "core", 1))

    df, keep, send = attention_backward(
        hilbert, o, lse, gain_one[None], w_qkv, w_out, pid, grad_pool, grad_gain_two, d_pooled
    )
    around = relay_y(df)
    df_other = shift(jnp.concatenate((df, *around), axis=0).reshape(4, ROWS, C), "core", 1)
    section_three, grad_feats, section_four = results(gord, att, (df, *around, df_other), s4)

    kept = keep + shift(send, "core", 1)
    kept = kept[:2] + swap(kept[2:], "grp", NEAR)
    piece = kept[0] + swap(kept[1], "grp", FAR)
    piece = sum_axis(sum_axis(piece, "x"), "z")
    two = jnp.stack([piece, swap(piece, "grp", FAR)])
    four = jnp.concatenate([two, swap(two, "grp", NEAR)])
    g_qkv, g_out, g_one, g_pool, g_two = parameter_results(four, shift(four, "core", 1))
    return (section_four.T, section_three, grad_feats, g_one[0], g_qkv, g_out, g_pool.T, g_two[0])


def solution(mesh):
    fine = Mesh(mesh.devices.reshape(4, 4, 2, 4), ("x", "z", "core", "grp"))
    pts = ("x", "z", "core")
    everywhere = pts + ("grp",)
    placed = (
        P(everywhere, None),
        P(everywhere),
        P(everywhere),
        P(),
        P(),
        P(),
        P(None, "grp"),
        P("grp"),
        P(pts, "grp"),
    )
    return jax.shard_map(
        shards,
        mesh=fine,
        in_specs=placed,
        out_specs=(
            P(pts, "grp"),
            P(everywhere, None),
            P(everywhere, None),
            P(),
            P(),
            P(),
            P(None, "grp"),
            P("grp"),
        ),
        check_vma=False,
    )
```

```python
import math

import jax
import jax.numpy as jnp
from jax import lax
from jax.experimental import pallas as pl
from jax.experimental.pallas import tpu as pltpu
from jax.sharding import Mesh, PartitionSpec as P

F32 = jnp.float32
BF16 = jnp.bfloat16
HEADS = 8
HD = 16
C = 128
ROWS = 1024
FBLK = 128
SBLK = 256
UNROLL = 4
BBLK = 256
GBLK = 256
DBLK = 256
RBLK = 256
EPS = 1e-05
QSCALE = HD ** (-0.5) * math.log2(math.e)
LN2 = math.log(2.0)
GELU_A = math.sqrt(2.0 / math.pi)
GELU_B = 0.044715


def vmem(mib):
    return pltpu.CompilerParams(vmem_limit_bytes=mib * 1024 * 1024)


def dot(a, b):
    return jnp.dot(a, b, preferred_element_type=F32)


def dot_nt(a, b):
    return lax.dot_general(a, b, (((1,), (1,)), ((), ())), preferred_element_type=F32)


def split2(x):
    hi = x.astype(BF16)
    return hi, (x - hi.astype(F32)).astype(BF16)


def dot3(a, b):
    ah, al = split2(a)
    bh, bl = split2(b)
    return dot(ah, bh) + (dot(al, bh) + dot(ah, bl))


def dot3_nt(a, b):
    ah, al = split2(a)
    bh, bl = split2(b)
    return dot_nt(ah, bh) + (dot_nt(al, bh) + dot_nt(ah, bl))


def norm_rows(values):
    center = values - jnp.mean(values, -1, keepdims=True)
    rstd = lax.rsqrt(jnp.mean(center * center, -1, keepdims=True) + EPS)
    return center * rstd, rstd


def select_matrix(parts, part_of_slot):
    shape = (parts * C, HEADS * C)
    row = lax.broadcasted_iota(jnp.int32, shape, 0)
    col = lax.broadcasted_iota(jnp.int32, shape, 1)
    slot = (col >> 4) & 7
    wanted = jnp.full(shape, parts, jnp.int32)
    for index, part in enumerate(part_of_slot):
        wanted = jnp.where(slot == index, part, wanted)
    hit = (row & 127) == ((col >> 7) * HD + (col & 15))
    hit = hit & ((row >> 7) == wanted)
    return jnp.where(hit, 1.0, 0.0).astype(BF16)


def place(parts, part_of_slot, out_ref, const=None):
    sel = select_matrix(len(parts), part_of_slot)
    packed = jnp.concatenate(parts, axis=1)
    for pair in range(HEADS // 2):
        both = dot(packed, sel[:, pair * 256 : pair * 256 + 256])
        for half in range(2):
            block = both[:, half * C : half * C + C]
            if const is not None:
                block = jnp.where(const(lax.broadcasted_iota(jnp.int32, block.shape, 1)), 1.0, block)
            out_ref[2 * pair + half] = block.astype(BF16)


def tile_key(column, lane):
    return jnp.where((column & 127) == lane, column >> 7, -1).astype(F32).astype(BF16)


def one_hot_tiles(key, tiles):
    one, zero = jnp.ones((), BF16), jnp.zeros((), BF16)
    return jnp.concatenate([jnp.where(key == jnp.full((), t, BF16), one, zero) for t in tiles], axis=1)


def one_hot_rows(row, iota):
    row = jnp.where((row >= 0) & (row < 256), row, 512).astype(F32)
    row = jnp.broadcast_to(row, (16, row.shape[1])).astype(BF16)
    row = jnp.concatenate([row] * (iota.shape[0] // 16), axis=0)
    return jnp.where(row == iota, jnp.ones((), BF16), jnp.zeros((), BF16))


def iota_rows(columns):
    return lax.broadcasted_iota(jnp.int32, (256, columns), 0).astype(F32).astype(BF16)


def head_norms(x):
    row = lax.broadcasted_iota(jnp.int32, (C, C), 0)
    col = lax.broadcasted_iota(jnp.int32, (C, C), 1)
    same = jnp.where((row >> 4) == (col >> 4), 1.0, 0.0).astype(BF16)
    return jnp.max(dot((x * x * 1.02).astype(BF16), same), axis=0, keepdims=True)


def head_mask(shape, h):
    return (lax.broadcasted_iota(jnp.int32, shape, 1) >> 4) == h


def place_of_device():
    return lax.axis_index("core"), lax.axis_index("grp")


HALF = 528
MESSAGE = 2 * HALF


def pack_kernel(feats, order, parent, cot, w, gain, msg_ref, m0, m1, m2, m3, order_v, parent_v, cot_v, w_v, gain_v, sems):
    _, y = place_of_device()
    copies = [
        pltpu.make_async_copy(source, target, sems.at[index])
        for index, (source, target) in enumerate(
            (
                (order, order_v),
                (parent, parent_v),
                (feats, msg_ref.at[pl.ds(0, ROWS)]),
                (gain, gain_v),
                (w, w_v),
                (cot, cot_v),
            )
        )
    ]
    for copy in copies:
        copy.start()
    for copy in copies:
        copy.wait()
    near = order_v[...] & 8191
    owner = parent_v[...] & 2047
    ids = jnp.concatenate([near >> 6, near & 63, owner >> 6, owner & 63], axis=0)
    msg_ref[ROWS:] = ids.astype(F32).astype(BF16)
    w_high, w_low = split2(w_v[...])
    weights = jnp.concatenate([w_high, w_low], axis=1)
    total = gain_v[...]
    first = total.astype(BF16).astype(F32)
    second = (total - first).astype(BF16).astype(F32)
    third = total - first - second
    row = lax.broadcasted_iota(jnp.int32, (16, 64), 0)
    gains = jnp.where(row == 0, first, jnp.where(row == 1, second, jnp.where(row == 2, third, 0.0)))
    gains = jnp.concatenate([gains, jnp.zeros((16, 192), F32)], axis=1).astype(BF16)
    for k, ref in enumerate((m0, m1, m2, m3)):
        ref[:64] = cot_v[:, pl.ds(pl.multiple_of(((y + k) & 3) * 256, 256), 256)]
        ref[64:128] = weights
        ref[128:] = gains


def pack(feats, order, parent, cot_t, w_t, gain_two):
    return pl.pallas_call(
        pack_kernel,
        in_specs=[pl.BlockSpec(memory_space=pltpu.HBM)] * 6,
        out_shape=(jax.ShapeDtypeStruct((MESSAGE, C), BF16),) + (jax.ShapeDtypeStruct((144, 256), BF16),) * 4,
        scratch_shapes=[
            pltpu.VMEM((8, C), jnp.int32),
            pltpu.VMEM((8, C), jnp.int32),
            pltpu.VMEM((64, ROWS), BF16),
            pltpu.VMEM((64, C), F32),
            pltpu.VMEM((1, 64), F32),
            pltpu.SemaphoreType.DMA((6,)),
        ],
        compiler_params=vmem(8),
        name="pack",
    )(feats, order, parent, cot_t, w_t, gain_two)


def gather_rows(order_ref, blocks, tab, rep, hil_ref, pid_ref, gord_ref, cnt_ref):
    core, y = place_of_device()
    lane = lax.broadcasted_iota(jnp.int32, (C, C), 1)
    digits = []
    for slot, (rows, ids) in enumerate(blocks):
        for start, part in rows:
            tab[slot, start : start + part.shape[0], :C] = part
        ids = ids.astype(F32)
        gord_ref[slot * 8 : slot * 8 + 8] = (ids[:8] * 64.0 + ids[8:16]).astype(jnp.int32)
        digits.append(ids[16:])
    digits = jnp.concatenate(digits, axis=0)
    turned = digits.T
    for slot in range(8):
        for t in range(8):
            tab[slot, t * C : t * C + C, C:] = jnp.where((lane & ~8) == slot * 16 + t, turned, 0.0).astype(BF16)

    count = jnp.zeros((256, C), F32)
    target = (lax.broadcasted_iota(jnp.int32, (256, C), 0) + (core * 1024 + y * 256)).astype(F32)
    for slot in range(4):
        parents = digits[slot * 16 : slot * 16 + 8] * 64.0 + digits[slot * 16 + 8 : slot * 16 + 16]
        for t in range(8):
            count = count + jnp.where(target == parents[t : t + 1], 1.0, 0.0)
    cnt_ref[...] = jnp.broadcast_to(jnp.sum(count, axis=1, keepdims=True), cnt_ref.shape)

    order = order_ref[...]
    source = (order >> 10) & 7
    slot = (((source >> 2) ^ core) << 2) + ((y - source) & 3)
    index = (slot * ROWS + (order & 1023)).astype(F32)
    for t in range(8):
        column = jnp.broadcast_to(index[t : t + 1], (C, C)).T.astype(jnp.int32)
        rep[t * C : t * C + C] = tile_key(column, lane)
    weight = jnp.where(lax.broadcasted_iota(jnp.int32, (GBLK, C), 1) & 8 == 0, 64.0, 1.0)
    for blk in range(ROWS // GBLK):
        rows = pl.ds(blk * GBLK, GBLK)
        away = rep[rows]
        got = jnp.zeros((GBLK, 2 * C), F32)
        for slot in range(8):
            got = got + dot(one_hot_tiles(away, range(slot * 8, slot * 8 + 8)), tab[slot])
        hil_ref[rows] = got[:, :C].astype(BF16)
        parent = jnp.sum(got[:, C:] * weight, axis=1, keepdims=True).astype(jnp.int32)
        pid_ref[rows] = jnp.broadcast_to(parent, (GBLK, C))


def fwd_kernel(
    order_ref, m0, m1, m2a, m2b, m3, other, gain_ref, wqkv_ref, wout_ref,
    hil_ref, pid_ref, gord_ref, cnt_ref, att_ref, mine_ref, theirs_ref, o_ref, ot_ref, lse_ref,
    tab, rep, qp, kp, vt, lt, ac,
):
    core, y = place_of_device()
    blocks = [
        ([(0, m0[:ROWS])], m0[ROWS:]),
        ([(0, m1[:ROWS])], m1[ROWS:]),
        ([(0, m2a[...]), (HALF, m2b[: ROWS - HALF])], m2b[ROWS - HALF :]),
        ([(0, m3[:ROWS])], m3[ROWS:]),
    ] + [([(0, other[k, :ROWS])], other[k, ROWS:]) for k in range(4)]
    gather_rows(order_ref, blocks, tab, rep, hil_ref, pid_ref, gord_ref, cnt_ref)

    r = hil_ref[...].astype(F32)
    xhat, _ = norm_rows(r)
    u = xhat * gain_ref[...]
    qkv = dot3(u, wqkv_ref[...])
    q = qkv[:, :C] * QSCALE
    k = qkv[:, C : 2 * C]
    place(split2(q), (0, 0, 1, 1), qp)
    place(split2(k), (0, 1, 0, 1), kp)
    for index, part in enumerate(split2(qkv[:, 2 * C :].T)):
        for h in range(HEADS):
            vt[h, index * HD : index * HD + HD] = part[h * HD : h * HD + HD]
    vt[:, 2 * HD :] = jnp.ones((HEADS, HD, ROWS), BF16)

    def head(size, shifted):
        def body(h, carry):
            keys = kp[h]
            values = vt[h]
            own = pl.ds(pl.multiple_of(h * HD, HD), HD)
            for blk in range(ROWS // size):
                cols = pl.ds(blk * size, size)
                s = dot_nt(keys, qp[h, cols])
                if shifted:
                    m = jnp.max(s, axis=0, keepdims=True)
                    s = s - m
                ph, plo = split2(jnp.exp2(s))
                oa = dot(values, ph) + dot(values, plo)
                total = oa[2 * HD : 2 * HD + 1]
                ot_ref[own, cols] = (oa[:HD] + oa[HD : 2 * HD]) / total
                lse = jnp.log2(total)
                if shifted:
                    lse = lse + m
                lt[own, cols] = jnp.broadcast_to(lse, (HD, size))
            return carry

        return body

    small = jnp.max(head_norms(q) * head_norms(k)) < 3600.0

    @pl.when(small)
    def _():
        lax.fori_loop(0, HEADS, head(FBLK, False), 0, unroll=UNROLL)

    @pl.when(jnp.logical_not(small))
    def _():
        lax.fori_loop(0, HEADS, head(SBLK, True), 0)

    o_ref[...] = ot_ref[...].T
    lse_ref[...] = lt[...].T
    att = r + dot3(o_ref[...], wout_ref[...])
    hi, lo = split2(att)
    att_ref[...] = hi
    ac[...] = jnp.concatenate([hi, lo], axis=1)
    parent = pid_ref[...].astype(F32).T[0:1].astype(jnp.int32)
    pid = (((parent >> 10) ^ core) << 10) + ((((parent >> 8) - y) & 3) << 8) + (parent & 255)
    for chunk in range(8):
        sums = dot(one_hot_rows(pid - chunk * 256, iota_rows(ROWS)), ac[...])
        target = mine_ref if chunk < 4 else theirs_ref
        target[chunk & 3] = sums[:, :C] + sums[:, C:]


def attention_forward(order, blocks, gain, w_qkv, w_out):
    return pl.pallas_call(
        fwd_kernel,
        out_shape=(
            jax.ShapeDtypeStruct((ROWS, C), BF16),
            jax.ShapeDtypeStruct((ROWS, C), jnp.int32),
            jax.ShapeDtypeStruct((64, C), jnp.int32),
            jax.ShapeDtypeStruct((256, C), F32),
            jax.ShapeDtypeStruct((ROWS, C), BF16),
            jax.ShapeDtypeStruct((4, 256, C), F32),
            jax.ShapeDtypeStruct((4, 256, C), F32),
            jax.ShapeDtypeStruct((ROWS, C), F32),
            jax.ShapeDtypeStruct((C, ROWS), F32),
            jax.ShapeDtypeStruct((ROWS, C), F32),
        ),
        scratch_shapes=[
            pltpu.VMEM((8, ROWS, 2 * C), BF16),
            pltpu.VMEM((ROWS, C), BF16),
            pltpu.VMEM((HEADS, ROWS, C), BF16),
            pltpu.VMEM((HEADS, ROWS, C), BF16),
            pltpu.VMEM((HEADS, 3 * HD, ROWS), BF16),
            pltpu.VMEM((C, ROWS), F32),
            pltpu.VMEM((ROWS, 2 * C), BF16),
        ],
        compiler_params=vmem(30),
        cost_estimate=pl.CostEstimate(flops=30_000_000_000, bytes_accessed=4_000_000, transcendentals=8_400_000),
        name="attention_forward",
    )(order, *blocks, gain, w_qkv, w_out)


def pool_kernel(mine, theirs, c1, c2, c3, cnt_ref, att_ref, w0, w1, w2, w3, s0, t1, t2, t3, dp_ref, gw_ref, gg_ref):
    cnt = cnt_ref[...]
    pooled = (mine[0] + theirs[0] + c1[...] + c2[...] + c3[...]) / cnt
    msgs = (w0, w1, w2, w3)
    wh = jnp.concatenate([m[64:128, :C] for m in msgs], axis=0)
    wl = jnp.concatenate([m[64:128, C:] for m in msgs], axis=0)
    cot = jnp.concatenate([m[:64] for m in msgs], axis=0).astype(F32).T
    gains = jnp.concatenate([m[128:, :64] for m in msgs], axis=1).astype(F32)
    gain = gains[0:1] + gains[1:2] + gains[2:3]
    ph, plo = split2(pooled)
    normed, rstd = norm_rows(dot_nt(ph, wh) + (dot_nt(plo, wh) + dot_nt(ph, wl)))
    v = normed * gain
    t = jnp.tanh(GELU_A * (v + GELU_B * (v * v * v)))
    s4 = (0.5 * v * (1.0 + t)).T.astype(BF16)
    s0[...] = s4[:64]
    for k, ref in enumerate((t1, t2, t3)):
        block = s4[64 * k + 64 : 64 * k + 128]
        ref[:ROWS] = att_ref[...]
        ref[ROWS : ROWS + 64] = block[:, :C]
        ref[ROWS + 64 :] = block[:, C:]
    slope = 0.5 * (1.0 + t) + 0.5 * v * (1.0 - t * t) * (GELU_A * (1.0 + (3.0 * GELU_B) * (v * v)))
    d_scaled = cot * slope
    d_normed = d_scaled * gain
    d_proj = rstd * (
        d_normed
        - jnp.mean(d_normed, -1, keepdims=True)
        - normed * jnp.mean(d_normed * normed, -1, keepdims=True)
    )
    dh, dl = split2(d_proj)
    dp_ref[...] = (dot(dh, wh) + (dot(dl, wh) + dot(dh, wl))) / cnt
    _, y = place_of_device()
    gw = dot3(d_proj.T, pooled)
    gg = jnp.sum(d_scaled * normed, axis=0, keepdims=True)
    gains = jnp.zeros((8, C), F32)
    row = lax.broadcasted_iota(jnp.int32, (8, C), 0)
    low = lax.broadcasted_iota(jnp.int32, (8, C), 1) < 64
    for k in range(4):
        owner = (y - k) & 3
        gw_ref[pl.ds(pl.multiple_of(owner * 64, 64), 64)] = gw[64 * k : 64 * k + 64]
        block = gg[:, 64 * k : 64 * k + 64]
        twice = jnp.concatenate([block, block], axis=1)
        hit = (row == 1 + (owner >> 1)) & (low == ((owner & 1) == 0))
        gains = jnp.where(hit, twice, gains)
    gg_ref[...] = gains


def pooled_section(mine, theirs, chunks, cnt, att, msgs):
    return pl.pallas_call(
        pool_kernel,
        out_shape=(jax.ShapeDtypeStruct((64, 256), BF16),)
        + (jax.ShapeDtypeStruct((ROWS + 128, C), BF16),) * 3
        + (
            jax.ShapeDtypeStruct((256, C), F32),
            jax.ShapeDtypeStruct((256, C), F32),
            jax.ShapeDtypeStruct((8, C), F32),
        ),
        compiler_params=vmem(12),
        name="pooled_section",
    )(mine, theirs, *chunks, cnt, att, *msgs)


def stack_heads(source, target):
    hi, lo = split2(source.T)
    for h in range(HEADS):
        target[h, :HD] = hi[h * HD : h * HD + HD]
        target[h, HD:] = lo[h * HD : h * HD + HD]


def prep_kernel(r_ref, lse_ref, gain_ref, wqkv_ref, qp, kp, vp, kh, kl, q_t):
    xhat, _ = norm_rows(r_ref[...].astype(F32))
    u = xhat * gain_ref[...]
    qkv = dot3(u, wqkv_ref[...])
    q = qkv[:, :C] * QSCALE
    qh, ql = split2(q)
    lse = -lse_ref[...]
    l1 = lse.astype(BF16).astype(F32)
    l2 = (lse - l1).astype(BF16).astype(F32)
    l3 = lse - l1 - l2
    which = lax.broadcasted_iota(jnp.int32, (ROWS, C), 1) & 15
    lp = jnp.where(which == 0, l1, jnp.where(which == 1, l2, jnp.where(which == 2, l3, 0.0))).astype(BF16)
    place((qh, ql, lp), (0, 0, 1, 1, 2), qp)
    khi, klo = split2(qkv[:, C : 2 * C])
    place((khi, klo), (0, 1, 0, 1), kp, const=lambda lane: (lane >= 64) & (lane < 67))
    kh[...] = khi
    kl[...] = klo
    place(split2(qkv[:, 2 * C :]), (0, 1, 0, 1), vp, const=lambda lane: (lane >= 64) & (lane < 96))
    stack_heads(q, q_t)


def backward_operands(rows, lse, gain, w_qkv):
    return pl.pallas_call(
        prep_kernel,
        out_shape=(jax.ShapeDtypeStruct((HEADS, ROWS, C), BF16),) * 3
        + (jax.ShapeDtypeStruct((ROWS, C), BF16),) * 2
        + (jax.ShapeDtypeStruct((HEADS, 2 * HD, ROWS), BF16),),
        compiler_params=vmem(24),
        cost_estimate=pl.CostEstimate(flops=6_000_000_000, bytes_accessed=8_000_000, transcendentals=0),
        name="backward_operands",
    )(rows, lse, gain, w_qkv)


def bwd_kernel(
    r_ref, o_ref, ot_ref, gain_ref, wqkv_ref, wout_ref, pid_ref, gw_ref, gg2_ref,
    qp, kp, vp, kh, kl, q_t, d0, d1, d2, d3, e0, e1, e2, e3,
    df_ref, flat,
    dop, tab, da_ref, dot_t, dv_t, dk_t, dq_ref,
):
    core, y = place_of_device()
    for chunk, ref in enumerate((d0, d1, d2, d3, e0, e1, e2, e3)):
        hi, lo = split2(ref[...])
        tab[chunk * 256 : chunk * 256 + 256, :C] = hi
        tab[chunk * 256 : chunk * 256 + 256, C:] = lo
    lane = lax.broadcasted_iota(jnp.int32, (DBLK, C), 1)
    for blk in range(ROWS // DBLK):
        rows = pl.ds(blk * DBLK, DBLK)
        pid = pid_ref[rows]
        index = (((pid >> 10) ^ core) << 10) + (((y - (pid >> 8)) & 3) << 8) + (pid & 255)
        got = dot(one_hot_tiles(tile_key(index, lane), range(16)), tab[...])
        da_ref[rows] = got[:, :C] + got[:, C:]

    da = da_ref[...]
    do = dot3_nt(da, wout_ref[...])
    place((*split2(do), *split2(-do * o_ref[...])), (0, 0, 1, 1, 2, 3), dop)
    stack_heads(do, dot_t)

    def head(h, carry):
        kmask = head_mask((ROWS, C), h)
        zero = jnp.zeros((), BF16)
        ka = jnp.concatenate([jnp.where(kmask, kh[...], zero), jnp.where(kmask, kl[...], zero)], axis=1)
        keys, vals = kp[h], vp[h]
        mask = head_mask((BBLK, C), h)
        dv = jnp.zeros((2 * HD, ROWS), F32)
        dk = jnp.zeros((2 * HD, ROWS), F32)
        for blk in range(ROWS // BBLK):
            rows = pl.ds(blk * BBLK, BBLK)
            p = jnp.exp2(dot_nt(qp[h, rows], keys))
            ds = p * dot_nt(dop[h, rows], vals)
            ph, plo = split2(p)
            sh, sl = split2(ds)
            left = dot_t[h, :, rows]
            dv = dv + (dot(left, ph) + dot(left, plo))
            left = q_t[h, :, rows]
            dk = dk + (dot(left, sh) + dot(left, sl))
            dq = dot(sh, ka) + dot(sl, ka)
            dq_ref[rows] = jnp.where(mask, dq[:, :C] + dq[:, C:], dq_ref[rows])
        place_rows = pl.ds(pl.multiple_of(h * HD, HD), HD)
        dv_t[place_rows] = dv[:HD] + dv[HD:]
        dk_t[place_rows] = dk[:HD] + dk[HD:]
        return carry

    lax.fori_loop(0, HEADS, head, 0, unroll=UNROLL)
    xhat, rstd = norm_rows(r_ref[...].astype(F32))
    u = xhat * gain_ref[...]
    grads = jnp.concatenate([dq_ref[...] * HD ** (-0.5), dk_t[...].T * LN2, dv_t[...].T], axis=1)
    du = dot3_nt(grads, wqkv_ref[...])
    gq = dot3(u.T, grads)
    for part in range(3):
        flat[part * C : part * C + C] = gq[:, part * C : part * C + C]
    flat[3 * C : 4 * C] = dot3(ot_ref[...], da)
    flat[4 * C : 6 * C] = gw_ref[...]
    row = lax.broadcasted_iota(jnp.int32, (8, C), 0)
    gains = jnp.where(row == 0, jnp.sum(du * xhat, axis=0, keepdims=True), gg2_ref[...])
    flat[6 * C : 6 * C + 8] = gains
    flat[6 * C + 8 :] = jnp.zeros((2 * C - 8, C), F32)
    dn = du * gain_ref[...]
    dx = rstd * (dn - jnp.mean(dn, -1, keepdims=True) - xhat * jnp.mean(dn * xhat, -1, keepdims=True))
    df_ref[...] = (da + dx).astype(BF16)


def attention_backward(rows, o, o_t, gain, w_qkv, w_out, pid, grad_pool, grad_gain_two, operands, d_pooled):
    return pl.pallas_call(
        bwd_kernel,
        out_shape=(jax.ShapeDtypeStruct((ROWS, C), BF16), jax.ShapeDtypeStruct((8 * C, C), F32)),
        scratch_shapes=[
            pltpu.VMEM((HEADS, ROWS, C), BF16),
            pltpu.VMEM((2048, 2 * C), BF16),
            pltpu.VMEM((ROWS, C), F32),
            pltpu.VMEM((HEADS, 2 * HD, ROWS), BF16),
            pltpu.VMEM((C, ROWS), F32),
            pltpu.VMEM((C, ROWS), F32),
            pltpu.VMEM((ROWS, C), F32),
        ],
        compiler_params=vmem(34),
        cost_estimate=pl.CostEstimate(flops=90_000_000_000, bytes_accessed=8_000_000, transcendentals=8_400_000),
        name="attention_backward",
    )(rows, o, o_t, gain, w_qkv, w_out, pid, grad_pool, grad_gain_two, *operands, *d_pooled)


def rows_kernel(gord_ref, a0, a1, a2, a3, ao, f0, f1, f2a, f2b, f3, fo, s0, s3_ref, gf_ref, s4_ref):
    core, y = place_of_device()
    att = [a0[...], a1[:ROWS], a2[:ROWS], a3[:ROWS]] + [ao[k] for k in range(4)]
    opposite = jnp.concatenate([f2a[...], f2b[...]], axis=0)
    grad = [f0[...], f1[...], opposite, f3[...]] + [fo[k] for k in range(4)]
    own = lax.broadcasted_iota(jnp.int32, (RBLK, C), 0) + (core * 4 + y) * ROWS
    for blk in range(ROWS // RBLK):
        rows = pl.ds(blk * RBLK, RBLK)
        got = jnp.zeros((RBLK, 2 * C), F32)
        for slot in range(8):
            ids = gord_ref[slot * 8 : slot * 8 + 8] - blk * RBLK
            hot = jnp.concatenate([jnp.where(own == ids[t : t + 1], 1.0, 0.0) for t in range(8)], axis=1).astype(BF16)
            got = got + dot(hot, jnp.concatenate([att[slot], grad[slot]], axis=1))
        s3_ref[rows] = got[:, :C].astype(BF16)
        gf_ref[rows] = got[:, C:].astype(BF16)
    s4_ref[:, pl.ds(pl.multiple_of(y * 256, 256), 256)] = s0[...]
    for k, ref in ((1, a3), (2, a2), (3, a1)):
        block = jnp.concatenate([ref[ROWS : ROWS + 64], ref[ROWS + 64 :]], axis=1)
        s4_ref[:, pl.ds(pl.multiple_of(((y + k) & 3) * 256, 256), 256)] = block


def results(gord, att, grad, s4):
    return pl.pallas_call(
        rows_kernel,
        out_shape=(
            jax.ShapeDtypeStruct((ROWS, C), BF16),
            jax.ShapeDtypeStruct((ROWS, C), BF16),
            jax.ShapeDtypeStruct((64, ROWS), BF16),
        ),
        compiler_params=vmem(16),
        cost_estimate=pl.CostEstimate(flops=8_000_000_000, bytes_accessed=5_000_000, transcendentals=0),
        name="rows_to_z_order",
    )(gord, *att, *grad, s4)


def params_kernel(flat, gq_ref, go_ref, g1_ref, gw_ref, g2_ref):
    _, y = place_of_device()
    for part in range(3):
        gq_ref[:, part * C : part * C + C] = flat[part * C : part * C + C]
    go_ref[...] = flat[3 * C : 4 * C]
    gw_ref[...] = flat[pl.ds(pl.multiple_of(4 * C + y * 64, 64), 64)]
    gains = flat[6 * C : 6 * C + 8]
    g1_ref[...] = gains[0:1]
    pair = jnp.where(y >= 2, gains[2:3], gains[1:2])
    g2_ref[...] = jnp.where((y & 1) == 0, pair[:, :64], pair[:, 64:])


def parameter_results(flat):
    return pl.pallas_call(
        params_kernel,
        out_shape=(
            jax.ShapeDtypeStruct((C, 3 * C), F32),
            jax.ShapeDtypeStruct((C, C), F32),
            jax.ShapeDtypeStruct((1, C), F32),
            jax.ShapeDtypeStruct((64, C), F32),
            jax.ShapeDtypeStruct((1, 64), F32),
        ),
        compiler_params=vmem(8),
        name="parameter_results",
    )(flat)


def shift(block, axis, apart):
    count = lax.axis_size(axis)
    return lax.ppermute(block, axis, [(i, (i + apart) % count) for i in range(count)])


def sum_all(flat):
    axes = ("x", "z", "core", "grp")
    count = lax.axis_size(axes)
    shares = lax.all_to_all(flat.reshape(count, -1, flat.shape[1]), axes, 0, 0)
    share = jnp.sum(shares, axis=0)
    return lax.all_to_all(jnp.broadcast_to(share, (count, *share.shape)), axes, 0, 0).reshape(flat.shape)


def relay_y(block):
    half = block.shape[0] // 2
    left = shift(block, "grp", 1)
    right = shift(block, "grp", -1)
    return left, shift(right[:half], "grp", -1), shift(left[half:], "grp", 1), right


def shards(feats, order, parent, gain_one, w_qkv, w_out, w_pool, gain_two, cotangent):
    order = order.reshape(8, C)
    msg, *w_msgs = pack(feats, order, parent.reshape(8, C), cotangent.T, w_pool.T, gain_two[None])

    around = relay_y(msg)
    w_msgs = [w_msgs[0]] + [shift(w_msgs[k], "grp", k) for k in (1, 2, 3)]
    other = shift(jnp.concatenate((msg, *around), axis=0).reshape(4, MESSAGE, C), "core", 1)
    hilbert, pid, gord, cnt, att, mine, theirs, o, o_t, lse = attention_forward(
        order, (msg, *around, other), gain_one[None], w_qkv, w_out
    )

    theirs = shift(theirs, "core", 1)
    chunks = [shift(mine[k] + theirs[k], "grp", k) for k in (1, 2, 3)]
    s4, *rows, d_pool, grad_pool, grad_gain_two = pooled_section(mine, theirs, chunks, cnt, att, w_msgs)
    own = [d_pool] + [shift(d_pool, "grp", k) for k in (1, 2, 3)]
    d_pooled = own + [shift(block, "core", 1) for block in own]

    from_y = [shift(rows[k - 1], "grp", -k) for k in (3, 2, 1)]
    att = [att] + from_y
    att.append(shift(jnp.stack([block[:ROWS] for block in att]), "core", 1))

    operands = backward_operands(hilbert, lse, gain_one[None], w_qkv)
    df, flat = attention_backward(
        hilbert, o, o_t, gain_one[None], w_qkv, w_out, pid, grad_pool, grad_gain_two, operands, d_pooled
    )
    around = relay_y(df)
    df_other = shift(jnp.concatenate((df, *around), axis=0).reshape(4, ROWS, C), "core", 1)
    section_three, grad_feats, section_four = results(gord, att, (df, *around, df_other), s4)
    g_qkv, g_out, g_one, g_pool, g_two = parameter_results(sum_all(flat))
    return (section_four.T, section_three, grad_feats, g_one[0], g_qkv, g_out, g_pool.T, g_two[0])


def solution(mesh):
    fine = Mesh(mesh.devices.reshape(4, 4, 2, 4), ("x", "z", "core", "grp"))
    pts = ("x", "z", "core")
    everywhere = pts + ("grp",)
    placed = (
        P(everywhere, None),
        P(everywhere),
        P(everywhere),
        P(),
        P(),
        P(),
        P(None, "grp"),
        P("grp"),
        P(pts, "grp"),
    )
    return jax.shard_map(
        shards,
        mesh=fine,
        in_specs=placed,
        out_specs=(
            P(pts, "grp"),
            P(everywhere, None),
            P(everywhere, None),
            P(),
            P(),
            P(),
            P(None, "grp"),
            P("grp"),
        ),
        check_vma=False,
    )
```

```python
import math

import jax
import jax.numpy as jnp
from jax import lax
from jax.experimental import pallas as pl
from jax.experimental.pallas import tpu as pltpu
from jax.sharding import Mesh, PartitionSpec as P

F32 = jnp.float32
BF16 = jnp.bfloat16
HEADS = 8
HD = 16
C = 128
ROWS = 1024
FBLK = 128
SBLK = 256
UNROLL = 4
BBLK = 256
GBLK = 256
DBLK = 256
RBLK = 256
EPS = 1e-05
QSCALE = HD ** (-0.5) * math.log2(math.e)
LN2 = math.log(2.0)
GELU_A = math.sqrt(2.0 / math.pi)
GELU_B = 0.044715


def vmem(mib):
    return pltpu.CompilerParams(vmem_limit_bytes=mib * 1024 * 1024)


def dot(a, b):
    return jnp.dot(a, b, preferred_element_type=F32)


def dot_nt(a, b):
    return lax.dot_general(a, b, (((1,), (1,)), ((), ())), preferred_element_type=F32)


def split2(x):
    hi = x.astype(BF16)
    return hi, (x - hi.astype(F32)).astype(BF16)


def dot3(a, b):
    ah, al = split2(a)
    bh, bl = split2(b)
    return dot(ah, bh) + (dot(al, bh) + dot(ah, bl))


def dot3_nt(a, b):
    ah, al = split2(a)
    bh, bl = split2(b)
    return dot_nt(ah, bh) + (dot_nt(al, bh) + dot_nt(ah, bl))


def norm_rows(values):
    center = values - jnp.mean(values, -1, keepdims=True)
    rstd = lax.rsqrt(jnp.mean(center * center, -1, keepdims=True) + EPS)
    return center * rstd, rstd


def select_matrix(parts, part_of_slot):
    shape = (parts * C, HEADS * C)
    row = lax.broadcasted_iota(jnp.int32, shape, 0)
    col = lax.broadcasted_iota(jnp.int32, shape, 1)
    slot = (col >> 4) & 7
    wanted = jnp.full(shape, parts, jnp.int32)
    for index, part in enumerate(part_of_slot):
        wanted = jnp.where(slot == index, part, wanted)
    hit = (row & 127) == ((col >> 7) * HD + (col & 15))
    hit = hit & ((row >> 7) == wanted)
    return jnp.where(hit, 1.0, 0.0).astype(BF16)


def place(parts, part_of_slot, out_ref, const=None):
    sel = select_matrix(len(parts), part_of_slot)
    packed = jnp.concatenate(parts, axis=1)
    for pair in range(HEADS // 2):
        both = dot(packed, sel[:, pair * 256 : pair * 256 + 256])
        for half in range(2):
            block = both[:, half * C : half * C + C]
            if const is not None:
                block = jnp.where(const(lax.broadcasted_iota(jnp.int32, block.shape, 1)), 1.0, block)
            out_ref[2 * pair + half] = block.astype(BF16)


def tile_key(column, lane):
    return jnp.where((column & 127) == lane, column >> 7, -1).astype(F32).astype(BF16)


def one_hot_tiles(key, tiles):
    one, zero = jnp.ones((), BF16), jnp.zeros((), BF16)
    return jnp.concatenate([jnp.where(key == jnp.full((), t, BF16), one, zero) for t in tiles], axis=1)


def one_hot_rows(row, iota):
    row = jnp.where((row >= 0) & (row < 256), row, 512).astype(F32)
    row = jnp.broadcast_to(row, (16, row.shape[1])).astype(BF16)
    row = jnp.concatenate([row] * (iota.shape[0] // 16), axis=0)
    return jnp.where(row == iota, jnp.ones((), BF16), jnp.zeros((), BF16))


def iota_rows(columns):
    return lax.broadcasted_iota(jnp.int32, (256, columns), 0).astype(F32).astype(BF16)


def head_norms(x):
    row = lax.broadcasted_iota(jnp.int32, (C, C), 0)
    col = lax.broadcasted_iota(jnp.int32, (C, C), 1)
    same = jnp.where((row >> 4) == (col >> 4), 1.0, 0.0).astype(BF16)
    return jnp.max(dot((x * x * 1.02).astype(BF16), same), axis=0, keepdims=True)


def head_mask(shape, h):
    return (lax.broadcasted_iota(jnp.int32, shape, 1) >> 4) == h


def place_of_device():
    return lax.axis_index("core"), lax.axis_index("grp")


HALF = 528
MESSAGE = 2 * HALF


def pack_kernel(feats, order, parent, cot, w, gain, msg_ref, m0, m1, m2, m3, order_v, parent_v, cot_v, w_v, gain_v, sems):
    _, y = place_of_device()
    copies = [
        pltpu.make_async_copy(source, target, sems.at[index])
        for index, (source, target) in enumerate(
            (
                (order, order_v),
                (parent, parent_v),
                (feats, msg_ref.at[pl.ds(0, ROWS)]),
                (gain, gain_v),
                (w, w_v),
                (cot, cot_v),
            )
        )
    ]
    for copy in copies:
        copy.start()
    for copy in copies:
        copy.wait()
    near = order_v[...] & 8191
    owner = parent_v[...] & 2047
    ids = jnp.concatenate([near >> 6, near & 63, owner >> 6, owner & 63], axis=0)
    msg_ref[ROWS:] = ids.astype(F32).astype(BF16)
    w_high, w_low = split2(w_v[...])
    weights = jnp.concatenate([w_high, w_low], axis=1)
    total = gain_v[...]
    first = total.astype(BF16).astype(F32)
    second = (total - first).astype(BF16).astype(F32)
    third = total - first - second
    row = lax.broadcasted_iota(jnp.int32, (16, 64), 0)
    gains = jnp.where(row == 0, first, jnp.where(row == 1, second, jnp.where(row == 2, third, 0.0)))
    gains = jnp.concatenate([gains, jnp.zeros((16, 192), F32)], axis=1).astype(BF16)
    for k, ref in enumerate((m0, m1, m2, m3)):
        ref[:64] = cot_v[:, pl.ds(pl.multiple_of(((y + k) & 3) * 256, 256), 256)]
        ref[64:128] = weights
        ref[128:] = gains


def pack(feats, order, parent, cot_t, w_t, gain_two):
    return pl.pallas_call(
        pack_kernel,
        in_specs=[pl.BlockSpec(memory_space=pltpu.HBM)] * 6,
        out_shape=(jax.ShapeDtypeStruct((MESSAGE, C), BF16),) + (jax.ShapeDtypeStruct((144, 256), BF16),) * 4,
        scratch_shapes=[
            pltpu.VMEM((8, C), jnp.int32),
            pltpu.VMEM((8, C), jnp.int32),
            pltpu.VMEM((64, ROWS), BF16),
            pltpu.VMEM((64, C), F32),
            pltpu.VMEM((1, 64), F32),
            pltpu.SemaphoreType.DMA((6,)),
        ],
        compiler_params=vmem(60),
        name="pack",
    )(feats, order, parent, cot_t, w_t, gain_two)


def gather_rows(order_ref, blocks, tab, rep, hil_ref, pid_ref, gord_ref, cnt_ref):
    core, y = place_of_device()
    lane = lax.broadcasted_iota(jnp.int32, (C, C), 1)
    digits = []
    for slot, (rows, ids) in enumerate(blocks):
        for start, part in rows:
            tab[slot, start : start + part.shape[0], :C] = part
        ids = ids.astype(F32)
        gord_ref[slot * 8 : slot * 8 + 8] = (ids[:8] * 64.0 + ids[8:16]).astype(jnp.int32)
        digits.append(ids[16:])
    digits = jnp.concatenate(digits, axis=0)
    turned = digits.T
    for slot in range(8):
        for t in range(8):
            tab[slot, t * C : t * C + C, C:] = jnp.where((lane & ~8) == slot * 16 + t, turned, 0.0).astype(BF16)

    count = jnp.zeros((256, C), F32)
    target = (lax.broadcasted_iota(jnp.int32, (256, C), 0) + (core * 1024 + y * 256)).astype(F32)
    for slot in range(4):
        parents = digits[slot * 16 : slot * 16 + 8] * 64.0 + digits[slot * 16 + 8 : slot * 16 + 16]
        for t in range(8):
            count = count + jnp.where(target == parents[t : t + 1], 1.0, 0.0)
    cnt_ref[...] = jnp.broadcast_to(jnp.sum(count, axis=1, keepdims=True), cnt_ref.shape)

    order = order_ref[...]
    source = (order >> 10) & 7
    slot = (((source >> 2) ^ core) << 2) + ((y - source) & 3)
    index = (slot * ROWS + (order & 1023)).astype(F32)
    for t in range(8):
        column = jnp.broadcast_to(index[t : t + 1], (C, C)).T.astype(jnp.int32)
        rep[t * C : t * C + C] = tile_key(column, lane)
    weight = jnp.where(lax.broadcasted_iota(jnp.int32, (GBLK, C), 1) & 8 == 0, 64.0, 1.0)
    for blk in range(ROWS // GBLK):
        rows = pl.ds(blk * GBLK, GBLK)
        away = rep[rows]
        got = jnp.zeros((GBLK, 2 * C), F32)
        for slot in range(8):
            got = got + dot(one_hot_tiles(away, range(slot * 8, slot * 8 + 8)), tab[slot])
        hil_ref[rows] = got[:, :C].astype(BF16)
        parent = jnp.sum(got[:, C:] * weight, axis=1, keepdims=True).astype(jnp.int32)
        pid_ref[rows] = jnp.broadcast_to(parent, (GBLK, C))


def fwd_kernel(
    order_ref, m0, m1, m2a, m2b, m3, other, gain_ref, wqkv_ref, wout_ref, after1, after2, after3,
    hil_ref, pid_ref, gord_ref, cnt_ref, att_ref, mine_ref, theirs_ref, o_ref, ot_ref, lse_ref,
    tab, rep, qp, kp, vt, lt, ac,
):
    core, y = place_of_device()
    blocks = [
        ([(0, m0[:ROWS])], m0[ROWS:]),
        ([(0, m1[:ROWS])], m1[ROWS:]),
        ([(0, m2a[...]), (HALF, m2b[: ROWS - HALF])], m2b[ROWS - HALF :]),
        ([(0, m3[:ROWS])], m3[ROWS:]),
    ] + [([(0, other[k, :ROWS])], other[k, ROWS:]) for k in range(4)]
    gather_rows(order_ref, blocks, tab, rep, hil_ref, pid_ref, gord_ref, cnt_ref)

    r = hil_ref[...].astype(F32)
    xhat, _ = norm_rows(r)
    u = xhat * gain_ref[...]
    qkv = dot3(u, wqkv_ref[...])
    q = qkv[:, :C] * QSCALE
    k = qkv[:, C : 2 * C]
    place(split2(q), (0, 0, 1, 1), qp)
    place(split2(k), (0, 1, 0, 1), kp)
    for index, part in enumerate(split2(qkv[:, 2 * C :].T)):
        for h in range(HEADS):
            vt[h, index * HD : index * HD + HD] = part[h * HD : h * HD + HD]
    vt[:, 2 * HD :] = jnp.ones((HEADS, HD, ROWS), BF16)

    def head(size, shifted):
        def body(h, carry):
            keys = kp[h]
            values = vt[h]
            own = pl.ds(pl.multiple_of(h * HD, HD), HD)
            for blk in range(ROWS // size):
                cols = pl.ds(blk * size, size)
                s = dot_nt(keys, qp[h, cols])
                if shifted:
                    m = jnp.max(s, axis=0, keepdims=True)
                    s = s - m
                ph, plo = split2(jnp.exp2(s))
                oa = dot(values, ph) + dot(values, plo)
                total = oa[2 * HD : 2 * HD + 1]
                ot_ref[own, cols] = (oa[:HD] + oa[HD : 2 * HD]) / total
                lse = jnp.log2(total)
                if shifted:
                    lse = lse + m
                lt[own, cols] = jnp.broadcast_to(lse, (HD, size))
            return carry

        return body

    small = jnp.max(head_norms(q) * head_norms(k)) < 3600.0

    @pl.when(small)
    def _():
        lax.fori_loop(0, HEADS, head(FBLK, False), 0, unroll=UNROLL)

    @pl.when(jnp.logical_not(small))
    def _():
        lax.fori_loop(0, HEADS, head(SBLK, True), 0)

    o_ref[...] = ot_ref[...].T
    lse_ref[...] = lt[...].T
    att = r + dot3(o_ref[...], wout_ref[...])
    hi, lo = split2(att)
    att_ref[...] = hi
    ac[...] = jnp.concatenate([hi, lo], axis=1)
    parent = pid_ref[...].astype(F32).T[0:1].astype(jnp.int32)
    pid = (((parent >> 10) ^ core) << 10) + ((((parent >> 8) - y) & 3) << 8) + (parent & 255)
    for chunk in range(8):
        sums = dot(one_hot_rows(pid - chunk * 256, iota_rows(ROWS)), ac[...])
        target = mine_ref if chunk < 4 else theirs_ref
        target[chunk & 3] = sums[:, :C] + sums[:, C:]


def attention_forward(order, blocks, gain, w_qkv, w_out, after):
    return pl.pallas_call(
        fwd_kernel,
        in_specs=[pl.BlockSpec(memory_space=pltpu.VMEM)] * 10 + [pl.BlockSpec(memory_space=pl.ANY)] * 3,
        out_shape=(
            jax.ShapeDtypeStruct((ROWS, C), BF16),
            jax.ShapeDtypeStruct((ROWS, C), jnp.int32),
            jax.ShapeDtypeStruct((64, C), jnp.int32),
            jax.ShapeDtypeStruct((256, C), F32),
            jax.ShapeDtypeStruct((ROWS, C), BF16),
            jax.ShapeDtypeStruct((4, 256, C), F32),
            jax.ShapeDtypeStruct((4, 256, C), F32),
            jax.ShapeDtypeStruct((ROWS, C), F32),
            jax.ShapeDtypeStruct((C, ROWS), F32),
            jax.ShapeDtypeStruct((ROWS, C), F32),
        ),
        scratch_shapes=[
            pltpu.VMEM((8, ROWS, 2 * C), BF16),
            pltpu.VMEM((ROWS, C), BF16),
            pltpu.VMEM((HEADS, ROWS, C), BF16),
            pltpu.VMEM((HEADS, ROWS, C), BF16),
            pltpu.VMEM((HEADS, 3 * HD, ROWS), BF16),
            pltpu.VMEM((C, ROWS), F32),
            pltpu.VMEM((ROWS, 2 * C), BF16),
        ],
        compiler_params=vmem(30),
        cost_estimate=pl.CostEstimate(flops=30_000_000_000, bytes_accessed=4_000_000, transcendentals=8_400_000),
        name="attention_forward",
    )(order, *blocks, gain, w_qkv, w_out, *after)


def pool_kernel(mine, theirs, c1, c2, c3, cnt_ref, att_ref, w0, w1, w2, w3, after, s0, t1, t2, t3, dp_ref, gw_ref, gg_ref):
    cnt = cnt_ref[...]
    pooled = (mine[0] + theirs[0] + c1[...] + c2[...] + c3[...]) / cnt
    msgs = (w0, w1, w2, w3)
    wh = jnp.concatenate([m[64:128, :C] for m in msgs], axis=0)
    wl = jnp.concatenate([m[64:128, C:] for m in msgs], axis=0)
    cot = jnp.concatenate([m[:64] for m in msgs], axis=0).astype(F32).T
    gains = jnp.concatenate([m[128:, :64] for m in msgs], axis=1).astype(F32)
    gain = gains[0:1] + gains[1:2] + gains[2:3]
    ph, plo = split2(pooled)
    normed, rstd = norm_rows(dot_nt(ph, wh) + (dot_nt(plo, wh) + dot_nt(ph, wl)))
    v = normed * gain
    t = jnp.tanh(GELU_A * (v + GELU_B * (v * v * v)))
    s4 = (0.5 * v * (1.0 + t)).T.astype(BF16)
    s0[...] = s4[:64]
    for k, ref in enumerate((t1, t2, t3)):
        block = s4[64 * k + 64 : 64 * k + 128]
        ref[:ROWS] = att_ref[...]
        ref[ROWS : ROWS + 64] = block[:, :C]
        ref[ROWS + 64 :] = block[:, C:]
    slope = 0.5 * (1.0 + t) + 0.5 * v * (1.0 - t * t) * (GELU_A * (1.0 + (3.0 * GELU_B) * (v * v)))
    d_scaled = cot * slope
    d_normed = d_scaled * gain
    d_proj = rstd * (
        d_normed
        - jnp.mean(d_normed, -1, keepdims=True)
        - normed * jnp.mean(d_normed * normed, -1, keepdims=True)
    )
    dh, dl = split2(d_proj)
    dp_ref[...] = (dot(dh, wh) + (dot(dl, wh) + dot(dh, wl))) / cnt
    _, y = place_of_device()
    gw = dot3(d_proj.T, pooled)
    gg = jnp.sum(d_scaled * normed, axis=0, keepdims=True)
    gains = jnp.zeros((8, C), F32)
    row = lax.broadcasted_iota(jnp.int32, (8, C), 0)
    low = lax.broadcasted_iota(jnp.int32, (8, C), 1) < 64
    for k in range(4):
        owner = (y - k) & 3
        gw_ref[pl.ds(pl.multiple_of(owner * 64, 64), 64)] = gw[64 * k : 64 * k + 64]
        block = gg[:, 64 * k : 64 * k + 64]
        twice = jnp.concatenate([block, block], axis=1)
        hit = (row == 1 + (owner >> 1)) & (low == ((owner & 1) == 0))
        gains = jnp.where(hit, twice, gains)
    gg_ref[...] = gains


def pooled_section(mine, theirs, chunks, cnt, att, msgs, after):
    return pl.pallas_call(
        pool_kernel,
        in_specs=[pl.BlockSpec(memory_space=pltpu.VMEM)] * 11 + [pl.BlockSpec(memory_space=pl.ANY)],
        out_shape=(jax.ShapeDtypeStruct((64, 256), BF16),)
        + (jax.ShapeDtypeStruct((ROWS + 128, C), BF16),) * 3
        + (
            jax.ShapeDtypeStruct((256, C), F32),
            jax.ShapeDtypeStruct((256, C), F32),
            jax.ShapeDtypeStruct((8, C), F32),
        ),
        compiler_params=vmem(12),
        name="pooled_section",
    )(mine, theirs, *chunks, cnt, att, *msgs, after)


def stack_heads(source, target):
    hi, lo = split2(source.T)
    for h in range(HEADS):
        target[h, :HD] = hi[h * HD : h * HD + HD]
        target[h, HD:] = lo[h * HD : h * HD + HD]


def prep_kernel(r_ref, lse_ref, gain_ref, wqkv_ref, qp, kp, vp, kh, kl, q_t):
    xhat, _ = norm_rows(r_ref[...].astype(F32))
    u = xhat * gain_ref[...]
    qkv = dot3(u, wqkv_ref[...])
    q = qkv[:, :C] * QSCALE
    qh, ql = split2(q)
    lse = -lse_ref[...]
    l1 = lse.astype(BF16).astype(F32)
    l2 = (lse - l1).astype(BF16).astype(F32)
    l3 = lse - l1 - l2
    which = lax.broadcasted_iota(jnp.int32, (ROWS, C), 1) & 15
    lp = jnp.where(which == 0, l1, jnp.where(which == 1, l2, jnp.where(which == 2, l3, 0.0))).astype(BF16)
    place((qh, ql, lp), (0, 0, 1, 1, 2), qp)
    khi, klo = split2(qkv[:, C : 2 * C])
    place((khi, klo), (0, 1, 0, 1), kp, const=lambda lane: (lane >= 64) & (lane < 67))
    kh[...] = khi
    kl[...] = klo
    place(split2(qkv[:, 2 * C :]), (0, 1, 0, 1), vp, const=lambda lane: (lane >= 64) & (lane < 96))
    stack_heads(q, q_t)


def backward_operands(rows, lse, gain, w_qkv):
    return pl.pallas_call(
        prep_kernel,
        out_shape=(jax.ShapeDtypeStruct((HEADS, ROWS, C), BF16),) * 3
        + (jax.ShapeDtypeStruct((ROWS, C), BF16),) * 2
        + (jax.ShapeDtypeStruct((HEADS, 2 * HD, ROWS), BF16),),
        compiler_params=vmem(24),
        cost_estimate=pl.CostEstimate(flops=6_000_000_000, bytes_accessed=8_000_000, transcendentals=0),
        name="backward_operands",
    )(rows, lse, gain, w_qkv)


def bwd_kernel(
    r_ref, o_ref, ot_ref, gain_ref, wqkv_ref, wout_ref, pid_ref, gw_ref, gg2_ref,
    qp, kp, vp, kh, kl, q_t, d0, d1, d2, d3, e0, e1, e2, e3,
    df_ref, flat,
    dop, tab, da_ref, dot_t, dv_t, dk_t, dq_ref,
):
    core, y = place_of_device()
    for chunk, ref in enumerate((d0, d1, d2, d3, e0, e1, e2, e3)):
        hi, lo = split2(ref[...])
        tab[chunk * 256 : chunk * 256 + 256, :C] = hi
        tab[chunk * 256 : chunk * 256 + 256, C:] = lo
    lane = lax.broadcasted_iota(jnp.int32, (DBLK, C), 1)
    for blk in range(ROWS // DBLK):
        rows = pl.ds(blk * DBLK, DBLK)
        pid = pid_ref[rows]
        index = (((pid >> 10) ^ core) << 10) + (((y - (pid >> 8)) & 3) << 8) + (pid & 255)
        got = dot(one_hot_tiles(tile_key(index, lane), range(16)), tab[...])
        da_ref[rows] = got[:, :C] + got[:, C:]

    da = da_ref[...]
    do = dot3_nt(da, wout_ref[...])
    place((*split2(do), *split2(-do * o_ref[...])), (0, 0, 1, 1, 2, 3), dop)
    stack_heads(do, dot_t)

    def head(h, carry):
        kmask = head_mask((ROWS, C), h)
        zero = jnp.zeros((), BF16)
        ka = jnp.concatenate([jnp.where(kmask, kh[...], zero), jnp.where(kmask, kl[...], zero)], axis=1)
        keys, vals = kp[h], vp[h]
        mask = head_mask((BBLK, C), h)
        dv = jnp.zeros((2 * HD, ROWS), F32)
        dk = jnp.zeros((2 * HD, ROWS), F32)
        for blk in range(ROWS // BBLK):
            rows = pl.ds(blk * BBLK, BBLK)
            p = jnp.exp2(dot_nt(qp[h, rows], keys))
            ds = p * dot_nt(dop[h, rows], vals)
            ph, plo = split2(p)
            sh, sl = split2(ds)
            left = dot_t[h, :, rows]
            dv = dv + (dot(left, ph) + dot(left, plo))
            left = q_t[h, :, rows]
            dk = dk + (dot(left, sh) + dot(left, sl))
            dq = dot(sh, ka) + dot(sl, ka)
            dq_ref[rows] = jnp.where(mask, dq[:, :C] + dq[:, C:], dq_ref[rows])
        place_rows = pl.ds(pl.multiple_of(h * HD, HD), HD)
        dv_t[place_rows] = dv[:HD] + dv[HD:]
        dk_t[place_rows] = dk[:HD] + dk[HD:]
        return carry

    lax.fori_loop(0, HEADS, head, 0, unroll=UNROLL)
    xhat, rstd = norm_rows(r_ref[...].astype(F32))
    u = xhat * gain_ref[...]
    grads = jnp.concatenate([dq_ref[...] * HD ** (-0.5), dk_t[...].T * LN2, dv_t[...].T], axis=1)
    du = dot3_nt(grads, wqkv_ref[...])
    gq = dot3(u.T, grads)
    for part in range(3):
        flat[part * C : part * C + C] = gq[:, part * C : part * C + C]
    flat[3 * C : 4 * C] = dot3(ot_ref[...], da)
    flat[4 * C : 6 * C] = gw_ref[...]
    row = lax.broadcasted_iota(jnp.int32, (8, C), 0)
    gains = jnp.where(row == 0, jnp.sum(du * xhat, axis=0, keepdims=True), gg2_ref[...])
    flat[6 * C : 6 * C + 8] = gains
    flat[6 * C + 8 :] = jnp.zeros((2 * C - 8, C), F32)
    dn = du * gain_ref[...]
    dx = rstd * (dn - jnp.mean(dn, -1, keepdims=True) - xhat * jnp.mean(dn * xhat, -1, keepdims=True))
    df_ref[...] = (da + dx).astype(BF16)


def attention_backward(rows, o, o_t, gain, w_qkv, w_out, pid, grad_pool, grad_gain_two, operands, d_pooled):
    return pl.pallas_call(
        bwd_kernel,
        out_shape=(jax.ShapeDtypeStruct((ROWS, C), BF16), jax.ShapeDtypeStruct((8 * C, C), F32)),
        scratch_shapes=[
            pltpu.VMEM((HEADS, ROWS, C), BF16),
            pltpu.VMEM((2048, 2 * C), BF16),
            pltpu.VMEM((ROWS, C), F32),
            pltpu.VMEM((HEADS, 2 * HD, ROWS), BF16),
            pltpu.VMEM((C, ROWS), F32),
            pltpu.VMEM((C, ROWS), F32),
            pltpu.VMEM((ROWS, C), F32),
        ],
        compiler_params=vmem(34),
        cost_estimate=pl.CostEstimate(flops=90_000_000_000, bytes_accessed=8_000_000, transcendentals=8_400_000),
        name="attention_backward",
    )(rows, o, o_t, gain, w_qkv, w_out, pid, grad_pool, grad_gain_two, *operands, *d_pooled)


def rows_kernel(gord_ref, a0, a1, a2, a3, f0, f1, f2, f3, other, s0, s3_ref, gf_ref, s4_ref):
    core, y = place_of_device()
    att = [ref[:ROWS] for ref in (a0, a1, a2, a3)] + [other[k] for k in range(4)]
    grad = [ref[...] for ref in (f0, f1, f2, f3)] + [other[k + 4] for k in range(4)]
    own = lax.broadcasted_iota(jnp.int32, (RBLK, C), 0) + (core * 4 + y) * ROWS
    for blk in range(ROWS // RBLK):
        rows = pl.ds(blk * RBLK, RBLK)
        got = jnp.zeros((RBLK, 2 * C), F32)
        for slot in range(8):
            ids = gord_ref[slot * 8 : slot * 8 + 8] - blk * RBLK
            hot = jnp.concatenate([jnp.where(own == ids[t : t + 1], 1.0, 0.0) for t in range(8)], axis=1).astype(BF16)
            got = got + dot(hot, jnp.concatenate([att[slot], grad[slot]], axis=1))
        s3_ref[rows] = got[:, :C].astype(BF16)
        gf_ref[rows] = got[:, C:].astype(BF16)
    s4_ref[:, pl.ds(pl.multiple_of(y * 256, 256), 256)] = s0[...]
    for k, ref in ((1, a3), (2, a2), (3, a1)):
        block = jnp.concatenate([ref[ROWS : ROWS + 64], ref[ROWS + 64 :]], axis=1)
        s4_ref[:, pl.ds(pl.multiple_of(((y + k) & 3) * 256, 256), 256)] = block


def results(gord, att, grad, other, s4):
    return pl.pallas_call(
        rows_kernel,
        out_shape=(
            jax.ShapeDtypeStruct((ROWS, C), BF16),
            jax.ShapeDtypeStruct((ROWS, C), BF16),
            jax.ShapeDtypeStruct((64, ROWS), BF16),
        ),
        compiler_params=vmem(16),
        cost_estimate=pl.CostEstimate(flops=8_000_000_000, bytes_accessed=5_000_000, transcendentals=0),
        name="rows_to_z_order",
    )(gord, *att, *grad, other, s4)


def params_kernel(flat, gq_ref, go_ref, g1_ref, gw_ref, g2_ref):
    _, y = place_of_device()
    for part in range(3):
        gq_ref[:, part * C : part * C + C] = flat[part * C : part * C + C]
    go_ref[...] = flat[3 * C : 4 * C]
    gw_ref[...] = flat[pl.ds(pl.multiple_of(4 * C + y * 64, 64), 64)]
    gains = flat[6 * C : 6 * C + 8]
    g1_ref[...] = gains[0:1]
    pair = jnp.where(y >= 2, gains[2:3], gains[1:2])
    g2_ref[...] = jnp.where((y & 1) == 0, pair[:, :64], pair[:, 64:])


def parameter_results(flat):
    return pl.pallas_call(
        params_kernel,
        out_shape=(
            jax.ShapeDtypeStruct((C, 3 * C), F32),
            jax.ShapeDtypeStruct((C, C), F32),
            jax.ShapeDtypeStruct((1, C), F32),
            jax.ShapeDtypeStruct((64, C), F32),
            jax.ShapeDtypeStruct((1, 64), F32),
        ),
        compiler_params=vmem(8),
        name="parameter_results",
    )(flat)


def share_kernel(shares, a0, a1, a2, a3, f0, f1, f2, f3, out_ref, rows_ref):
    total = shares[0]
    for source in range(1, shares.shape[0]):
        total = total + shares[source]
    out_ref[...] = jnp.broadcast_to(total, out_ref.shape)
    for k, ref in enumerate((a0, a1, a2, a3, f0, f1, f2, f3)):
        rows_ref[k] = ref[:ROWS]


def share_of_all(shares, att, df):
    return pl.pallas_call(
        share_kernel,
        out_shape=(jax.ShapeDtypeStruct(shares.shape, F32), jax.ShapeDtypeStruct((8, ROWS, C), BF16)),
        compiler_params=vmem(16),
        name="share_of_all",
    )(shares, *att, *df)


def shift(block, axis, apart):
    count = lax.axis_size(axis)
    return lax.ppermute(block, axis, [(i, (i + apart) % count) for i in range(count)])


EVERYWHERE = ("x", "z", "core", "grp")


def deal_rows(flat):
    return lax.all_to_all(flat.reshape(lax.axis_size(EVERYWHERE), -1, flat.shape[1]), EVERYWHERE, 0, 0)


def gather_rows_of_all(shares):
    count = lax.axis_size(EVERYWHERE)
    every = lax.all_to_all(shares, EVERYWHERE, 0, 0)
    return every.reshape(-1, shares.shape[2])


def relay_y(block):
    half = block.shape[0] // 2
    left = shift(block, "grp", 1)
    right = shift(block, "grp", -1)
    return left, shift(right[:half], "grp", -1), shift(left[half:], "grp", 1), right


def shards(feats, order, parent, gain_one, w_qkv, w_out, w_pool, gain_two, cotangent):
    order = order.reshape(8, C)
    msg, *w_msgs = pack(feats, order, parent.reshape(8, C), cotangent.T, w_pool.T, gain_two[None])

    around = relay_y(msg)
    w_msgs = [w_msgs[0]] + [shift(w_msgs[k], "grp", k) for k in (1, 2, 3)]
    other = shift(jnp.concatenate((msg, *around), axis=0).reshape(4, MESSAGE, C), "core", 1)
    hilbert, pid, gord, cnt, att, mine, theirs, o, o_t, lse = attention_forward(
        order, (msg, *around, other), gain_one[None], w_qkv, w_out, w_msgs[1:]
    )

    operands = backward_operands(hilbert, lse, gain_one[None], w_qkv)

    theirs = shift(theirs, "core", 1)
    chunks = [shift(mine[k] + theirs[k], "grp", k) for k in (1, 2, 3)]
    s4, *rows, d_pool, grad_pool, grad_gain_two = pooled_section(mine, theirs, chunks, cnt, att, w_msgs, operands[-1])
    own = [d_pool] + [shift(d_pool, "grp", k) for k in (1, 2, 3)]
    d_pooled = own + [shift(block, "core", 1) for block in own]

    from_y = [shift(rows[k - 1], "grp", -k) for k in (3, 2, 1)]
    att = [att] + from_y

    df, flat = attention_backward(
        hilbert, o, o_t, gain_one[None], w_qkv, w_out, pid, grad_pool, grad_gain_two, operands, d_pooled
    )
    df = [df] + [shift(df, "grp", k) for k in (1, 2, 3)]
    shares, rows = share_of_all(deal_rows(flat), att, df)
    other = shift(rows, "core", 1)
    total = gather_rows_of_all(shares)
    section_three, grad_feats, section_four = results(gord, att, df, other, s4)
    g_qkv, g_out, g_one, g_pool, g_two = parameter_results(total)
    return (section_four.T, section_three, grad_feats, g_one[0], g_qkv, g_out, g_pool.T, g_two[0])


def solution(mesh):
    fine = Mesh(mesh.devices.reshape(4, 4, 2, 4), ("x", "z", "core", "grp"))
    pts = ("x", "z", "core")
    everywhere = pts + ("grp",)
    placed = (
        P(everywhere, None),
        P(everywhere),
        P(everywhere),
        P(),
        P(),
        P(),
        P(None, "grp"),
        P("grp"),
        P(pts, "grp"),
    )
    return jax.shard_map(
        shards,
        mesh=fine,
        in_specs=placed,
        out_specs=(
            P(pts, "grp"),
            P(everywhere, None),
            P(everywhere, None),
            P(),
            P(),
            P(),
            P(None, "grp"),
            P("grp"),
        ),
        check_vma=False,
    )
```

```python
import math

import jax
import jax.numpy as jnp
from jax import lax
from jax.experimental import pallas as pl
from jax.experimental.pallas import tpu as pltpu
from jax.sharding import Mesh, PartitionSpec as P

F32 = jnp.float32
BF16 = jnp.bfloat16
HEADS = 8
HD = 16
C = 128
ROWS = 1024
FBLK = 128
SBLK = 256
UNROLL = 4
BBLK = 256
GBLK = 256
DBLK = 256
RBLK = 256
EPS = 1e-05
QSCALE = HD ** (-0.5) * math.log2(math.e)
LN2 = math.log(2.0)
GELU_A = math.sqrt(2.0 / math.pi)
GELU_B = 0.044715


def vmem(mib):
    return pltpu.CompilerParams(vmem_limit_bytes=mib * 1024 * 1024)


def dot(a, b):
    return jnp.dot(a, b, preferred_element_type=F32)


def dot_nt(a, b):
    return lax.dot_general(a, b, (((1,), (1,)), ((), ())), preferred_element_type=F32)


def split2(x):
    hi = x.astype(BF16)
    return hi, (x - hi.astype(F32)).astype(BF16)


def dot3(a, b):
    ah, al = split2(a)
    bh, bl = split2(b)
    return dot(ah, bh) + (dot(al, bh) + dot(ah, bl))


def dot3_nt(a, b):
    ah, al = split2(a)
    bh, bl = split2(b)
    return dot_nt(ah, bh) + (dot_nt(al, bh) + dot_nt(ah, bl))


def norm_rows(values):
    center = values - jnp.mean(values, -1, keepdims=True)
    rstd = lax.rsqrt(jnp.mean(center * center, -1, keepdims=True) + EPS)
    return center * rstd, rstd


def select_matrix(parts, part_of_slot):
    shape = (parts * C, HEADS * C)
    row = lax.broadcasted_iota(jnp.int32, shape, 0)
    col = lax.broadcasted_iota(jnp.int32, shape, 1)
    slot = (col >> 4) & 7
    wanted = jnp.full(shape, parts, jnp.int32)
    for index, part in enumerate(part_of_slot):
        wanted = jnp.where(slot == index, part, wanted)
    hit = (row & 127) == ((col >> 7) * HD + (col & 15))
    hit = hit & ((row >> 7) == wanted)
    return jnp.where(hit, 1.0, 0.0).astype(BF16)


def place(parts, part_of_slot, out_ref, const=None):
    sel = select_matrix(len(parts), part_of_slot)
    packed = jnp.concatenate(parts, axis=1)
    for pair in range(HEADS // 2):
        both = dot(packed, sel[:, pair * 256 : pair * 256 + 256])
        for half in range(2):
            block = both[:, half * C : half * C + C]
            if const is not None:
                block = jnp.where(const(lax.broadcasted_iota(jnp.int32, block.shape, 1)), 1.0, block)
            out_ref[2 * pair + half] = block.astype(BF16)


def tile_key(column, lane):
    return jnp.where((column & 127) == lane, column >> 7, -1).astype(F32).astype(BF16)


def one_hot_tiles(key, tiles):
    one, zero = jnp.ones((), BF16), jnp.zeros((), BF16)
    return jnp.concatenate([jnp.where(key == jnp.full((), t, BF16), one, zero) for t in tiles], axis=1)


def one_hot_rows(row, iota):
    row = jnp.where((row >= 0) & (row < 256), row, 512).astype(F32)
    row = jnp.broadcast_to(row, (16, row.shape[1])).astype(BF16)
    row = jnp.concatenate([row] * (iota.shape[0] // 16), axis=0)
    return jnp.where(row == iota, jnp.ones((), BF16), jnp.zeros((), BF16))


def iota_rows(columns):
    return lax.broadcasted_iota(jnp.int32, (256, columns), 0).astype(F32).astype(BF16)


def head_norms(x):
    row = lax.broadcasted_iota(jnp.int32, (C, C), 0)
    col = lax.broadcasted_iota(jnp.int32, (C, C), 1)
    same = jnp.where((row >> 4) == (col >> 4), 1.0, 0.0).astype(BF16)
    return jnp.max(dot((x * x * 1.02).astype(BF16), same), axis=0, keepdims=True)


def head_mask(shape, h):
    return (lax.broadcasted_iota(jnp.int32, shape, 1) >> 4) == h


def place_of_device():
    return lax.axis_index("core"), lax.axis_index("grp")


HALF = 528
MESSAGE = 2 * HALF


def pack_kernel(feats, order, parent, cot, w, gain, msg_ref, m0, m1, m2, m3, order_v, parent_v, cot_v, w_v, gain_v, sems):
    _, y = place_of_device()
    copies = [
        pltpu.make_async_copy(source, target, sems.at[index])
        for index, (source, target) in enumerate(
            (
                (order, order_v),
                (parent, parent_v),
                (feats, msg_ref.at[pl.ds(0, ROWS)]),
                (gain, gain_v),
                (w, w_v),
                (cot, cot_v),
            )
        )
    ]
    for copy in copies:
        copy.start()
    for copy in copies:
        copy.wait()
    near = order_v[...] & 8191
    owner = parent_v[...] & 2047
    ids = jnp.concatenate([near >> 6, near & 63, owner >> 6, owner & 63], axis=0)
    msg_ref[ROWS:] = ids.astype(F32).astype(BF16)
    w_high, w_low = split2(w_v[...])
    weights = jnp.concatenate([w_high, w_low], axis=1)
    total = gain_v[...]
    first = total.astype(BF16).astype(F32)
    second = (total - first).astype(BF16).astype(F32)
    third = total - first - second
    row = lax.broadcasted_iota(jnp.int32, (16, 64), 0)
    gains = jnp.where(row == 0, first, jnp.where(row == 1, second, jnp.where(row == 2, third, 0.0)))
    gains = jnp.concatenate([gains, jnp.zeros((16, 192), F32)], axis=1).astype(BF16)
    for k, ref in enumerate((m0, m1, m2, m3)):
        ref[:64] = cot_v[:, pl.ds(pl.multiple_of(((y + k) & 3) * 256, 256), 256)]
        ref[64:128] = weights
        ref[128:] = gains


def pack(feats, order, parent, cot_t, w_t, gain_two):
    return pl.pallas_call(
        pack_kernel,
        in_specs=[pl.BlockSpec(memory_space=pltpu.HBM)] * 6,
        out_shape=(jax.ShapeDtypeStruct((MESSAGE, C), BF16),) + (jax.ShapeDtypeStruct((144, 256), BF16),) * 4,
        scratch_shapes=[
            pltpu.VMEM((8, C), jnp.int32),
            pltpu.VMEM((8, C), jnp.int32),
            pltpu.VMEM((64, ROWS), BF16),
            pltpu.VMEM((64, C), F32),
            pltpu.VMEM((1, 64), F32),
            pltpu.SemaphoreType.DMA((6,)),
        ],
        compiler_params=vmem(60),
        name="pack",
    )(feats, order, parent, cot_t, w_t, gain_two)


def gather_rows(order_ref, blocks, tab, rep, hil_ref, pid_ref, gord_ref, cnt_ref):
    core, y = place_of_device()
    lane = lax.broadcasted_iota(jnp.int32, (C, C), 1)
    digits = []
    for slot, (rows, ids) in enumerate(blocks):
        for start, part in rows:
            tab[slot, start : start + part.shape[0], :C] = part
        ids = ids.astype(F32)
        gord_ref[slot * 8 : slot * 8 + 8] = (ids[:8] * 64.0 + ids[8:16]).astype(jnp.int32)
        digits.append(ids[16:])
    digits = jnp.concatenate(digits, axis=0)
    turned = digits.T
    for slot in range(8):
        for t in range(8):
            tab[slot, t * C : t * C + C, C:] = jnp.where((lane & ~8) == slot * 16 + t, turned, 0.0).astype(BF16)

    count = jnp.zeros((256, C), F32)
    target = (lax.broadcasted_iota(jnp.int32, (256, C), 0) + (core * 1024 + y * 256)).astype(F32)
    for slot in range(4):
        parents = digits[slot * 16 : slot * 16 + 8] * 64.0 + digits[slot * 16 + 8 : slot * 16 + 16]
        for t in range(8):
            count = count + jnp.where(target == parents[t : t + 1], 1.0, 0.0)
    cnt_ref[...] = jnp.broadcast_to(jnp.sum(count, axis=1, keepdims=True), cnt_ref.shape)

    order = order_ref[...]
    source = (order >> 10) & 7
    slot = (((source >> 2) ^ core) << 2) + ((y - source) & 3)
    index = (slot * ROWS + (order & 1023)).astype(F32)
    for t in range(8):
        column = jnp.broadcast_to(index[t : t + 1], (C, C)).T.astype(jnp.int32)
        rep[t * C : t * C + C] = tile_key(column, lane)
    weight = jnp.where(lax.broadcasted_iota(jnp.int32, (GBLK, C), 1) & 8 == 0, 64.0, 1.0)
    for blk in range(ROWS // GBLK):
        rows = pl.ds(blk * GBLK, GBLK)
        away = rep[rows]
        got = jnp.zeros((GBLK, 2 * C), F32)
        for slot in range(8):
            got = got + dot(one_hot_tiles(away, range(slot * 8, slot * 8 + 8)), tab[slot])
        hil_ref[rows] = got[:, :C].astype(BF16)
        parent = jnp.sum(got[:, C:] * weight, axis=1, keepdims=True).astype(jnp.int32)
        pid_ref[rows] = jnp.broadcast_to(parent, (GBLK, C))


def fwd_kernel(
    order_ref, m0, m1, m2a, m2b, m3, other, gain_ref, wqkv_ref, wout_ref,
    hil_ref, pid_ref, gord_ref, cnt_ref, att_ref, mine_ref, theirs_ref, o_ref, ot_ref, lse_ref,
    tab, rep, qp, kp, vt, lt, ac,
):
    core, y = place_of_device()
    blocks = [
        ([(0, m0[:ROWS])], m0[ROWS:]),
        ([(0, m1[:ROWS])], m1[ROWS:]),
        ([(0, m2a[...]), (HALF, m2b[: ROWS - HALF])], m2b[ROWS - HALF :]),
        ([(0, m3[:ROWS])], m3[ROWS:]),
    ] + [([(0, other[k, :ROWS])], other[k, ROWS:]) for k in range(4)]
    gather_rows(order_ref, blocks, tab, rep, hil_ref, pid_ref, gord_ref, cnt_ref)

    r = hil_ref[...].astype(F32)
    xhat, _ = norm_rows(r)
    u = xhat * gain_ref[...]
    qkv = dot3(u, wqkv_ref[...])
    q = qkv[:, :C] * QSCALE
    k = qkv[:, C : 2 * C]
    place(split2(q), (0, 0, 1, 1), qp)
    place(split2(k), (0, 1, 0, 1), kp)
    for index, part in enumerate(split2(qkv[:, 2 * C :].T)):
        for h in range(HEADS):
            vt[h, index * HD : index * HD + HD] = part[h * HD : h * HD + HD]
    vt[:, 2 * HD :] = jnp.ones((HEADS, HD, ROWS), BF16)

    def head(size, shifted):
        def body(h, carry):
            keys = kp[h]
            values = vt[h]
            own = pl.ds(pl.multiple_of(h * HD, HD), HD)
            for blk in range(ROWS // size):
                cols = pl.ds(blk * size, size)
                s = dot_nt(keys, qp[h, cols])
                if shifted:
                    m = jnp.max(s, axis=0, keepdims=True)
                    s = s - m
                ph, plo = split2(jnp.exp2(s))
                oa = dot(values, ph) + dot(values, plo)
                total = oa[2 * HD : 2 * HD + 1]
                ot_ref[own, cols] = (oa[:HD] + oa[HD : 2 * HD]) / total
                lse = jnp.log2(total)
                if shifted:
                    lse = lse + m
                lt[own, cols] = jnp.broadcast_to(lse, (HD, size))
            return carry

        return body

    small = jnp.max(head_norms(q) * head_norms(k)) < 3600.0

    @pl.when(small)
    def _():
        lax.fori_loop(0, HEADS, head(FBLK, False), 0, unroll=UNROLL)

    @pl.when(jnp.logical_not(small))
    def _():
        lax.fori_loop(0, HEADS, head(SBLK, True), 0)

    o_ref[...] = ot_ref[...].T
    lse_ref[...] = lt[...].T
    att = r + dot3(o_ref[...], wout_ref[...])
    hi, lo = split2(att)
    att_ref[...] = hi
    ac[...] = jnp.concatenate([hi, lo], axis=1)
    parent = pid_ref[...].astype(F32).T[0:1].astype(jnp.int32)
    pid = (((parent >> 10) ^ core) << 10) + ((((parent >> 8) - y) & 3) << 8) + (parent & 255)
    for chunk in range(8):
        sums = dot(one_hot_rows(pid - chunk * 256, iota_rows(ROWS)), ac[...])
        target = mine_ref if chunk < 4 else theirs_ref
        target[chunk & 3] = sums[:, :C] + sums[:, C:]


def attention_forward(order, blocks, gain, w_qkv, w_out):
    return pl.pallas_call(
        fwd_kernel,
        out_shape=(
            jax.ShapeDtypeStruct((ROWS, C), BF16),
            jax.ShapeDtypeStruct((ROWS, C), jnp.int32),
            jax.ShapeDtypeStruct((64, C), jnp.int32),
            jax.ShapeDtypeStruct((256, C), F32),
            jax.ShapeDtypeStruct((ROWS, C), BF16),
            jax.ShapeDtypeStruct((4, 256, C), F32),
            jax.ShapeDtypeStruct((4, 256, C), F32),
            jax.ShapeDtypeStruct((ROWS, C), F32),
            jax.ShapeDtypeStruct((C, ROWS), F32),
            jax.ShapeDtypeStruct((ROWS, C), F32),
        ),
        scratch_shapes=[
            pltpu.VMEM((8, ROWS, 2 * C), BF16),
            pltpu.VMEM((ROWS, C), BF16),
            pltpu.VMEM((HEADS, ROWS, C), BF16),
            pltpu.VMEM((HEADS, ROWS, C), BF16),
            pltpu.VMEM((HEADS, 3 * HD, ROWS), BF16),
            pltpu.VMEM((C, ROWS), F32),
            pltpu.VMEM((ROWS, 2 * C), BF16),
        ],
        compiler_params=vmem(30),
        cost_estimate=pl.CostEstimate(flops=30_000_000_000, bytes_accessed=4_000_000, transcendentals=8_400_000),
        name="attention_forward",
    )(order, *blocks, gain, w_qkv, w_out)


def pool_kernel(mine, theirs, c1, c2, c3, cnt_ref, att_ref, w0, w1, w2, w3, after, s0, t1, t2, t3, dp_ref, gw_ref, gg_ref):
    cnt = cnt_ref[...]
    pooled = (mine[0] + theirs[0] + c1[...] + c2[...] + c3[...]) / cnt
    msgs = (w0, w1, w2, w3)
    wh = jnp.concatenate([m[64:128, :C] for m in msgs], axis=0)
    wl = jnp.concatenate([m[64:128, C:] for m in msgs], axis=0)
    cot = jnp.concatenate([m[:64] for m in msgs], axis=0).astype(F32).T
    gains = jnp.concatenate([m[128:, :64] for m in msgs], axis=1).astype(F32)
    gain = gains[0:1] + gains[1:2] + gains[2:3]
    ph, plo = split2(pooled)
    normed, rstd = norm_rows(dot_nt(ph, wh) + (dot_nt(plo, wh) + dot_nt(ph, wl)))
    v = normed * gain
    t = jnp.tanh(GELU_A * (v + GELU_B * (v * v * v)))
    s4 = (0.5 * v * (1.0 + t)).T.astype(BF16)
    s0[...] = s4[:64]
    for k, ref in enumerate((t1, t2, t3)):
        block = s4[64 * k + 64 : 64 * k + 128]
        ref[:ROWS] = att_ref[...]
        ref[ROWS : ROWS + 64] = block[:, :C]
        ref[ROWS + 64 :] = block[:, C:]
    slope = 0.5 * (1.0 + t) + 0.5 * v * (1.0 - t * t) * (GELU_A * (1.0 + (3.0 * GELU_B) * (v * v)))
    d_scaled = cot * slope
    d_normed = d_scaled * gain
    d_proj = rstd * (
        d_normed
        - jnp.mean(d_normed, -1, keepdims=True)
        - normed * jnp.mean(d_normed * normed, -1, keepdims=True)
    )
    dh, dl = split2(d_proj)
    dp_ref[...] = (dot(dh, wh) + (dot(dl, wh) + dot(dh, wl))) / cnt
    _, y = place_of_device()
    gw = dot3(d_proj.T, pooled)
    gg = jnp.sum(d_scaled * normed, axis=0, keepdims=True)
    gains = jnp.zeros((8, C), F32)
    row = lax.broadcasted_iota(jnp.int32, (8, C), 0)
    low = lax.broadcasted_iota(jnp.int32, (8, C), 1) < 64
    for k in range(4):
        owner = (y - k) & 3
        gw_ref[pl.ds(pl.multiple_of(owner * 64, 64), 64)] = gw[64 * k : 64 * k + 64]
        block = gg[:, 64 * k : 64 * k + 64]
        twice = jnp.concatenate([block, block], axis=1)
        hit = (row == 1 + (owner >> 1)) & (low == ((owner & 1) == 0))
        gains = jnp.where(hit, twice, gains)
    gg_ref[...] = gains


def pooled_section(mine, theirs, chunks, cnt, att, msgs, after):
    return pl.pallas_call(
        pool_kernel,
        in_specs=[pl.BlockSpec(memory_space=pltpu.VMEM)] * 11 + [pl.BlockSpec(memory_space=pl.ANY)],
        out_shape=(jax.ShapeDtypeStruct((64, 256), BF16),)
        + (jax.ShapeDtypeStruct((ROWS + 128, C), BF16),) * 3
        + (
            jax.ShapeDtypeStruct((256, C), F32),
            jax.ShapeDtypeStruct((256, C), F32),
            jax.ShapeDtypeStruct((8, C), F32),
        ),
        compiler_params=vmem(12),
        name="pooled_section",
    )(mine, theirs, *chunks, cnt, att, *msgs, after)


def stack_heads(source, target):
    hi, lo = split2(source.T)
    for h in range(HEADS):
        target[h, :HD] = hi[h * HD : h * HD + HD]
        target[h, HD:] = lo[h * HD : h * HD + HD]


def prep_kernel(r_ref, lse_ref, gain_ref, wqkv_ref, qp, kp, vp, kh, kl, q_t):
    xhat, _ = norm_rows(r_ref[...].astype(F32))
    u = xhat * gain_ref[...]
    qkv = dot3(u, wqkv_ref[...])
    q = qkv[:, :C] * QSCALE
    qh, ql = split2(q)
    lse = -lse_ref[...]
    l1 = lse.astype(BF16).astype(F32)
    l2 = (lse - l1).astype(BF16).astype(F32)
    l3 = lse - l1 - l2
    which = lax.broadcasted_iota(jnp.int32, (ROWS, C), 1) & 15
    lp = jnp.where(which == 0, l1, jnp.where(which == 1, l2, jnp.where(which == 2, l3, 0.0))).astype(BF16)
    place((qh, ql, lp), (0, 0, 1, 1, 2), qp)
    khi, klo = split2(qkv[:, C : 2 * C])
    place((khi, klo), (0, 1, 0, 1), kp, const=lambda lane: (lane >= 64) & (lane < 67))
    kh[...] = khi
    kl[...] = klo
    place(split2(qkv[:, 2 * C :]), (0, 1, 0, 1), vp, const=lambda lane: (lane >= 64) & (lane < 96))
    stack_heads(q, q_t)


def backward_operands(rows, lse, gain, w_qkv):
    return pl.pallas_call(
        prep_kernel,
        out_shape=(jax.ShapeDtypeStruct((HEADS, ROWS, C), BF16),) * 3
        + (jax.ShapeDtypeStruct((ROWS, C), BF16),) * 2
        + (jax.ShapeDtypeStruct((HEADS, 2 * HD, ROWS), BF16),),
        compiler_params=vmem(24),
        cost_estimate=pl.CostEstimate(flops=6_000_000_000, bytes_accessed=8_000_000, transcendentals=0),
        name="backward_operands",
    )(rows, lse, gain, w_qkv)


def bwd_kernel(
    r_ref, o_ref, ot_ref, gain_ref, wqkv_ref, wout_ref, pid_ref, gw_ref, gg2_ref,
    qp, kp, vp, kh, kl, q_t, d0, d1, d2, d3, e0, e1, e2, e3,
    df_ref, flat,
    dop, tab, da_ref, dot_t, dv_t, dk_t, dq_ref,
):
    core, y = place_of_device()
    for chunk, ref in enumerate((d0, d1, d2, d3, e0, e1, e2, e3)):
        hi, lo = split2(ref[...])
        tab[chunk * 256 : chunk * 256 + 256, :C] = hi
        tab[chunk * 256 : chunk * 256 + 256, C:] = lo
    lane = lax.broadcasted_iota(jnp.int32, (DBLK, C), 1)
    for blk in range(ROWS // DBLK):
        rows = pl.ds(blk * DBLK, DBLK)
        pid = pid_ref[rows]
        index = (((pid >> 10) ^ core) << 10) + (((y - (pid >> 8)) & 3) << 8) + (pid & 255)
        got = dot(one_hot_tiles(tile_key(index, lane), range(16)), tab[...])
        da_ref[rows] = got[:, :C] + got[:, C:]

    da = da_ref[...]
    do = dot3_nt(da, wout_ref[...])
    place((*split2(do), *split2(-do * o_ref[...])), (0, 0, 1, 1, 2, 3), dop)
    stack_heads(do, dot_t)

    def head(h, carry):
        kmask = head_mask((ROWS, C), h)
        zero = jnp.zeros((), BF16)
        ka = jnp.concatenate([jnp.where(kmask, kh[...], zero), jnp.where(kmask, kl[...], zero)], axis=1)
        keys, vals = kp[h], vp[h]
        mask = head_mask((BBLK, C), h)
        dv = jnp.zeros((2 * HD, ROWS), F32)
        dk = jnp.zeros((2 * HD, ROWS), F32)
        for blk in range(ROWS // BBLK):
            rows = pl.ds(blk * BBLK, BBLK)
            p = jnp.exp2(dot_nt(qp[h, rows], keys))
            ds = p * dot_nt(dop[h, rows], vals)
            ph, plo = split2(p)
            sh, sl = split2(ds)
            left = dot_t[h, :, rows]
            dv = dv + (dot(left, ph) + dot(left, plo))
            left = q_t[h, :, rows]
            dk = dk + (dot(left, sh) + dot(left, sl))
            dq = dot(sh, ka) + dot(sl, ka)
            dq_ref[rows] = jnp.where(mask, dq[:, :C] + dq[:, C:], dq_ref[rows])
        place_rows = pl.ds(pl.multiple_of(h * HD, HD), HD)
        dv_t[place_rows] = dv[:HD] + dv[HD:]
        dk_t[place_rows] = dk[:HD] + dk[HD:]
        return carry

    lax.fori_loop(0, HEADS, head, 0, unroll=UNROLL)
    xhat, rstd = norm_rows(r_ref[...].astype(F32))
    u = xhat * gain_ref[...]
    grads = jnp.concatenate([dq_ref[...] * HD ** (-0.5), dk_t[...].T * LN2, dv_t[...].T], axis=1)
    du = dot3_nt(grads, wqkv_ref[...])
    gq = dot3(u.T, grads)
    for part in range(3):
        flat[part * C : part * C + C] = gq[:, part * C : part * C + C]
    flat[3 * C : 4 * C] = dot3(ot_ref[...], da)
    flat[4 * C : 6 * C] = gw_ref[...]
    row = lax.broadcasted_iota(jnp.int32, (8, C), 0)
    gains = jnp.where(row == 0, jnp.sum(du * xhat, axis=0, keepdims=True), gg2_ref[...])
    flat[6 * C : 6 * C + 8] = gains
    flat[6 * C + 8 :] = jnp.zeros((2 * C - 8, C), F32)
    dn = du * gain_ref[...]
    dx = rstd * (dn - jnp.mean(dn, -1, keepdims=True) - xhat * jnp.mean(dn * xhat, -1, keepdims=True))
    df_ref[...] = (da + dx).astype(BF16)


def attention_backward(rows, o, o_t, gain, w_qkv, w_out, pid, grad_pool, grad_gain_two, operands, d_pooled):
    return pl.pallas_call(
        bwd_kernel,
        out_shape=(jax.ShapeDtypeStruct((ROWS, C), BF16), jax.ShapeDtypeStruct((8 * C, C), F32)),
        scratch_shapes=[
            pltpu.VMEM((HEADS, ROWS, C), BF16),
            pltpu.VMEM((2048, 2 * C), BF16),
            pltpu.VMEM((ROWS, C), F32),
            pltpu.VMEM((HEADS, 2 * HD, ROWS), BF16),
            pltpu.VMEM((C, ROWS), F32),
            pltpu.VMEM((C, ROWS), F32),
            pltpu.VMEM((ROWS, C), F32),
        ],
        compiler_params=vmem(34),
        cost_estimate=pl.CostEstimate(flops=90_000_000_000, bytes_accessed=8_000_000, transcendentals=8_400_000),
        name="attention_backward",
    )(rows, o, o_t, gain, w_qkv, w_out, pid, grad_pool, grad_gain_two, *operands, *d_pooled)


def rows_kernel(gord_ref, a0, a1, a2, a3, ao, f0, f1, f2a, f2b, f3, fo, s0, s3_ref, gf_ref, s4_ref):
    core, y = place_of_device()
    att = [ref[:ROWS] for ref in (a0, a1, a2, a3)] + [ao[k] for k in range(4)]
    opposite = jnp.concatenate([f2a[...], f2b[...]], axis=0)
    grad = [f0[...], f1[...], opposite, f3[...]] + [fo[k] for k in range(4)]
    own = lax.broadcasted_iota(jnp.int32, (RBLK, C), 0) + (core * 4 + y) * ROWS
    for blk in range(ROWS // RBLK):
        rows = pl.ds(blk * RBLK, RBLK)
        got = jnp.zeros((RBLK, 2 * C), F32)
        for slot in range(8):
            ids = gord_ref[slot * 8 : slot * 8 + 8] - blk * RBLK
            hot = jnp.concatenate([jnp.where(own == ids[t : t + 1], 1.0, 0.0) for t in range(8)], axis=1).astype(BF16)
            got = got + dot(hot, jnp.concatenate([att[slot], grad[slot]], axis=1))
        s3_ref[rows] = got[:, :C].astype(BF16)
        gf_ref[rows] = got[:, C:].astype(BF16)
    s4_ref[:, pl.ds(pl.multiple_of(y * 256, 256), 256)] = s0[...]
    for k, ref in ((1, a3), (2, a2), (3, a1)):
        block = jnp.concatenate([ref[ROWS : ROWS + 64], ref[ROWS + 64 :]], axis=1)
        s4_ref[:, pl.ds(pl.multiple_of(((y + k) & 3) * 256, 256), 256)] = block


def results(gord, att, grad, s4):
    return pl.pallas_call(
        rows_kernel,
        out_shape=(
            jax.ShapeDtypeStruct((ROWS, C), BF16),
            jax.ShapeDtypeStruct((ROWS, C), BF16),
            jax.ShapeDtypeStruct((64, ROWS), BF16),
        ),
        compiler_params=vmem(60),
        cost_estimate=pl.CostEstimate(flops=8_000_000_000, bytes_accessed=5_000_000, transcendentals=0),
        name="rows_to_z_order",
    )(gord, *att, *grad, s4)


def params_kernel(flat, gq_ref, go_ref, g1_ref, gw_ref, g2_ref):
    _, y = place_of_device()
    for part in range(3):
        gq_ref[:, part * C : part * C + C] = flat[part * C : part * C + C]
    go_ref[...] = flat[3 * C : 4 * C]
    gw_ref[...] = flat[pl.ds(pl.multiple_of(4 * C + y * 64, 64), 64)]
    gains = flat[6 * C : 6 * C + 8]
    g1_ref[...] = gains[0:1]
    pair = jnp.where(y >= 2, gains[2:3], gains[1:2])
    g2_ref[...] = jnp.where((y & 1) == 0, pair[:, :64], pair[:, 64:])


def parameter_results(flat):
    return pl.pallas_call(
        params_kernel,
        out_shape=(
            jax.ShapeDtypeStruct((C, 3 * C), F32),
            jax.ShapeDtypeStruct((C, C), F32),
            jax.ShapeDtypeStruct((1, C), F32),
            jax.ShapeDtypeStruct((64, C), F32),
            jax.ShapeDtypeStruct((1, 64), F32),
        ),
        compiler_params=vmem(8),
        name="parameter_results",
    )(flat)


def message_kernel(m0, m1, m2a, m2b, m3, after1, after2, after3, out_ref):
    out_ref[0] = m0[...]
    out_ref[1] = m1[...]
    out_ref[2, :HALF] = m2a[...]
    out_ref[2, HALF:] = m2b[...]
    out_ref[3] = m3[...]


def core_message(blocks, after):
    return pl.pallas_call(
        message_kernel,
        in_specs=[pl.BlockSpec(memory_space=pltpu.VMEM)] * 5 + [pl.BlockSpec(memory_space=pl.ANY)] * 3,
        out_shape=jax.ShapeDtypeStruct((4, MESSAGE, C), BF16),
        compiler_params=vmem(8),
        name="core_message",
    )(*blocks, *after)


def four_kernel(*refs):
    *blocks, rows_ref = refs
    if len(blocks) == 5:
        b0, b1, b2a, b2b, b3 = blocks
        rows_ref[2, : ROWS // 2] = b2a[...]
        rows_ref[2, ROWS // 2 :] = b2b[...]
        blocks = [b0, b1, None, b3]
    for k, ref in enumerate(blocks):
        if ref is not None:
            rows_ref[k] = ref[:ROWS]


def four_rows(blocks):
    return pl.pallas_call(
        four_kernel,
        out_shape=jax.ShapeDtypeStruct((4, ROWS, C), BF16),
        compiler_params=vmem(8),
        name="four_rows",
    )(*blocks)


def share_kernel(shares, out_ref):
    total = shares[0]
    for source in range(1, shares.shape[0]):
        total = total + shares[source]
    out_ref[...] = jnp.broadcast_to(total, out_ref.shape)


def share_of_all(shares):
    return pl.pallas_call(
        share_kernel,
        out_shape=jax.ShapeDtypeStruct(shares.shape, F32),
        compiler_params=vmem(8),
        name="share_of_all",
    )(shares)


def shift(block, axis, apart):
    count = lax.axis_size(axis)
    return lax.ppermute(block, axis, [(i, (i + apart) % count) for i in range(count)])


EVERYWHERE = ("x", "z", "core", "grp")


def deal_rows(flat):
    return lax.all_to_all(flat.reshape(lax.axis_size(EVERYWHERE), -1, flat.shape[1]), EVERYWHERE, 0, 0)


def gather_rows_of_all(shares):
    count = lax.axis_size(EVERYWHERE)
    every = lax.all_to_all(shares, EVERYWHERE, 0, 0)
    return every.reshape(-1, shares.shape[2])


def relay_y(block):
    half = block.shape[0] // 2
    left = shift(block, "grp", 1)
    right = shift(block, "grp", -1)
    return left, shift(right[:half], "grp", -1), shift(left[half:], "grp", 1), right


def shards(feats, order, parent, gain_one, w_qkv, w_out, w_pool, gain_two, cotangent):
    order = order.reshape(8, C)
    msg, *w_msgs = pack(feats, order, parent.reshape(8, C), cotangent.T, w_pool.T, gain_two[None])

    around = relay_y(msg)
    w_msgs = [w_msgs[0]] + [shift(w_msgs[k], "grp", k) for k in (1, 2, 3)]
    other = shift(core_message((msg, *around), w_msgs[1:]), "core", 1)
    hilbert, pid, gord, cnt, att, mine, theirs, o, o_t, lse = attention_forward(
        order, (msg, *around, other), gain_one[None], w_qkv, w_out
    )

    operands = backward_operands(hilbert, lse, gain_one[None], w_qkv)

    theirs = shift(theirs, "core", 1)
    chunks = [shift(mine[k] + theirs[k], "grp", k) for k in (1, 2, 3)]
    s4, *rows, d_pool, grad_pool, grad_gain_two = pooled_section(mine, theirs, chunks, cnt, att, w_msgs, operands[-1])
    own = [d_pool] + [shift(d_pool, "grp", k) for k in (1, 2, 3)]
    d_pooled = own + [shift(block, "core", 1) for block in own]

    from_y = [shift(rows[k - 1], "grp", -k) for k in (3, 2, 1)]
    att = [att] + from_y

    df, flat = attention_backward(
        hilbert, o, o_t, gain_one[None], w_qkv, w_out, pid, grad_pool, grad_gain_two, operands, d_pooled
    )
    left = shift(df, "grp", 1)
    right = shift(df, "grp", -1)
    att_rows = four_rows(att)
    flat, left, right, att_rows = lax.optimization_barrier((flat, left, right, att_rows))
    shares = deal_rows(flat)
    att.append(shift(att_rows, "core", 1))
    half = ROWS // 2
    upper = shift(right[:half], "grp", -1)
    lower = shift(left[half:], "grp", 1)
    shares, upper, lower = lax.optimization_barrier((shares, upper, lower))
    df = [df, left, upper, lower, right]
    df.append(shift(four_rows(df), "core", 1))
    total = gather_rows_of_all(share_of_all(shares))
    rows = results(gord, att, df, s4)
    total, rows = lax.optimization_barrier((total, rows))
    section_three, grad_feats, section_four = rows
    g_qkv, g_out, g_one, g_pool, g_two = parameter_results(total)
    return (section_four.T, section_three, grad_feats, g_one[0], g_qkv, g_out, g_pool.T, g_two[0])


def solution(mesh):
    fine = Mesh(mesh.devices.reshape(4, 4, 2, 4), ("x", "z", "core", "grp"))
    pts = ("x", "z", "core")
    everywhere = pts + ("grp",)
    placed = (
        P(everywhere, None),
        P(everywhere),
        P(everywhere),
        P(),
        P(),
        P(),
        P(None, "grp"),
        P("grp"),
        P(pts, "grp"),
    )
    return jax.shard_map(
        shards,
        mesh=fine,
        in_specs=placed,
        out_specs=(
            P(pts, "grp"),
            P(everywhere, None),
            P(everywhere, None),
            P(),
            P(),
            P(),
            P(None, "grp"),
            P("grp"),
        ),
        check_vma=False,
    )
```

```python
import math

import jax
import jax.numpy as jnp
from jax import lax
from jax.experimental import pallas as pl
from jax.experimental.pallas import tpu as pltpu
from jax.sharding import Mesh, PartitionSpec as P

F32 = jnp.float32
BF16 = jnp.bfloat16
HEADS = 8
HD = 16
C = 128
ROWS = 1024
FBLK = 128
SBLK = 256
UNROLL = 4
BBLK = 256
GBLK = 256
DBLK = 256
RBLK = 256
EPS = 1e-05
QSCALE = HD ** (-0.5) * math.log2(math.e)
LN2 = math.log(2.0)
GELU_A = math.sqrt(2.0 / math.pi)
GELU_B = 0.044715


def vmem(mib):
    return pltpu.CompilerParams(vmem_limit_bytes=mib * 1024 * 1024)


def dot(a, b):
    return jnp.dot(a, b, preferred_element_type=F32)


def dot_nt(a, b):
    return lax.dot_general(a, b, (((1,), (1,)), ((), ())), preferred_element_type=F32)


def split2(x):
    hi = x.astype(BF16)
    return hi, (x - hi.astype(F32)).astype(BF16)


def dot3(a, b):
    ah, al = split2(a)
    bh, bl = split2(b)
    return dot(ah, bh) + (dot(al, bh) + dot(ah, bl))


def dot3_nt(a, b):
    ah, al = split2(a)
    bh, bl = split2(b)
    return dot_nt(ah, bh) + (dot_nt(al, bh) + dot_nt(ah, bl))


def norm_rows(values):
    center = values - jnp.mean(values, -1, keepdims=True)
    rstd = lax.rsqrt(jnp.mean(center * center, -1, keepdims=True) + EPS)
    return center * rstd, rstd


def select_matrix(parts, part_of_slot):
    shape = (parts * C, HEADS * C)
    row = lax.broadcasted_iota(jnp.int32, shape, 0)
    col = lax.broadcasted_iota(jnp.int32, shape, 1)
    slot = (col >> 4) & 7
    wanted = jnp.full(shape, parts, jnp.int32)
    for index, part in enumerate(part_of_slot):
        wanted = jnp.where(slot == index, part, wanted)
    hit = (row & 127) == ((col >> 7) * HD + (col & 15))
    hit = hit & ((row >> 7) == wanted)
    return jnp.where(hit, 1.0, 0.0).astype(BF16)


def place(parts, part_of_slot, out_ref, const=None):
    sel = select_matrix(len(parts), part_of_slot)
    packed = jnp.concatenate(parts, axis=1)
    for pair in range(HEADS // 2):
        both = dot(packed, sel[:, pair * 256 : pair * 256 + 256])
        for half in range(2):
            block = both[:, half * C : half * C + C]
            if const is not None:
                block = jnp.where(const(lax.broadcasted_iota(jnp.int32, block.shape, 1)), 1.0, block)
            out_ref[2 * pair + half] = block.astype(BF16)


def tile_key(column, lane):
    return jnp.where((column & 127) == lane, column >> 7, -1).astype(F32).astype(BF16)


def one_hot_tiles(key, tiles):
    one, zero = jnp.ones((), BF16), jnp.zeros((), BF16)
    return jnp.concatenate([jnp.where(key == jnp.full((), t, BF16), one, zero) for t in tiles], axis=1)


def one_hot_rows(row, iota):
    row = jnp.where((row >= 0) & (row < 256), row, 512).astype(F32)
    row = jnp.broadcast_to(row, (16, row.shape[1])).astype(BF16)
    row = jnp.concatenate([row] * (iota.shape[0] // 16), axis=0)
    return jnp.where(row == iota, jnp.ones((), BF16), jnp.zeros((), BF16))


def iota_rows(columns):
    return lax.broadcasted_iota(jnp.int32, (256, columns), 0).astype(F32).astype(BF16)


def head_norms(x):
    row = lax.broadcasted_iota(jnp.int32, (C, C), 0)
    col = lax.broadcasted_iota(jnp.int32, (C, C), 1)
    same = jnp.where((row >> 4) == (col >> 4), 1.0, 0.0).astype(BF16)
    return jnp.max(dot((x * x * 1.02).astype(BF16), same), axis=0, keepdims=True)


def head_mask(shape, h):
    return (lax.broadcasted_iota(jnp.int32, shape, 1) >> 4) == h


def place_of_device():
    return lax.axis_index("core"), lax.axis_index("grp")


HALF = 528
MESSAGE = 2 * HALF


def pack_kernel(feats, order, parent, cot, w, gain, msg_ref, r_ref, l_ref, own_ref, order_v, parent_v, cot_v, w_v, gain_v, sems):
    _, y = place_of_device()
    copies = [
        pltpu.make_async_copy(source, target, sems.at[index])
        for index, (source, target) in enumerate(
            (
                (order, order_v),
                (parent, parent_v),
                (feats, msg_ref.at[pl.ds(0, ROWS)]),
                (gain, gain_v),
                (w, w_v),
                (cot, cot_v),
            )
        )
    ]
    for copy in copies:
        copy.start()
    for copy in copies:
        copy.wait()
    near = order_v[...] & 8191
    owner = parent_v[...] & 2047
    ids = jnp.concatenate([near >> 6, near & 63, owner >> 6, owner & 63], axis=0)
    msg_ref[ROWS:] = ids.astype(F32).astype(BF16)
    w_high, w_low = split2(w_v[...])
    total = gain_v[...]
    first = total.astype(BF16).astype(F32)
    second = (total - first).astype(BF16).astype(F32)
    third = total - first - second
    row = lax.broadcasted_iota(jnp.int32, (16, 64), 0)
    gains = jnp.where(row == 0, first, jnp.where(row == 1, second, jnp.where(row == 2, third, 0.0)))
    gains = jnp.concatenate([gains, jnp.zeros((16, 64), F32)], axis=1).astype(BF16)

    def cot(k, half):
        start = ((y + k) & 3) * 256 + half * C
        return cot_v[:, pl.ds(pl.multiple_of(start, C), C)]

    own_ref[...] = pool_message(cot(0, 0), cot(0, 1), w_high, w_low, gains)
    r_ref[:64] = cot(1, 0)
    r_ref[64:128] = cot(1, 1)
    r_ref[128:192] = w_high
    r_ref[192:1248] = msg_ref[...]
    r_ref[1248:1312] = w_low
    r_ref[1312:1328] = gains
    r_ref[1328:] = cot(2, 1)
    l_ref[:64] = cot(2, 0)
    l_ref[64:128] = w_high
    l_ref[128:1184] = msg_ref[...]
    l_ref[1184:1248] = w_low
    l_ref[1248:1264] = gains
    l_ref[1264:1328] = cot(3, 0)
    l_ref[1328:] = cot(3, 1)


def pool_message(cot_low, cot_high, w_high, w_low, gains):
    rows = [
        jnp.concatenate([cot_low, cot_high], axis=1),
        jnp.concatenate([w_high, w_low], axis=1),
        jnp.concatenate([gains, jnp.zeros_like(gains)], axis=1),
    ]
    return jnp.concatenate(rows, axis=0)


def pack(feats, order, parent, cot_t, w_t, gain_two):
    return pl.pallas_call(
        pack_kernel,
        in_specs=[pl.BlockSpec(memory_space=pltpu.HBM)] * 6,
        out_shape=(
            jax.ShapeDtypeStruct((MESSAGE, C), BF16),
            jax.ShapeDtypeStruct((1392, C), BF16),
            jax.ShapeDtypeStruct((1392, C), BF16),
            jax.ShapeDtypeStruct((144, 256), BF16),
        ),
        scratch_shapes=[
            pltpu.VMEM((8, C), jnp.int32),
            pltpu.VMEM((8, C), jnp.int32),
            pltpu.VMEM((64, ROWS), BF16),
            pltpu.VMEM((64, C), F32),
            pltpu.VMEM((1, 64), F32),
            pltpu.SemaphoreType.DMA((6,)),
        ],
        compiler_params=vmem(60),
        name="pack",
    )(feats, order, parent, cot_t, w_t, gain_two)


def gather_rows(order_ref, blocks, tab, rep, hil_ref, pid_ref, gord_ref, cnt_ref):
    core, y = place_of_device()
    lane = lax.broadcasted_iota(jnp.int32, (C, C), 1)
    digits = []
    for slot, (rows, ids) in enumerate(blocks):
        for start, part in rows:
            tab[slot, start : start + part.shape[0], :C] = part
        ids = ids.astype(F32)
        gord_ref[slot * 8 : slot * 8 + 8] = (ids[:8] * 64.0 + ids[8:16]).astype(jnp.int32)
        digits.append(ids[16:])
    digits = jnp.concatenate(digits, axis=0)
    turned = digits.T
    for slot in range(8):
        for t in range(8):
            tab[slot, t * C : t * C + C, C:] = jnp.where((lane & ~8) == slot * 16 + t, turned, 0.0).astype(BF16)

    count = jnp.zeros((256, C), F32)
    target = (lax.broadcasted_iota(jnp.int32, (256, C), 0) + (core * 1024 + y * 256)).astype(F32)
    for slot in range(4):
        parents = digits[slot * 16 : slot * 16 + 8] * 64.0 + digits[slot * 16 + 8 : slot * 16 + 16]
        for t in range(8):
            count = count + jnp.where(target == parents[t : t + 1], 1.0, 0.0)
    cnt_ref[...] = jnp.broadcast_to(jnp.sum(count, axis=1, keepdims=True), cnt_ref.shape)

    order = order_ref[...]
    source = (order >> 10) & 7
    slot = (((source >> 2) ^ core) << 2) + ((y - source) & 3)
    index = (slot * ROWS + (order & 1023)).astype(F32)
    for t in range(8):
        column = jnp.broadcast_to(index[t : t + 1], (C, C)).T.astype(jnp.int32)
        rep[t * C : t * C + C] = tile_key(column, lane)
    weight = jnp.where(lax.broadcasted_iota(jnp.int32, (GBLK, C), 1) & 8 == 0, 64.0, 1.0)
    for blk in range(ROWS // GBLK):
        rows = pl.ds(blk * GBLK, GBLK)
        away = rep[rows]
        got = jnp.zeros((GBLK, 2 * C), F32)
        for slot in range(8):
            got = got + dot(one_hot_tiles(away, range(slot * 8, slot * 8 + 8)), tab[slot])
        hil_ref[rows] = got[:, :C].astype(BF16)
        parent = jnp.sum(got[:, C:] * weight, axis=1, keepdims=True).astype(jnp.int32)
        pid_ref[rows] = jnp.broadcast_to(parent, (GBLK, C))


def fwd_kernel(
    order_ref, own, left, upper, lower, right, other, gain_ref, wqkv_ref, wout_ref,
    hil_ref, pid_ref, gord_ref, cnt_ref, att_ref, mine_ref, theirs_ref, o_ref, ot_ref, lse_ref,
    tab, rep, qp, kp, vt, lt, ac,
):
    core, y = place_of_device()
    blocks = [
        ([(0, own[:ROWS])], own[ROWS:]),
        ([(0, left[192:1216])], left[1216:1248]),
        ([(0, upper[128:]), (HALF, lower[: ROWS - HALF])], lower[ROWS - HALF : HALF]),
        ([(0, right[128:1152])], right[1152:1184]),
    ] + [([(0, other[k, :ROWS])], other[k, ROWS:]) for k in range(4)]
    gather_rows(order_ref, blocks, tab, rep, hil_ref, pid_ref, gord_ref, cnt_ref)

    r = hil_ref[...].astype(F32)
    xhat, _ = norm_rows(r)
    u = xhat * gain_ref[...]
    qkv = dot3(u, wqkv_ref[...])
    q = qkv[:, :C] * QSCALE
    k = qkv[:, C : 2 * C]
    place(split2(q), (0, 0, 1, 1), qp)
    place(split2(k), (0, 1, 0, 1), kp)
    for index, part in enumerate(split2(qkv[:, 2 * C :].T)):
        for h in range(HEADS):
            vt[h, index * HD : index * HD + HD] = part[h * HD : h * HD + HD]
    vt[:, 2 * HD :] = jnp.ones((HEADS, HD, ROWS), BF16)

    def head(size, shifted):
        def body(h, carry):
            keys = kp[h]
            values = vt[h]
            own = pl.ds(pl.multiple_of(h * HD, HD), HD)
            for blk in range(ROWS // size):
                cols = pl.ds(blk * size, size)
                s = dot_nt(keys, qp[h, cols])
                if shifted:
                    m = jnp.max(s, axis=0, keepdims=True)
                    s = s - m
                ph, plo = split2(jnp.exp2(s))
                oa = dot(values, ph) + dot(values, plo)
                total = oa[2 * HD : 2 * HD + 1]
                ot_ref[own, cols] = (oa[:HD] + oa[HD : 2 * HD]) / total
                lse = jnp.log2(total)
                if shifted:
                    lse = lse + m
                lt[own, cols] = jnp.broadcast_to(lse, (HD, size))
            return carry

        return body

    small = jnp.max(head_norms(q) * head_norms(k)) < 3600.0

    @pl.when(small)
    def _():
        lax.fori_loop(0, HEADS, head(FBLK, False), 0, unroll=UNROLL)

    @pl.when(jnp.logical_not(small))
    def _():
        lax.fori_loop(0, HEADS, head(SBLK, True), 0)

    o_ref[...] = ot_ref[...].T
    lse_ref[...] = lt[...].T
    att = r + dot3(o_ref[...], wout_ref[...])
    hi, lo = split2(att)
    att_ref[...] = hi
    ac[...] = jnp.concatenate([hi, lo], axis=1)
    parent = pid_ref[...].astype(F32).T[0:1].astype(jnp.int32)
    pid = (((parent >> 10) ^ core) << 10) + ((((parent >> 8) - y) & 3) << 8) + (parent & 255)
    for chunk in range(8):
        sums = dot(one_hot_rows(pid - chunk * 256, iota_rows(ROWS)), ac[...])
        target = mine_ref if chunk < 4 else theirs_ref
        target[chunk & 3] = sums[:, :C] + sums[:, C:]


def attention_forward(order, blocks, gain, w_qkv, w_out):
    return pl.pallas_call(
        fwd_kernel,
        out_shape=(
            jax.ShapeDtypeStruct((ROWS, C), BF16),
            jax.ShapeDtypeStruct((ROWS, C), jnp.int32),
            jax.ShapeDtypeStruct((64, C), jnp.int32),
            jax.ShapeDtypeStruct((256, C), F32),
            jax.ShapeDtypeStruct((ROWS, C), BF16),
            jax.ShapeDtypeStruct((4, 256, C), F32),
            jax.ShapeDtypeStruct((4, 256, C), F32),
            jax.ShapeDtypeStruct((ROWS, C), F32),
            jax.ShapeDtypeStruct((C, ROWS), F32),
            jax.ShapeDtypeStruct((ROWS, C), F32),
        ),
        scratch_shapes=[
            pltpu.VMEM((8, ROWS, 2 * C), BF16),
            pltpu.VMEM((ROWS, C), BF16),
            pltpu.VMEM((HEADS, ROWS, C), BF16),
            pltpu.VMEM((HEADS, ROWS, C), BF16),
            pltpu.VMEM((HEADS, 3 * HD, ROWS), BF16),
            pltpu.VMEM((C, ROWS), F32),
            pltpu.VMEM((ROWS, 2 * C), BF16),
        ],
        compiler_params=vmem(30),
        cost_estimate=pl.CostEstimate(flops=30_000_000_000, bytes_accessed=4_000_000, transcendentals=8_400_000),
        name="attention_forward",
    )(order, *blocks, gain, w_qkv, w_out)


def pool_kernel(mine, theirs, c1, c2, c3, cnt_ref, att_ref, w0, w1, w2, w3, after, s0, t1, t2, t3, dp_ref, gw_ref, gg_ref):
    cnt = cnt_ref[...]
    pooled = (mine[0] + theirs[0] + c1[...] + c2[...] + c3[...]) / cnt
    msgs = (w0, w1, w2, w3)
    wh = jnp.concatenate([m[64:128, :C] for m in msgs], axis=0)
    wl = jnp.concatenate([m[64:128, C:] for m in msgs], axis=0)
    cot = jnp.concatenate([m[:64] for m in msgs], axis=0).astype(F32).T
    gains = jnp.concatenate([m[128:, :64] for m in msgs], axis=1).astype(F32)
    gain = gains[0:1] + gains[1:2] + gains[2:3]
    ph, plo = split2(pooled)
    normed, rstd = norm_rows(dot_nt(ph, wh) + (dot_nt(plo, wh) + dot_nt(ph, wl)))
    v = normed * gain
    t = jnp.tanh(GELU_A * (v + GELU_B * (v * v * v)))
    s4 = (0.5 * v * (1.0 + t)).T.astype(BF16)
    s0[...] = s4[:64]
    for k, ref in enumerate((t1, t2, t3)):
        block = s4[64 * k + 64 : 64 * k + 128]
        ref[:ROWS] = att_ref[...]
        ref[ROWS : ROWS + 64] = block[:, :C]
        ref[ROWS + 64 :] = block[:, C:]
    slope = 0.5 * (1.0 + t) + 0.5 * v * (1.0 - t * t) * (GELU_A * (1.0 + (3.0 * GELU_B) * (v * v)))
    d_scaled = cot * slope
    d_normed = d_scaled * gain
    d_proj = rstd * (
        d_normed
        - jnp.mean(d_normed, -1, keepdims=True)
        - normed * jnp.mean(d_normed * normed, -1, keepdims=True)
    )
    dh, dl = split2(d_proj)
    dp_ref[...] = (dot(dh, wh) + (dot(dl, wh) + dot(dh, wl))) / cnt
    _, y = place_of_device()
    gw = dot3(d_proj.T, pooled)
    gg = jnp.sum(d_scaled * normed, axis=0, keepdims=True)
    gains = jnp.zeros((8, C), F32)
    row = lax.broadcasted_iota(jnp.int32, (8, C), 0)
    low = lax.broadcasted_iota(jnp.int32, (8, C), 1) < 64
    for k in range(4):
        owner = (y - k) & 3
        gw_ref[pl.ds(pl.multiple_of(owner * 64, 64), 64)] = gw[64 * k : 64 * k + 64]
        block = gg[:, 64 * k : 64 * k + 64]
        twice = jnp.concatenate([block, block], axis=1)
        hit = (row == 1 + (owner >> 1)) & (low == ((owner & 1) == 0))
        gains = jnp.where(hit, twice, gains)
    gg_ref[...] = gains


def pooled_section(mine, theirs, chunks, cnt, att, msgs, after):
    return pl.pallas_call(
        pool_kernel,
        in_specs=[pl.BlockSpec(memory_space=pltpu.VMEM)] * 11 + [pl.BlockSpec(memory_space=pl.ANY)],
        out_shape=(jax.ShapeDtypeStruct((64, 256), BF16),)
        + (jax.ShapeDtypeStruct((ROWS + 128, C), BF16),) * 3
        + (
            jax.ShapeDtypeStruct((256, C), F32),
            jax.ShapeDtypeStruct((256, C), F32),
            jax.ShapeDtypeStruct((8, C), F32),
        ),
        compiler_params=vmem(12),
        name="pooled_section",
    )(mine, theirs, *chunks, cnt, att, *msgs, after)


def stack_heads(source, target):
    hi, lo = split2(source.T)
    for h in range(HEADS):
        target[h, :HD] = hi[h * HD : h * HD + HD]
        target[h, HD:] = lo[h * HD : h * HD + HD]


def prep_kernel(r_ref, lse_ref, gain_ref, wqkv_ref, qp, kp, vp, kh, kl, q_t):
    xhat, _ = norm_rows(r_ref[...].astype(F32))
    u = xhat * gain_ref[...]
    qkv = dot3(u, wqkv_ref[...])
    q = qkv[:, :C] * QSCALE
    qh, ql = split2(q)
    lse = -lse_ref[...]
    l1 = lse.astype(BF16).astype(F32)
    l2 = (lse - l1).astype(BF16).astype(F32)
    l3 = lse - l1 - l2
    which = lax.broadcasted_iota(jnp.int32, (ROWS, C), 1) & 15
    lp = jnp.where(which == 0, l1, jnp.where(which == 1, l2, jnp.where(which == 2, l3, 0.0))).astype(BF16)
    place((qh, ql, lp), (0, 0, 1, 1, 2), qp)
    khi, klo = split2(qkv[:, C : 2 * C])
    place((khi, klo), (0, 1, 0, 1), kp, const=lambda lane: (lane >= 64) & (lane < 67))
    kh[...] = khi
    kl[...] = klo
    place(split2(qkv[:, 2 * C :]), (0, 1, 0, 1), vp, const=lambda lane: (lane >= 64) & (lane < 96))
    stack_heads(q, q_t)


def backward_operands(rows, lse, gain, w_qkv):
    return pl.pallas_call(
        prep_kernel,
        out_shape=(jax.ShapeDtypeStruct((HEADS, ROWS, C), BF16),) * 3
        + (jax.ShapeDtypeStruct((ROWS, C), BF16),) * 2
        + (jax.ShapeDtypeStruct((HEADS, 2 * HD, ROWS), BF16),),
        compiler_params=vmem(24),
        cost_estimate=pl.CostEstimate(flops=6_000_000_000, bytes_accessed=8_000_000, transcendentals=0),
        name="backward_operands",
    )(rows, lse, gain, w_qkv)


def bwd_kernel(
    r_ref, o_ref, ot_ref, gain_ref, wqkv_ref, wout_ref, pid_ref, gw_ref, gg2_ref,
    qp, kp, vp, kh, kl, q_t, d0, d1, d2, d3, e0, e1, e2, e3,
    df_ref, flat,
    dop, tab, da_ref, dot_t, dv_t, dk_t, dq_ref,
):
    core, y = place_of_device()
    for chunk, ref in enumerate((d0, d1, d2, d3, e0, e1, e2, e3)):
        hi, lo = split2(ref[...])
        tab[chunk * 256 : chunk * 256 + 256, :C] = hi
        tab[chunk * 256 : chunk * 256 + 256, C:] = lo
    lane = lax.broadcasted_iota(jnp.int32, (DBLK, C), 1)
    for blk in range(ROWS // DBLK):
        rows = pl.ds(blk * DBLK, DBLK)
        pid = pid_ref[rows]
        index = (((pid >> 10) ^ core) << 10) + (((y - (pid >> 8)) & 3) << 8) + (pid & 255)
        got = dot(one_hot_tiles(tile_key(index, lane), range(16)), tab[...])
        da_ref[rows] = got[:, :C] + got[:, C:]

    da = da_ref[...]
    do = dot3_nt(da, wout_ref[...])
    place((*split2(do), *split2(-do * o_ref[...])), (0, 0, 1, 1, 2, 3), dop)
    stack_heads(do, dot_t)

    def head(h, carry):
        kmask = head_mask((ROWS, C), h)
        zero = jnp.zeros((), BF16)
        ka = jnp.concatenate([jnp.where(kmask, kh[...], zero), jnp.where(kmask, kl[...], zero)], axis=1)
        keys, vals = kp[h], vp[h]
        mask = head_mask((BBLK, C), h)
        dv = jnp.zeros((2 * HD, ROWS), F32)
        dk = jnp.zeros((2 * HD, ROWS), F32)
        for blk in range(ROWS // BBLK):
            rows = pl.ds(blk * BBLK, BBLK)
            p = jnp.exp2(dot_nt(qp[h, rows], keys))
            ds = p * dot_nt(dop[h, rows], vals)
            ph, plo = split2(p)
            sh, sl = split2(ds)
            left = dot_t[h, :, rows]
            dv = dv + (dot(left, ph) + dot(left, plo))
            left = q_t[h, :, rows]
            dk = dk + (dot(left, sh) + dot(left, sl))
            dq = dot(sh, ka) + dot(sl, ka)
            dq_ref[rows] = jnp.where(mask, dq[:, :C] + dq[:, C:], dq_ref[rows])
        place_rows = pl.ds(pl.multiple_of(h * HD, HD), HD)
        dv_t[place_rows] = dv[:HD] + dv[HD:]
        dk_t[place_rows] = dk[:HD] + dk[HD:]
        return carry

    lax.fori_loop(0, HEADS, head, 0, unroll=UNROLL)
    xhat, rstd = norm_rows(r_ref[...].astype(F32))
    u = xhat * gain_ref[...]
    grads = jnp.concatenate([dq_ref[...] * HD ** (-0.5), dk_t[...].T * LN2, dv_t[...].T], axis=1)
    du = dot3_nt(grads, wqkv_ref[...])
    gq = dot3(u.T, grads)
    for part in range(3):
        flat[part * C : part * C + C] = gq[:, part * C : part * C + C]
    flat[3 * C : 4 * C] = dot3(ot_ref[...], da)
    flat[4 * C : 6 * C] = gw_ref[...]
    row = lax.broadcasted_iota(jnp.int32, (8, C), 0)
    gains = jnp.where(row == 0, jnp.sum(du * xhat, axis=0, keepdims=True), gg2_ref[...])
    flat[6 * C : 6 * C + 8] = gains
    flat[6 * C + 8 :] = jnp.zeros((2 * C - 8, C), F32)
    dn = du * gain_ref[...]
    dx = rstd * (dn - jnp.mean(dn, -1, keepdims=True) - xhat * jnp.mean(dn * xhat, -1, keepdims=True))
    df_ref[...] = (da + dx).astype(BF16)


def attention_backward(rows, o, o_t, gain, w_qkv, w_out, pid, grad_pool, grad_gain_two, operands, d_pooled):
    return pl.pallas_call(
        bwd_kernel,
        out_shape=(jax.ShapeDtypeStruct((ROWS, C), BF16), jax.ShapeDtypeStruct((8 * C, C), F32)),
        scratch_shapes=[
            pltpu.VMEM((HEADS, ROWS, C), BF16),
            pltpu.VMEM((2048, 2 * C), BF16),
            pltpu.VMEM((ROWS, C), F32),
            pltpu.VMEM((HEADS, 2 * HD, ROWS), BF16),
            pltpu.VMEM((C, ROWS), F32),
            pltpu.VMEM((C, ROWS), F32),
            pltpu.VMEM((ROWS, C), F32),
        ],
        compiler_params=vmem(34),
        cost_estimate=pl.CostEstimate(flops=90_000_000_000, bytes_accessed=8_000_000, transcendentals=8_400_000),
        name="attention_backward",
    )(rows, o, o_t, gain, w_qkv, w_out, pid, grad_pool, grad_gain_two, *operands, *d_pooled)


def rows_kernel(gord_ref, a0, a1, a2, a3, ao, f0, f1, f2a, f2b, f3, fo, s0, s3_ref, gf_ref, s4_ref):
    core, y = place_of_device()
    att = [ref[:ROWS] for ref in (a0, a1, a2, a3)] + [ao[k] for k in range(4)]
    opposite = jnp.concatenate([f2a[...], f2b[...]], axis=0)
    grad = [f0[...], f1[...], opposite, f3[...]] + [fo[k] for k in range(4)]
    own = lax.broadcasted_iota(jnp.int32, (RBLK, C), 0) + (core * 4 + y) * ROWS
    for blk in range(ROWS // RBLK):
        rows = pl.ds(blk * RBLK, RBLK)
        got = jnp.zeros((RBLK, 2 * C), F32)
        for slot in range(8):
            ids = gord_ref[slot * 8 : slot * 8 + 8] - blk * RBLK
            hot = jnp.concatenate([jnp.where(own == ids[t : t + 1], 1.0, 0.0) for t in range(8)], axis=1).astype(BF16)
            got = got + dot(hot, jnp.concatenate([att[slot], grad[slot]], axis=1))
        s3_ref[rows] = got[:, :C].astype(BF16)
        gf_ref[rows] = got[:, C:].astype(BF16)
    s4_ref[:, pl.ds(pl.multiple_of(y * 256, 256), 256)] = s0[...]
    for k, ref in ((1, a3), (2, a2), (3, a1)):
        block = jnp.concatenate([ref[ROWS : ROWS + 64], ref[ROWS + 64 :]], axis=1)
        s4_ref[:, pl.ds(pl.multiple_of(((y + k) & 3) * 256, 256), 256)] = block


def results(gord, att, grad, s4):
    return pl.pallas_call(
        rows_kernel,
        out_shape=(
            jax.ShapeDtypeStruct((ROWS, C), BF16),
            jax.ShapeDtypeStruct((ROWS, C), BF16),
            jax.ShapeDtypeStruct((64, ROWS), BF16),
        ),
        compiler_params=vmem(60),
        cost_estimate=pl.CostEstimate(flops=8_000_000_000, bytes_accessed=5_000_000, transcendentals=0),
        name="rows_to_z_order",
    )(gord, *att, *grad, s4)


def params_kernel(flat, gq_ref, go_ref, g1_ref, gw_ref, g2_ref):
    _, y = place_of_device()
    for part in range(3):
        gq_ref[:, part * C : part * C + C] = flat[part * C : part * C + C]
    go_ref[...] = flat[3 * C : 4 * C]
    gw_ref[...] = flat[pl.ds(pl.multiple_of(4 * C + y * 64, 64), 64)]
    gains = flat[6 * C : 6 * C + 8]
    g1_ref[...] = gains[0:1]
    pair = jnp.where(y >= 2, gains[2:3], gains[1:2])
    g2_ref[...] = jnp.where((y & 1) == 0, pair[:, :64], pair[:, 64:])


def parameter_results(flat):
    return pl.pallas_call(
        params_kernel,
        out_shape=(
            jax.ShapeDtypeStruct((C, 3 * C), F32),
            jax.ShapeDtypeStruct((C, C), F32),
            jax.ShapeDtypeStruct((1, C), F32),
            jax.ShapeDtypeStruct((64, C), F32),
            jax.ShapeDtypeStruct((1, 64), F32),
        ),
        compiler_params=vmem(8),
        name="parameter_results",
    )(flat)


def message_kernel(own, left, upper, lower, right, out_ref, w1, w2, w3):
    out_ref[0] = own[...]
    out_ref[1] = left[192:1248]
    out_ref[2, :HALF] = upper[128:]
    out_ref[2, HALF:] = lower[:HALF]
    out_ref[3] = right[128:1184]
    w1[...] = pool_message(left[:64], left[64:128], left[128:192], left[1248:1312], left[1312:1328])
    w2[...] = pool_message(upper[:64], lower[608:], upper[64:128], lower[528:592], lower[592:608])
    w3[...] = pool_message(right[1264:1328], right[1328:], right[64:128], right[1184:1248], right[1248:1264])


def core_message(blocks):
    return pl.pallas_call(
        message_kernel,
        out_shape=(jax.ShapeDtypeStruct((4, MESSAGE, C), BF16),) + (jax.ShapeDtypeStruct((144, 256), BF16),) * 3,
        compiler_params=vmem(8),
        name="core_message",
    )(*blocks)


def four_kernel(*refs):
    *blocks, rows_ref = refs
    if len(blocks) == 5:
        b0, b1, b2a, b2b, b3 = blocks
        rows_ref[2, : ROWS // 2] = b2a[...]
        rows_ref[2, ROWS // 2 :] = b2b[...]
        blocks = [b0, b1, None, b3]
    for k, ref in enumerate(blocks):
        if ref is not None:
            rows_ref[k] = ref[:ROWS]


def four_rows(blocks):
    return pl.pallas_call(
        four_kernel,
        out_shape=jax.ShapeDtypeStruct((4, ROWS, C), BF16),
        compiler_params=vmem(8),
        name="four_rows",
    )(*blocks)


def share_kernel(shares, out_ref):
    total = shares[0]
    for source in range(1, shares.shape[0]):
        total = total + shares[source]
    out_ref[...] = jnp.broadcast_to(total, out_ref.shape)


def share_of_all(shares):
    return pl.pallas_call(
        share_kernel,
        out_shape=jax.ShapeDtypeStruct(shares.shape, F32),
        compiler_params=vmem(8),
        name="share_of_all",
    )(shares)


def shift(block, axis, apart):
    count = lax.axis_size(axis)
    return lax.ppermute(block, axis, [(i, (i + apart) % count) for i in range(count)])


EVERYWHERE = ("x", "z", "core", "grp")


def deal_rows(flat):
    return lax.all_to_all(flat.reshape(lax.axis_size(EVERYWHERE), -1, flat.shape[1]), EVERYWHERE, 0, 0)


def gather_rows_of_all(shares):
    count = lax.axis_size(EVERYWHERE)
    every = lax.all_to_all(shares, EVERYWHERE, 0, 0)
    return every.reshape(-1, shares.shape[2])


def shards(feats, order, parent, gain_one, w_qkv, w_out, w_pool, gain_two, cotangent):
    order = order.reshape(8, C)
    msg, to_right, to_left, own_pool = pack(
        feats, order, parent.reshape(8, C), cotangent.T, w_pool.T, gain_two[None]
    )

    left = shift(to_right, "grp", 1)
    right = shift(to_left, "grp", -1)
    around = (left, shift(right[:656], "grp", -1), shift(left[720:], "grp", 1), right)
    message, *pool_msgs = core_message((msg, *around))
    other = shift(message, "core", 1)
    w_msgs = [own_pool] + pool_msgs
    hilbert, pid, gord, cnt, att, mine, theirs, o, o_t, lse = attention_forward(
        order, (msg, *around, other), gain_one[None], w_qkv, w_out
    )

    operands = backward_operands(hilbert, lse, gain_one[None], w_qkv)

    theirs = shift(theirs, "core", 1)
    chunks = [shift(mine[k] + theirs[k], "grp", k) for k in (1, 2, 3)]
    s4, *rows, d_pool, grad_pool, grad_gain_two = pooled_section(mine, theirs, chunks, cnt, att, w_msgs, operands[-1])
    own = [d_pool] + [shift(d_pool, "grp", k) for k in (1, 2, 3)]
    d_pooled = own + [shift(block, "core", 1) for block in own]

    from_y = [shift(rows[k - 1], "grp", -k) for k in (3, 2, 1)]
    att = [att] + from_y

    df, flat = attention_backward(
        hilbert, o, o_t, gain_one[None], w_qkv, w_out, pid, grad_pool, grad_gain_two, operands, d_pooled
    )
    left = shift(df, "grp", 1)
    right = shift(df, "grp", -1)
    att_rows = four_rows(att)
    flat, left, right, att_rows = lax.optimization_barrier((flat, left, right, att_rows))
    shares = deal_rows(flat)
    att.append(shift(att_rows, "core", 1))
    half = ROWS // 2
    upper = shift(right[:half], "grp", -1)
    lower = shift(left[half:], "grp", 1)
    shares, upper, lower = lax.optimization_barrier((shares, upper, lower))
    df = [df, left, upper, lower, right]
    df.append(shift(four_rows(df), "core", 1))
    total = gather_rows_of_all(share_of_all(shares))
    rows = results(gord, att, df, s4)
    total, rows = lax.optimization_barrier((total, rows))
    section_three, grad_feats, section_four = rows
    g_qkv, g_out, g_one, g_pool, g_two = parameter_results(total)
    return (section_four.T, section_three, grad_feats, g_one[0], g_qkv, g_out, g_pool.T, g_two[0])


def solution(mesh):
    fine = Mesh(mesh.devices.reshape(4, 4, 2, 4), ("x", "z", "core", "grp"))
    pts = ("x", "z", "core")
    everywhere = pts + ("grp",)
    placed = (
        P(everywhere, None),
        P(everywhere),
        P(everywhere),
        P(),
        P(),
        P(),
        P(None, "grp"),
        P("grp"),
        P(pts, "grp"),
    )
    return jax.shard_map(
        shards,
        mesh=fine,
        in_specs=placed,
        out_specs=(
            P(pts, "grp"),
            P(everywhere, None),
            P(everywhere, None),
            P(),
            P(),
            P(),
            P(None, "grp"),
            P("grp"),
        ),
        check_vma=False,
    )
```

```python
import math

import jax
import jax.numpy as jnp
from jax import lax
from jax.experimental import pallas as pl
from jax.experimental.pallas import tpu as pltpu
from jax.sharding import Mesh, PartitionSpec as P

F32 = jnp.float32
BF16 = jnp.bfloat16
HEADS = 8
HD = 16
C = 128
ROWS = 1024
FBLK = 128
SBLK = 256
UNROLL = 4
BBLK = 256
GBLK = 512
DBLK = 512
RBLK = 256
EPS = 1e-05
QSCALE = HD ** (-0.5) * math.log2(math.e)
LN2 = math.log(2.0)
GELU_A = math.sqrt(2.0 / math.pi)
GELU_B = 0.044715


def vmem(mib):
    return pltpu.CompilerParams(vmem_limit_bytes=mib * 1024 * 1024)


def dot(a, b):
    return jnp.dot(a, b, preferred_element_type=F32)


def dot_nt(a, b):
    return lax.dot_general(a, b, (((1,), (1,)), ((), ())), preferred_element_type=F32)


def split2(x):
    hi = x.astype(BF16)
    return hi, (x - hi.astype(F32)).astype(BF16)


def dot3(a, b):
    ah, al = split2(a)
    bh, bl = split2(b)
    return dot(ah, bh) + (dot(al, bh) + dot(ah, bl))


def dot3_nt(a, b):
    ah, al = split2(a)
    bh, bl = split2(b)
    return dot_nt(ah, bh) + (dot_nt(al, bh) + dot_nt(ah, bl))


def norm_rows(values):
    center = values - jnp.mean(values, -1, keepdims=True)
    rstd = lax.rsqrt(jnp.mean(center * center, -1, keepdims=True) + EPS)
    return center * rstd, rstd


def select_matrix(parts, part_of_slot):
    shape = (parts * C, HEADS * C)
    row = lax.broadcasted_iota(jnp.int32, shape, 0)
    col = lax.broadcasted_iota(jnp.int32, shape, 1)
    slot = (col >> 4) & 7
    wanted = jnp.full(shape, parts, jnp.int32)
    for index, part in enumerate(part_of_slot):
        wanted = jnp.where(slot == index, part, wanted)
    hit = (row & 127) == ((col >> 7) * HD + (col & 15))
    hit = hit & ((row >> 7) == wanted)
    return jnp.where(hit, 1.0, 0.0).astype(BF16)


def place(parts, part_of_slot, out_ref, const=None):
    sel = select_matrix(len(parts), part_of_slot)
    packed = jnp.concatenate(parts, axis=1)
    for pair in range(HEADS // 2):
        both = dot(packed, sel[:, pair * 256 : pair * 256 + 256])
        for half in range(2):
            block = both[:, half * C : half * C + C]
            if const is not None:
                block = jnp.where(const(lax.broadcasted_iota(jnp.int32, block.shape, 1)), 1.0, block)
            out_ref[2 * pair + half] = block.astype(BF16)


def tile_key(column, lane):
    return jnp.where((column & 127) == lane, column >> 7, -1).astype(F32).astype(BF16)


def one_hot_tiles(key, tiles):
    one, zero = jnp.ones((), BF16), jnp.zeros((), BF16)
    return jnp.concatenate([jnp.where(key == jnp.full((), t, BF16), one, zero) for t in tiles], axis=1)


def one_hot_rows(row, iota):
    row = jnp.where((row >= 0) & (row < 256), row, 512).astype(F32)
    row = jnp.broadcast_to(row, (16, row.shape[1])).astype(BF16)
    row = jnp.concatenate([row] * (iota.shape[0] // 16), axis=0)
    return jnp.where(row == iota, jnp.ones((), BF16), jnp.zeros((), BF16))


def iota_rows(columns):
    return lax.broadcasted_iota(jnp.int32, (256, columns), 0).astype(F32).astype(BF16)


def head_norms(x):
    row = lax.broadcasted_iota(jnp.int32, (C, C), 0)
    col = lax.broadcasted_iota(jnp.int32, (C, C), 1)
    same = jnp.where((row >> 4) == (col >> 4), 1.0, 0.0).astype(BF16)
    return jnp.max(dot((x * x * 1.02).astype(BF16), same), axis=0, keepdims=True)


def head_mask(shape, h):
    return (lax.broadcasted_iota(jnp.int32, shape, 1) >> 4) == h


def place_of_device():
    return lax.axis_index("core"), lax.axis_index("grp")


HALF = 528
MESSAGE = 2 * HALF


def pack_kernel(feats, order, parent, cot, w, gain, msg_ref, r_ref, l_ref, own_ref, order_v, parent_v, cot_v, w_v, gain_v, sems):
    _, y = place_of_device()
    copies = [
        pltpu.make_async_copy(source, target, sems.at[index])
        for index, (source, target) in enumerate(
            (
                (order, order_v),
                (parent, parent_v),
                (feats, msg_ref.at[pl.ds(0, ROWS)]),
                (gain, gain_v),
                (w, w_v),
                (cot, cot_v),
            )
        )
    ]
    for copy in copies:
        copy.start()
    for copy in copies:
        copy.wait()
    near = order_v[...] & 8191
    owner = parent_v[...] & 2047
    ids = jnp.concatenate([near >> 6, near & 63, owner >> 6, owner & 63], axis=0)
    msg_ref[ROWS:] = ids.astype(F32).astype(BF16)
    w_high, w_low = split2(w_v[...])
    total = gain_v[...]
    first = total.astype(BF16).astype(F32)
    second = (total - first).astype(BF16).astype(F32)
    third = total - first - second
    row = lax.broadcasted_iota(jnp.int32, (16, 64), 0)
    gains = jnp.where(row == 0, first, jnp.where(row == 1, second, jnp.where(row == 2, third, 0.0)))
    gains = jnp.concatenate([gains, jnp.zeros((16, 64), F32)], axis=1).astype(BF16)

    def cot(k, half):
        start = ((y + k) & 3) * 256 + half * C
        return cot_v[:, pl.ds(pl.multiple_of(start, C), C)]

    own_ref[...] = pool_message(cot(0, 0), cot(0, 1), w_high, w_low, gains)
    r_ref[:64] = cot(1, 0)
    r_ref[64:128] = cot(1, 1)
    r_ref[128:192] = w_high
    r_ref[192:1248] = msg_ref[...]
    r_ref[1248:1312] = w_low
    r_ref[1312:1328] = gains
    r_ref[1328:] = cot(2, 1)
    l_ref[:64] = cot(2, 0)
    l_ref[64:128] = w_high
    l_ref[128:1184] = msg_ref[...]
    l_ref[1184:1248] = w_low
    l_ref[1248:1264] = gains
    l_ref[1264:1328] = cot(3, 0)
    l_ref[1328:] = cot(3, 1)


def pool_message(cot_low, cot_high, w_high, w_low, gains):
    rows = [
        jnp.concatenate([cot_low, cot_high], axis=1),
        jnp.concatenate([w_high, w_low], axis=1),
        jnp.concatenate([gains, jnp.zeros_like(gains)], axis=1),
    ]
    return jnp.concatenate(rows, axis=0)


def pack(feats, order, parent, cot_t, w_t, gain_two):
    return pl.pallas_call(
        pack_kernel,
        in_specs=[pl.BlockSpec(memory_space=pltpu.HBM)] * 6,
        out_shape=(
            jax.ShapeDtypeStruct((MESSAGE, C), BF16),
            jax.ShapeDtypeStruct((1392, C), BF16),
            jax.ShapeDtypeStruct((1392, C), BF16),
            jax.ShapeDtypeStruct((144, 256), BF16),
        ),
        scratch_shapes=[
            pltpu.VMEM((8, C), jnp.int32),
            pltpu.VMEM((8, C), jnp.int32),
            pltpu.VMEM((64, ROWS), BF16),
            pltpu.VMEM((64, C), F32),
            pltpu.VMEM((1, 64), F32),
            pltpu.SemaphoreType.DMA((6,)),
        ],
        compiler_params=vmem(60),
        name="pack",
    )(feats, order, parent, cot_t, w_t, gain_two)


def gather_rows(order_ref, blocks, tab, rep, hil_ref, pid_ref, gord_ref, cnt_ref):
    core, y = place_of_device()
    lane = lax.broadcasted_iota(jnp.int32, (C, C), 1)
    digits = []
    for slot, (rows, ids) in enumerate(blocks):
        for start, part in rows:
            tab[slot, start : start + part.shape[0], :C] = part
        ids = ids.astype(F32)
        gord_ref[slot * 8 : slot * 8 + 8] = (ids[:8] * 64.0 + ids[8:16]).astype(jnp.int32)
        digits.append(ids[16:])
    digits = jnp.concatenate(digits, axis=0)
    turned = digits.T
    for slot in range(8):
        for t in range(8):
            tab[slot, t * C : t * C + C, C:] = jnp.where((lane & ~8) == slot * 16 + t, turned, 0.0).astype(BF16)

    count = jnp.zeros((256, C), F32)
    target = (lax.broadcasted_iota(jnp.int32, (256, C), 0) + (core * 1024 + y * 256)).astype(F32)
    for slot in range(4):
        parents = digits[slot * 16 : slot * 16 + 8] * 64.0 + digits[slot * 16 + 8 : slot * 16 + 16]
        for t in range(8):
            count = count + jnp.where(target == parents[t : t + 1], 1.0, 0.0)
    cnt_ref[...] = jnp.broadcast_to(jnp.sum(count, axis=1, keepdims=True), cnt_ref.shape)

    order = order_ref[...]
    source = (order >> 10) & 7
    slot = (((source >> 2) ^ core) << 2) + ((y - source) & 3)
    index = (slot * ROWS + (order & 1023)).astype(F32)
    for t in range(8):
        column = jnp.broadcast_to(index[t : t + 1], (C, C)).T.astype(jnp.int32)
        rep[t * C : t * C + C] = tile_key(column, lane)
    weight = jnp.where(lax.broadcasted_iota(jnp.int32, (GBLK, C), 1) & 8 == 0, 64.0, 1.0)
    for blk in range(ROWS // GBLK):
        rows = pl.ds(blk * GBLK, GBLK)
        away = rep[rows]
        got = jnp.zeros((GBLK, 2 * C), F32)
        for slot in range(8):
            got = got + dot(one_hot_tiles(away, range(slot * 8, slot * 8 + 8)), tab[slot])
        hil_ref[rows] = got[:, :C].astype(BF16)
        parent = jnp.sum(got[:, C:] * weight, axis=1, keepdims=True).astype(jnp.int32)
        pid_ref[rows] = jnp.broadcast_to(parent, (GBLK, C))


def fwd_kernel(
    order_ref, own, left, upper, lower, right, other, gain_ref, wqkv_ref, wout_ref,
    hil_ref, pid_ref, gord_ref, cnt_ref, att_ref, mine_ref, theirs_ref, o_ref, ot_ref, lse_ref,
    tab, rep, qp, kp, vt, lt, ac,
):
    core, y = place_of_device()
    blocks = [
        ([(0, own[:ROWS])], own[ROWS:]),
        ([(0, left[192:1216])], left[1216:1248]),
        ([(0, upper[128:]), (HALF, lower[: ROWS - HALF])], lower[ROWS - HALF : HALF]),
        ([(0, right[128:1152])], right[1152:1184]),
    ] + [([(0, other[k, :ROWS])], other[k, ROWS:]) for k in range(4)]
    gather_rows(order_ref, blocks, tab, rep, hil_ref, pid_ref, gord_ref, cnt_ref)

    r = hil_ref[...].astype(F32)
    xhat, _ = norm_rows(r)
    u = xhat * gain_ref[...]
    qkv = dot3(u, wqkv_ref[...])
    q = qkv[:, :C] * QSCALE
    k = qkv[:, C : 2 * C]
    place(split2(q), (0, 0, 1, 1), qp)
    place(split2(k), (0, 1, 0, 1), kp)
    for index, part in enumerate(split2(qkv[:, 2 * C :].T)):
        for h in range(HEADS):
            vt[h, index * HD : index * HD + HD] = part[h * HD : h * HD + HD]
    vt[:, 2 * HD :] = jnp.ones((HEADS, HD, ROWS), BF16)

    def head(size, shifted):
        def body(h, carry):
            keys = kp[h]
            values = vt[h]
            own = pl.ds(pl.multiple_of(h * HD, HD), HD)
            for blk in range(ROWS // size):
                cols = pl.ds(blk * size, size)
                s = dot_nt(keys, qp[h, cols])
                if shifted:
                    m = jnp.max(s, axis=0, keepdims=True)
                    s = s - m
                ph, plo = split2(jnp.exp2(s))
                oa = dot(values, ph) + dot(values, plo)
                total = oa[2 * HD : 2 * HD + 1]
                ot_ref[own, cols] = (oa[:HD] + oa[HD : 2 * HD]) / total
                lse = jnp.log2(total)
                if shifted:
                    lse = lse + m
                lt[own, cols] = jnp.broadcast_to(lse, (HD, size))
            return carry

        return body

    small = jnp.max(head_norms(q) * head_norms(k)) < 3600.0

    @pl.when(small)
    def _():
        lax.fori_loop(0, HEADS, head(FBLK, False), 0, unroll=UNROLL)

    @pl.when(jnp.logical_not(small))
    def _():
        lax.fori_loop(0, HEADS, head(SBLK, True), 0)

    o_ref[...] = ot_ref[...].T
    lse_ref[...] = lt[...].T
    att = r + dot3(o_ref[...], wout_ref[...])
    hi, lo = split2(att)
    att_ref[...] = hi
    ac[...] = jnp.concatenate([hi, lo], axis=1)
    parent = pid_ref[...].astype(F32).T[0:1].astype(jnp.int32)
    pid = (((parent >> 10) ^ core) << 10) + ((((parent >> 8) - y) & 3) << 8) + (parent & 255)
    for chunk in range(8):
        sums = dot(one_hot_rows(pid - chunk * 256, iota_rows(ROWS)), ac[...])
        target = mine_ref if chunk < 4 else theirs_ref
        target[chunk & 3] = sums[:, :C] + sums[:, C:]


def attention_forward(order, blocks, gain, w_qkv, w_out):
    return pl.pallas_call(
        fwd_kernel,
        out_shape=(
            jax.ShapeDtypeStruct((ROWS, C), BF16),
            jax.ShapeDtypeStruct((ROWS, C), jnp.int32),
            jax.ShapeDtypeStruct((64, C), jnp.int32),
            jax.ShapeDtypeStruct((256, C), F32),
            jax.ShapeDtypeStruct((ROWS, C), BF16),
            jax.ShapeDtypeStruct((4, 256, C), F32),
            jax.ShapeDtypeStruct((4, 256, C), F32),
            jax.ShapeDtypeStruct((ROWS, C), F32),
            jax.ShapeDtypeStruct((C, ROWS), F32),
            jax.ShapeDtypeStruct((ROWS, C), F32),
        ),
        scratch_shapes=[
            pltpu.VMEM((8, ROWS, 2 * C), BF16),
            pltpu.VMEM((ROWS, C), BF16),
            pltpu.VMEM((HEADS, ROWS, C), BF16),
            pltpu.VMEM((HEADS, ROWS, C), BF16),
            pltpu.VMEM((HEADS, 3 * HD, ROWS), BF16),
            pltpu.VMEM((C, ROWS), F32),
            pltpu.VMEM((ROWS, 2 * C), BF16),
        ],
        compiler_params=vmem(30),
        cost_estimate=pl.CostEstimate(flops=30_000_000_000, bytes_accessed=4_000_000, transcendentals=8_400_000),
        name="attention_forward",
    )(order, *blocks, gain, w_qkv, w_out)


def pool_kernel(mine, theirs, c1, c2, c3, cnt_ref, att_ref, w0, w1, w2, w3, after, s0, t1, t2, t3, dp_ref, gw_ref, gg_ref):
    cnt = cnt_ref[...]
    pooled = (mine[0] + theirs[0] + c1[...] + c2[...] + c3[...]) / cnt
    msgs = (w0, w1, w2, w3)
    wh = jnp.concatenate([m[64:128, :C] for m in msgs], axis=0)
    wl = jnp.concatenate([m[64:128, C:] for m in msgs], axis=0)
    cot = jnp.concatenate([m[:64] for m in msgs], axis=0).astype(F32).T
    gains = jnp.concatenate([m[128:, :64] for m in msgs], axis=1).astype(F32)
    gain = gains[0:1] + gains[1:2] + gains[2:3]
    ph, plo = split2(pooled)
    normed, rstd = norm_rows(dot_nt(ph, wh) + (dot_nt(plo, wh) + dot_nt(ph, wl)))
    v = normed * gain
    t = jnp.tanh(GELU_A * (v + GELU_B * (v * v * v)))
    s4 = (0.5 * v * (1.0 + t)).T.astype(BF16)
    s0[...] = s4[:64]
    for k, ref in enumerate((t1, t2, t3)):
        block = s4[64 * k + 64 : 64 * k + 128]
        ref[:ROWS] = att_ref[...]
        ref[ROWS : ROWS + 64] = block[:, :C]
        ref[ROWS + 64 :] = block[:, C:]
    slope = 0.5 * (1.0 + t) + 0.5 * v * (1.0 - t * t) * (GELU_A * (1.0 + (3.0 * GELU_B) * (v * v)))
    d_scaled = cot * slope
    d_normed = d_scaled * gain
    d_proj = rstd * (
        d_normed
        - jnp.mean(d_normed, -1, keepdims=True)
        - normed * jnp.mean(d_normed * normed, -1, keepdims=True)
    )
    dh, dl = split2(d_proj)
    dp_ref[...] = (dot(dh, wh) + (dot(dl, wh) + dot(dh, wl))) / cnt
    _, y = place_of_device()
    gw = dot3(d_proj.T, pooled)
    gg = jnp.sum(d_scaled * normed, axis=0, keepdims=True)
    gains = jnp.zeros((8, C), F32)
    row = lax.broadcasted_iota(jnp.int32, (8, C), 0)
    low = lax.broadcasted_iota(jnp.int32, (8, C), 1) < 64
    for k in range(4):
        owner = (y - k) & 3
        gw_ref[pl.ds(pl.multiple_of(owner * 64, 64), 64)] = gw[64 * k : 64 * k + 64]
        block = gg[:, 64 * k : 64 * k + 64]
        twice = jnp.concatenate([block, block], axis=1)
        hit = (row == 1 + (owner >> 1)) & (low == ((owner & 1) == 0))
        gains = jnp.where(hit, twice, gains)
    gg_ref[...] = gains


def pooled_section(mine, theirs, chunks, cnt, att, msgs, after):
    return pl.pallas_call(
        pool_kernel,
        in_specs=[pl.BlockSpec(memory_space=pltpu.VMEM)] * 11 + [pl.BlockSpec(memory_space=pl.ANY)],
        out_shape=(jax.ShapeDtypeStruct((64, 256), BF16),)
        + (jax.ShapeDtypeStruct((ROWS + 128, C), BF16),) * 3
        + (
            jax.ShapeDtypeStruct((256, C), F32),
            jax.ShapeDtypeStruct((256, C), F32),
            jax.ShapeDtypeStruct((8, C), F32),
        ),
        compiler_params=vmem(12),
        name="pooled_section",
    )(mine, theirs, *chunks, cnt, att, *msgs, after)


def stack_heads(source, target):
    hi, lo = split2(source.T)
    for h in range(HEADS):
        target[h, :HD] = hi[h * HD : h * HD + HD]
        target[h, HD:] = lo[h * HD : h * HD + HD]


def prep_kernel(r_ref, lse_ref, gain_ref, wqkv_ref, qp, kp, vp, kh, kl, q_t):
    xhat, _ = norm_rows(r_ref[...].astype(F32))
    u = xhat * gain_ref[...]
    qkv = dot3(u, wqkv_ref[...])
    q = qkv[:, :C] * QSCALE
    qh, ql = split2(q)
    lse = -lse_ref[...]
    l1 = lse.astype(BF16).astype(F32)
    l2 = (lse - l1).astype(BF16).astype(F32)
    l3 = lse - l1 - l2
    which = lax.broadcasted_iota(jnp.int32, (ROWS, C), 1) & 15
    lp = jnp.where(which == 0, l1, jnp.where(which == 1, l2, jnp.where(which == 2, l3, 0.0))).astype(BF16)
    place((qh, ql, lp), (0, 0, 1, 1, 2), qp)
    khi, klo = split2(qkv[:, C : 2 * C])
    place((khi, klo), (0, 1, 0, 1), kp, const=lambda lane: (lane >= 64) & (lane < 67))
    kh[...] = khi
    kl[...] = klo
    place(split2(qkv[:, 2 * C :]), (0, 1, 0, 1), vp, const=lambda lane: (lane >= 64) & (lane < 96))
    stack_heads(q, q_t)


def backward_operands(rows, lse, gain, w_qkv):
    return pl.pallas_call(
        prep_kernel,
        out_shape=(jax.ShapeDtypeStruct((HEADS, ROWS, C), BF16),) * 3
        + (jax.ShapeDtypeStruct((ROWS, C), BF16),) * 2
        + (jax.ShapeDtypeStruct((HEADS, 2 * HD, ROWS), BF16),),
        compiler_params=vmem(24),
        cost_estimate=pl.CostEstimate(flops=6_000_000_000, bytes_accessed=8_000_000, transcendentals=0),
        name="backward_operands",
    )(rows, lse, gain, w_qkv)


def bwd_kernel(
    r_ref, o_ref, ot_ref, gain_ref, wqkv_ref, wout_ref, pid_ref, gw_ref, gg2_ref,
    qp, kp, vp, kh, kl, q_t, d0, d1, d2, d3, e0, e1, e2, e3,
    df_ref, flat,
    dop, tab, da_ref, dot_t, dv_t, dk_t, dq_ref,
):
    core, y = place_of_device()
    for chunk, ref in enumerate((d0, d1, d2, d3, e0, e1, e2, e3)):
        hi, lo = split2(ref[...])
        tab[chunk * 256 : chunk * 256 + 256, :C] = hi
        tab[chunk * 256 : chunk * 256 + 256, C:] = lo
    lane = lax.broadcasted_iota(jnp.int32, (DBLK, C), 1)
    for blk in range(ROWS // DBLK):
        rows = pl.ds(blk * DBLK, DBLK)
        pid = pid_ref[rows]
        index = (((pid >> 10) ^ core) << 10) + (((y - (pid >> 8)) & 3) << 8) + (pid & 255)
        got = dot(one_hot_tiles(tile_key(index, lane), range(16)), tab[...])
        da_ref[rows] = got[:, :C] + got[:, C:]

    da = da_ref[...]
    do = dot3_nt(da, wout_ref[...])
    place((*split2(do), *split2(-do * o_ref[...])), (0, 0, 1, 1, 2, 3), dop)
    stack_heads(do, dot_t)

    def head(h, carry):
        kmask = head_mask((ROWS, C), h)
        zero = jnp.zeros((), BF16)
        ka = jnp.concatenate([jnp.where(kmask, kh[...], zero), jnp.where(kmask, kl[...], zero)], axis=1)
        keys, vals = kp[h], vp[h]
        mask = head_mask((BBLK, C), h)
        dv = jnp.zeros((2 * HD, ROWS), F32)
        dk = jnp.zeros((2 * HD, ROWS), F32)
        for blk in range(ROWS // BBLK):
            rows = pl.ds(blk * BBLK, BBLK)
            p = jnp.exp2(dot_nt(qp[h, rows], keys))
            ds = p * dot_nt(dop[h, rows], vals)
            ph, plo = split2(p)
            sh, sl = split2(ds)
            left = dot_t[h, :, rows]
            dv = dv + (dot(left, ph) + dot(left, plo))
            left = q_t[h, :, rows]
            dk = dk + (dot(left, sh) + dot(left, sl))
            dq = dot(sh, ka) + dot(sl, ka)
            dq_ref[rows] = jnp.where(mask, dq[:, :C] + dq[:, C:], dq_ref[rows])
        place_rows = pl.ds(pl.multiple_of(h * HD, HD), HD)
        dv_t[place_rows] = dv[:HD] + dv[HD:]
        dk_t[place_rows] = dk[:HD] + dk[HD:]
        return carry

    lax.fori_loop(0, HEADS, head, 0, unroll=UNROLL)
    xhat, rstd = norm_rows(r_ref[...].astype(F32))
    u = xhat * gain_ref[...]
    grads = jnp.concatenate([dq_ref[...] * HD ** (-0.5), dk_t[...].T * LN2, dv_t[...].T], axis=1)
    du = dot3_nt(grads, wqkv_ref[...])
    gq = dot3(u.T, grads)
    for part in range(3):
        flat[part * C : part * C + C] = gq[:, part * C : part * C + C]
    flat[3 * C : 4 * C] = dot3(ot_ref[...], da)
    flat[4 * C : 6 * C] = gw_ref[...]
    row = lax.broadcasted_iota(jnp.int32, (8, C), 0)
    gains = jnp.where(row == 0, jnp.sum(du * xhat, axis=0, keepdims=True), gg2_ref[...])
    flat[6 * C : 6 * C + 8] = gains
    flat[6 * C + 8 :] = jnp.zeros((2 * C - 8, C), F32)
    dn = du * gain_ref[...]
    dx = rstd * (dn - jnp.mean(dn, -1, keepdims=True) - xhat * jnp.mean(dn * xhat, -1, keepdims=True))
    df_ref[...] = (da + dx).astype(BF16)


def attention_backward(rows, o, o_t, gain, w_qkv, w_out, pid, grad_pool, grad_gain_two, operands, d_pooled):
    return pl.pallas_call(
        bwd_kernel,
        out_shape=(jax.ShapeDtypeStruct((ROWS, C), BF16), jax.ShapeDtypeStruct((8 * C, C), F32)),
        scratch_shapes=[
            pltpu.VMEM((HEADS, ROWS, C), BF16),
            pltpu.VMEM((2048, 2 * C), BF16),
            pltpu.VMEM((ROWS, C), F32),
            pltpu.VMEM((HEADS, 2 * HD, ROWS), BF16),
            pltpu.VMEM((C, ROWS), F32),
            pltpu.VMEM((C, ROWS), F32),
            pltpu.VMEM((ROWS, C), F32),
        ],
        compiler_params=vmem(34),
        cost_estimate=pl.CostEstimate(flops=90_000_000_000, bytes_accessed=8_000_000, transcendentals=8_400_000),
        name="attention_backward",
    )(rows, o, o_t, gain, w_qkv, w_out, pid, grad_pool, grad_gain_two, *operands, *d_pooled)


def rows_kernel(gord_ref, a0, a1, a2, a3, ao, f0, f1, f2a, f2b, f3, fo, s0, s3_ref, gf_ref, s4_ref):
    core, y = place_of_device()
    att = [ref[:ROWS] for ref in (a0, a1, a2, a3)] + [ao[k] for k in range(4)]
    opposite = jnp.concatenate([f2a[...], f2b[...]], axis=0)
    grad = [f0[...], f1[...], opposite, f3[...]] + [fo[k] for k in range(4)]
    own = lax.broadcasted_iota(jnp.int32, (RBLK, C), 0) + (core * 4 + y) * ROWS
    for blk in range(ROWS // RBLK):
        rows = pl.ds(blk * RBLK, RBLK)
        got = jnp.zeros((RBLK, 2 * C), F32)
        for slot in range(8):
            ids = gord_ref[slot * 8 : slot * 8 + 8] - blk * RBLK
            hot = jnp.concatenate([jnp.where(own == ids[t : t + 1], 1.0, 0.0) for t in range(8)], axis=1).astype(BF16)
            got = got + dot(hot, jnp.concatenate([att[slot], grad[slot]], axis=1))
        s3_ref[rows] = got[:, :C].astype(BF16)
        gf_ref[rows] = got[:, C:].astype(BF16)
    s4_ref[:, pl.ds(pl.multiple_of(y * 256, 256), 256)] = s0[...]
    for k, ref in ((1, a3), (2, a2), (3, a1)):
        block = jnp.concatenate([ref[ROWS : ROWS + 64], ref[ROWS + 64 :]], axis=1)
        s4_ref[:, pl.ds(pl.multiple_of(((y + k) & 3) * 256, 256), 256)] = block


def results(gord, att, grad, s4):
    return pl.pallas_call(
        rows_kernel,
        out_shape=(
            jax.ShapeDtypeStruct((ROWS, C), BF16),
            jax.ShapeDtypeStruct((ROWS, C), BF16),
            jax.ShapeDtypeStruct((64, ROWS), BF16),
        ),
        compiler_params=vmem(60),
        cost_estimate=pl.CostEstimate(flops=8_000_000_000, bytes_accessed=5_000_000, transcendentals=0),
        name="rows_to_z_order",
    )(gord, *att, *grad, s4)


def params_kernel(flat, gq_ref, go_ref, g1_ref, gw_ref, g2_ref):
    _, y = place_of_device()
    for part in range(3):
        gq_ref[:, part * C : part * C + C] = flat[part * C : part * C + C]
    go_ref[...] = flat[3 * C : 4 * C]
    gw_ref[...] = flat[pl.ds(pl.multiple_of(4 * C + y * 64, 64), 64)]
    gains = flat[6 * C : 6 * C + 8]
    g1_ref[...] = gains[0:1]
    pair = jnp.where(y >= 2, gains[2:3], gains[1:2])
    g2_ref[...] = jnp.where((y & 1) == 0, pair[:, :64], pair[:, 64:])


def parameter_results(flat):
    return pl.pallas_call(
        params_kernel,
        out_shape=(
            jax.ShapeDtypeStruct((C, 3 * C), F32),
            jax.ShapeDtypeStruct((C, C), F32),
            jax.ShapeDtypeStruct((1, C), F32),
            jax.ShapeDtypeStruct((64, C), F32),
            jax.ShapeDtypeStruct((1, 64), F32),
        ),
        compiler_params=vmem(8),
        name="parameter_results",
    )(flat)


def message_kernel(own, left, upper, lower, right, out_ref, w1, w2, w3):
    out_ref[0] = own[...]
    out_ref[1] = left[192:1248]
    out_ref[2, :HALF] = upper[128:]
    out_ref[2, HALF:] = lower[:HALF]
    out_ref[3] = right[128:1184]
    w1[...] = pool_message(left[:64], left[64:128], left[128:192], left[1248:1312], left[1312:1328])
    w2[...] = pool_message(upper[:64], lower[608:], upper[64:128], lower[528:592], lower[592:608])
    w3[...] = pool_message(right[1264:1328], right[1328:], right[64:128], right[1184:1248], right[1248:1264])


def core_message(blocks):
    return pl.pallas_call(
        message_kernel,
        out_shape=(jax.ShapeDtypeStruct((4, MESSAGE, C), BF16),) + (jax.ShapeDtypeStruct((144, 256), BF16),) * 3,
        compiler_params=vmem(8),
        name="core_message",
    )(*blocks)


def four_kernel(*refs):
    *blocks, rows_ref = refs
    if len(blocks) == 5:
        b0, b1, b2a, b2b, b3 = blocks
        rows_ref[2, : ROWS // 2] = b2a[...]
        rows_ref[2, ROWS // 2 :] = b2b[...]
        blocks = [b0, b1, None, b3]
    for k, ref in enumerate(blocks):
        if ref is not None:
            rows_ref[k] = ref[:ROWS]


def four_rows(blocks):
    return pl.pallas_call(
        four_kernel,
        out_shape=jax.ShapeDtypeStruct((4, ROWS, C), BF16),
        compiler_params=vmem(8),
        name="four_rows",
    )(*blocks)


def share_kernel(shares, out_ref):
    total = shares[0]
    for source in range(1, shares.shape[0]):
        total = total + shares[source]
    out_ref[...] = jnp.broadcast_to(total, out_ref.shape)


def share_of_all(shares):
    return pl.pallas_call(
        share_kernel,
        out_shape=jax.ShapeDtypeStruct(shares.shape, F32),
        compiler_params=vmem(8),
        name="share_of_all",
    )(shares)


def shift(block, axis, apart):
    count = lax.axis_size(axis)
    return lax.ppermute(block, axis, [(i, (i + apart) % count) for i in range(count)])


EVERYWHERE = ("x", "z", "core", "grp")


def deal_rows(flat):
    return lax.all_to_all(flat.reshape(lax.axis_size(EVERYWHERE), -1, flat.shape[1]), EVERYWHERE, 0, 0)


def gather_rows_of_all(shares):
    count = lax.axis_size(EVERYWHERE)
    every = lax.all_to_all(shares, EVERYWHERE, 0, 0)
    return every.reshape(-1, shares.shape[2])


def shards(feats, order, parent, gain_one, w_qkv, w_out, w_pool, gain_two, cotangent):
    order = order.reshape(8, C)
    msg, to_right, to_left, own_pool = pack(
        feats, order, parent.reshape(8, C), cotangent.T, w_pool.T, gain_two[None]
    )

    left = shift(to_right, "grp", 1)
    right = shift(to_left, "grp", -1)
    around = (left, shift(right[:656], "grp", -1), shift(left[720:], "grp", 1), right)
    message, *pool_msgs = core_message((msg, *around))
    other = shift(message, "core", 1)
    w_msgs = [own_pool] + pool_msgs
    hilbert, pid, gord, cnt, att, mine, theirs, o, o_t, lse = attention_forward(
        order, (msg, *around, other), gain_one[None], w_qkv, w_out
    )

    operands = backward_operands(hilbert, lse, gain_one[None], w_qkv)

    theirs = shift(theirs, "core", 1)
    chunks = [shift(mine[k] + theirs[k], "grp", k) for k in (1, 2, 3)]
    s4, *rows, d_pool, grad_pool, grad_gain_two = pooled_section(mine, theirs, chunks, cnt, att, w_msgs, operands[-1])
    own = [d_pool] + [shift(d_pool, "grp", k) for k in (1, 2, 3)]
    d_pooled = own + [shift(block, "core", 1) for block in own]

    from_y = [shift(rows[k - 1], "grp", -k) for k in (3, 2, 1)]
    att = [att] + from_y

    df, flat = attention_backward(
        hilbert, o, o_t, gain_one[None], w_qkv, w_out, pid, grad_pool, grad_gain_two, operands, d_pooled
    )
    left = shift(df, "grp", 1)
    right = shift(df, "grp", -1)
    att_rows = four_rows(att)
    flat, left, right, att_rows = lax.optimization_barrier((flat, left, right, att_rows))
    shares = deal_rows(flat)
    att.append(shift(att_rows, "core", 1))
    half = ROWS // 2
    upper = shift(right[:half], "grp", -1)
    lower = shift(left[half:], "grp", 1)
    shares, upper, lower = lax.optimization_barrier((shares, upper, lower))
    df = [df, left, upper, lower, right]
    df.append(shift(four_rows(df), "core", 1))
    total = gather_rows_of_all(share_of_all(shares))
    rows = results(gord, att, df, s4)
    total, rows = lax.optimization_barrier((total, rows))
    section_three, grad_feats, section_four = rows
    g_qkv, g_out, g_one, g_pool, g_two = parameter_results(total)
    return (section_four.T, section_three, grad_feats, g_one[0], g_qkv, g_out, g_pool.T, g_two[0])


def solution(mesh):
    fine = Mesh(mesh.devices.reshape(4, 4, 2, 4), ("x", "z", "core", "grp"))
    pts = ("x", "z", "core")
    everywhere = pts + ("grp",)
    placed = (
        P(everywhere, None),
        P(everywhere),
        P(everywhere),
        P(),
        P(),
        P(),
        P(None, "grp"),
        P("grp"),
        P(pts, "grp"),
    )
    return jax.shard_map(
        shards,
        mesh=fine,
        in_specs=placed,
        out_specs=(
            P(pts, "grp"),
            P(everywhere, None),
            P(everywhere, None),
            P(),
            P(),
            P(),
            P(None, "grp"),
            P("grp"),
        ),
        check_vma=False,
    )
```
